32 devices in a mesh: dp: 8 (over z, x), mp: 4 (over y, core).
Axes of the slice: x: 2, y: 2, z: 4, core: 2. Of those that a mesh axis runs over, the one named last changes fastest.
Arguments:
- tokens: bfloat16 [2, 4096, 768], P(None, ('dp', 'mp')), may hold values from -6 to 6
- cluster_ids: int32 [2, 4096, 12], P(None, 'dp', 'mp'), may hold values from 0 to 199, as said below
- query_weight: bfloat16 [768, 768], P(None, 'mp'), may hold values from -0.21875 to 0.21875
- query_bias: bfloat16 [768], P('mp'), may hold values from -8 to 8
- key_weight: bfloat16 [768, 768], P(None, 'mp'), may hold values from -0.21875 to 0.21875
- value_weight: bfloat16 [768, 768], P(None, 'mp'), may hold values from -0.21875 to 0.21875
- value_bias: bfloat16 [768], P('mp'), may hold values from -0.59765625 to 0.59765625
- output_weight: bfloat16 [768, 768], P('mp'), may hold values from -1.75 to 1.75
- output_bias: bfloat16 [768], replicated, may hold values from -1.1953125 to 1.1953125
- expand_weight: bfloat16 [768, 3072], P(None, 'mp'), may hold values from -0.21875 to 0.21875
- expand_bias: bfloat16 [3072], P('mp'), may hold values from -1.1953125 to 1.1953125
- shrink_weight: bfloat16 [3072, 768], P('mp'), may hold values from -0.109375 to 0.109375
- shrink_bias: bfloat16 [768], replicated, may hold values from -1.1953125 to 1.1953125
- first_gain: bfloat16 [768], replicated, may hold values from 0.5 to 1.5
- first_shift: bfloat16 [768], replicated, may hold values from -1.1953125 to 1.1953125
- second_gain: bfloat16 [768], replicated, may hold values from 0.5 to 1.5
- second_shift: bfloat16 [768], replicated, may hold values from -1.1953125 to 1.1953125
- cotangent: bfloat16 [2, 4096, 768], P(None, ('dp', 'mp')), may hold values from -6 to 6
Outputs:
- result: bfloat16 [2, 4096, 768], P(None, ('dp', 'mp'))
- token_grad: float32 [2, 4096, 768], P(None, ('dp', 'mp'))
- query_weight_grad: float32 [768, 768], P(None, 'mp')
- query_bias_grad: float32 [768], P('mp')
- key_weight_grad: float32 [768, 768], P(None, 'mp')
- value_weight_grad: float32 [768, 768], P(None, 'mp')
- value_bias_grad: float32 [768], P('mp')
- output_weight_grad: float32 [768, 768], P('mp')
- output_bias_grad: float32 [768], replicated
- expand_weight_grad: float32 [768, 3072], P(None, 'mp')
- expand_bias_grad: float32 [3072], P('mp')
- shrink_weight_grad: float32 [3072, 768], P('mp')
- shrink_bias_grad: float32 [768], replicated
- first_gain_grad: float32 [768], replicated
- first_shift_grad: float32 [768], replicated
- second_gain_grad: float32 [768], replicated
- second_shift_grad: float32 [768], replicated
The draws below stay inside these ranges and needn't reach their ends.
Inputs may be any that keep to these rules, and one draw needn't show every extreme that they name: `cluster_ids`: all ids of one sequence lie below one of 25, 100 or 200, the same for all its heads; some sequence uses 200.
All inputs are finite; a program needn't handle non-finite values.
Results may differ from the reference program's by a relative error of at most 0.014.
The reference program's roundings to bfloat16 on the way count: a program that leaves them out, or rounds other values in their place, can miss the bound.
Values may be sent and summed in bfloat16 or wider, within the bound.
No kernel may reach another device: no remote copies, remote signals or barrier semaphores. Data moves between devices by JAX's collectives and lax.ppermute only.
A program may use at most 640 MiB of HBM per device.

```python
import jax
import jax.numpy as jnp
from jax import lax

D = 768
HEADS = 12
HEAD_DIM = 64
FF = 3072
LENGTH = 4096
FEW_CLUSTERS = 25
MID_CLUSTERS = 100
MAX_CLUSTERS = 200
SEQUENCES = 2


def draw_cluster_ids(key, part):
    group_key = jax.random.fold_in(key, 11)
    id_key = jax.random.fold_in(key, 12)
    pick_key = jax.random.fold_in(key, 13)
    groups = jax.random.randint(group_key, (SEQUENCES,), 0, 3)
    chosen = jax.random.randint(pick_key, (), 0, SEQUENCES)
    seq_index = jnp.arange(SEQUENCES, dtype=jnp.int32)
    groups = jnp.where(seq_index == chosen, 2, groups)
    limits = jnp.where(groups == 0, FEW_CLUSTERS, jnp.where(groups == 1, MID_CLUSTERS, MAX_CLUSTERS))
    raw_ids = jax.random.randint(id_key, (SEQUENCES, LENGTH, HEADS), 0, limits[:, None, None])
    seq_grid = seq_index[:, None, None]
    pos_grid = jnp.arange(LENGTH, dtype=jnp.int32)[None, :, None]
    head_grid = jnp.arange(HEADS, dtype=jnp.int32)[None, None, :]
    first_cell = (seq_grid == chosen) & (pos_grid == 0) & (head_grid == 0)
    second_cell = (seq_grid == chosen) & (pos_grid == 1) & (head_grid == 0)
    raw_ids = jnp.where(first_cell, MAX_CLUSTERS - 1, raw_ids)
    raw_ids = jnp.where(second_cell, 0, raw_ids)
    return raw_ids.astype(jnp.int32)


def block_scale(own_key, dims, pieces, low, largest):
    def one(position, shards_of):
        draws = jax.random.uniform(jax.random.fold_in(jax.random.fold_in(own_key, 6), position), (shards_of,), jnp.float32, low / len(pieces), largest / len(pieces))
        return jnp.repeat(jnp.exp(draws), dims[position] // shards_of).reshape((-1,) + (1,) * (len(dims) - position - 1))

    level = one(*pieces[0])
    for cut in pieces[1:]:
        level = level * one(*cut)
    return level


def centred(rng, shape, width, bound, cuts=(), kind=jnp.bfloat16):
    level = block_scale(rng, shape, cuts, -0.22, 0.18) if cuts else 1.0
    entries = jax.random.normal(rng, shape, jnp.float32) * width * level
    return jnp.minimum(jnp.maximum(entries, -bound), bound).astype(kind)


def setup_inputs(seed: int = 0) -> dict:
    arg_keys = jax.random.split(jax.random.key(seed), 19)
    return {
        "tokens": centred(arg_keys[0], (SEQUENCES, LENGTH, D), 1.0, 6.0, ((1, 32),)),
        "cluster_ids": draw_cluster_ids(jax.random.fold_in(arg_keys[18], 71), 0),
        "query_weight": centred(arg_keys[2], (D, D), D ** -0.5, 0.21875, ((1, 4),)),
        "query_bias": centred(arg_keys[3], (D,), 2.0, 8.0, ((0, 4),)),
        "key_weight": centred(arg_keys[4], (D, D), D ** -0.5, 0.21875, ((1, 4),)),
        "value_weight": centred(arg_keys[5], (D, D), D ** -0.5, 0.21875, ((1, 4),)),
        "value_bias": centred(arg_keys[6], (D,), 0.1, 0.59765625, ((0, 4),)),
        "output_weight": centred(arg_keys[7], (D, D), (D // 64) ** -0.5, 1.75, ((0, 4),)),
        "output_bias": centred(arg_keys[8], (D,), 0.2, 1.1953125),
        "expand_weight": centred(arg_keys[9], (D, FF), D ** -0.5, 0.21875, ((1, 4),)),
        "expand_bias": centred(arg_keys[10], (FF,), 0.2, 1.1953125, ((0, 4),)),
        "shrink_weight": centred(arg_keys[11], (FF, D), FF ** -0.5, 0.109375, ((0, 4),)),
        "shrink_bias": centred(arg_keys[12], (D,), 0.2, 1.1953125),
        "first_gain": jnp.clip(1.0 + 0.1 * jax.random.normal(arg_keys[13], (D,), jnp.float32), 0.5, 1.5).astype(jnp.bfloat16),
        "first_shift": centred(arg_keys[14], (D,), 0.2, 1.1953125),
        "second_gain": jnp.clip(1.0 + 0.1 * jax.random.normal(arg_keys[15], (D,), jnp.float32), 0.5, 1.5).astype(jnp.bfloat16),
        "second_shift": centred(arg_keys[16], (D,), 0.2, 1.1953125),
        "cotangent": centred(arg_keys[17], (SEQUENCES, LENGTH, D), 1.0, 6.0, ((1, 32),)),
    }


@jax.custom_vjp
def low(v):
    return lax.optimization_barrier(v.astype(jnp.bfloat16)).astype(jnp.float32)

@jax.custom_vjp
def low_back(v):
    return v

def low_keep(v):
    return (low(v), None)

def low_pass(kept, grad):
    return (grad,)

def back_keep(v):
    return (v, None)

def back_low(kept, grad):
    return (low(grad),)
low.defvjp(low_keep, low_pass)
low_back.defvjp(back_keep, back_low)
highest = lax.Precision.HIGHEST

def product(left, right):
    return jnp.dot(left, right, precision=highest)

def contract(form, left, right):
    return jnp.einsum(form, left, right, precision=highest)

def layer_norm(values, gain, shift):
    average = lax.optimization_barrier(jnp.mean(values, axis=-1, keepdims=True))
    centered = values - average
    variance = lax.optimization_barrier(jnp.mean(centered * centered, axis=-1, keepdims=True))
    return centered * lax.rsqrt(variance + 1e-05) * gain + shift

def sequence_forward(weights, rows, ids):
    query_weight, query_bias, key_weight, value_weight, value_bias, output_weight, output_bias, expand_weight, expand_bias, shrink_weight, shrink_bias, first_gain, first_shift, second_gain, second_shift = weights
    count_rows = rows.shape[0]
    normed = low(layer_norm(rows, first_gain, first_shift))
    queries = low_back(low(product(normed, query_weight) + query_bias)).reshape(count_rows, HEADS, HEAD_DIM)
    key_heads = low_back(low(product(normed, key_weight))).reshape(count_rows, HEADS, HEAD_DIM)
    value_heads = low_back(low(product(normed, value_weight) + value_bias)).reshape(count_rows, HEADS, HEAD_DIM)
    onehot = (ids[:, :, None] == jnp.arange(MAX_CLUSTERS, dtype=jnp.int32)).astype(jnp.float32)
    sums = contract('thc,thd->hcd', onehot, queries)
    counts = lax.optimization_barrier(jnp.sum(onehot, axis=0))
    centroid = low(sums / jnp.maximum(counts, 1.0)[:, :, None])
    scores = contract('hcd,thd->hct', centroid, key_heads) * 0.125
    probs = jax.nn.softmax(scores, axis=-1)
    cluster_out = contract('hct,thd->hcd', probs, value_heads)
    attended = low_back(low(contract('thc,hcd->thd', onehot, cluster_out))).reshape(count_rows, D)
    hidden = rows + low_back(product(attended, output_weight)) + output_bias
    second = low(layer_norm(hidden, second_gain, second_shift))
    expanded = low_back(product(second, expand_weight) + expand_bias)
    activated = low(jax.nn.gelu(expanded, approximate=False))
    return hidden + product(activated, shrink_weight) + shrink_bias

def reference(tokens, cluster_ids, query_weight, query_bias, key_weight, value_weight, value_bias, output_weight, output_bias, expand_weight, expand_bias, shrink_weight, shrink_bias, first_gain, first_shift, second_gain, second_shift, cotangent):
    weights = tuple((w.astype(jnp.float32) for w in (query_weight, query_bias, key_weight, value_weight, value_bias, output_weight, output_bias, expand_weight, expand_bias, shrink_weight, shrink_bias, first_gain, first_shift, second_gain, second_shift)))
    rows_all = tokens.astype(jnp.float32)

    def forward(inputs, params):

        def one_sequence(packed):
            return sequence_forward(params, packed[0], packed[1])
        return lax.map(jax.checkpoint(one_sequence), (inputs, cluster_ids))
    output, pullback = jax.vjp(forward, rows_all, weights)
    token_grad, grads = pullback(cotangent.astype(jnp.float32))
    return (output.astype(jnp.bfloat16), token_grad, grads[0], grads[1], grads[2], grads[3], grads[4], grads[5], grads[6], grads[7], grads[8], grads[9], grads[10], grads[11], grads[12], grads[13], grads[14])
```

```python
from functools import partial

import jax
import jax.numpy as jnp
from jax import lax
from jax.sharding import PartitionSpec as P

HEAD_DIM = 64
MAX_CLUSTERS = 200
F32 = jnp.float32
LOW = jnp.bfloat16


def layer_norm(values, gain, shift):
    average = jnp.mean(values, axis=-1, keepdims=True)
    centered = values - average
    variance = jnp.mean(centered * centered, axis=-1, keepdims=True)
    return centered * lax.rsqrt(variance + 1e-05) * gain + shift


def normalized(values):
    average = jnp.mean(values, axis=-1, keepdims=True)
    centered = values - average
    variance = jnp.mean(centered * centered, axis=-1, keepdims=True)
    return centered * lax.rsqrt(variance + 1e-05)


def split3(values):
    high = lax.reduce_precision(values, 8, 7)
    rest = values - high
    middle = lax.reduce_precision(rest, 8, 7)
    return high.astype(LOW), middle.astype(LOW), (rest - middle).astype(LOW)


def partner(value, step):
    size = lax.axis_size("mp")
    return lax.ppermute(value, "mp", [(i, i ^ step) for i in range(size)])


def gather_rows(value):
    far = partner(value, 2)
    near = partner(value, 1)
    return value, near, far, partner(far, 1)


def scatter_rows(pieces):
    own, near, far, diagonal = pieces
    far_in = partner(diagonal.astype(LOW), 1)
    far_sum = far.astype(F32) + far_in.astype(F32)
    across = partner(far_sum.astype(LOW), 2)
    near_in = partner(near.astype(LOW), 1)
    return own.astype(F32) + near_in.astype(F32) + across.astype(F32)


def gather_by_exchange(value, axes, count):
    return lax.all_to_all(jnp.broadcast_to(value[None], (count, *value.shape)), axes, 0, 0)


def paired(values):
    half = values.shape[0] // 2
    both = jnp.concatenate([values[:half], values[half:]], axis=-1)
    return both.reshape(-1, both.shape[-1])


def unpaired(rows, half, heads):
    both = rows.reshape(half, heads, MAX_CLUSTERS, 2 * HEAD_DIM)
    return jnp.concatenate([both[..., :HEAD_DIM], both[..., HEAD_DIM:]], axis=0)


def shards(
    tokens,
    cluster_ids,
    query_weight,
    query_bias,
    key_weight,
    value_weight,
    value_bias,
    output_weight,
    output_bias,
    expand_weight,
    expand_bias,
    shrink_weight,
    shrink_bias,
    first_gain,
    first_shift,
    second_gain,
    second_shift,
    cotangent,
):
    seqs, share_rows, width = tokens.shape
    heads = cluster_ids.shape[2]
    n_dp, n_mp = lax.axis_size("dp"), lax.axis_size("mp")
    both_axes = ("dp", "mp")
    n_all = n_dp * n_mp
    all_heads = heads * n_mp
    half = seqs // 2
    local_rows = share_rows * n_mp
    count_rows = seqs * local_rows
    head_width = heads * HEAD_DIM
    table_rows = half * heads * MAX_CLUSTERS
    shard_rows = table_rows // n_dp
    me = lax.axis_index("mp")
    (
        query_shift,
        value_shift,
        output_shift,
        expand_shift,
        shrink_shift,
        gain_one,
        shift_one,
        gain_two,
        shift_two,
    ) = [
        w.astype(F32)
        for w in (
            query_bias,
            value_bias,
            output_bias,
            expand_bias,
            shrink_bias,
            first_gain,
            first_shift,
            second_gain,
            second_shift,
        )
    ]

    def whole(pieces):
        return jnp.concatenate(pieces, axis=1).reshape(count_rows, width)

    def pieces_of(values):
        cut = values.reshape(seqs, n_mp, share_rows, width)
        return [cut[:, k] for k in range(n_mp)]

    def reorder(ids):
        cut = ids.reshape(seqs, n_mp // 2, 2, share_rows, -1)
        cut = jnp.where(me % 2 == 1, cut[:, :, ::-1], cut)
        cut = jnp.where(me // 2 == 1, cut[:, ::-1], cut)
        return cut.reshape(seqs, local_rows, -1)

    token_rows = whole(gather_rows(tokens))
    ids_all = gather_by_exchange(cluster_ids, "mp", n_mp)
    ids_all = reorder(ids_all.transpose(1, 2, 0, 3).reshape(seqs, local_rows, all_heads))
    ids_own = reorder(cluster_ids)
    output_whole = lax.all_gather(output_weight, "mp", axis=0, tiled=True)
    query_whole = lax.all_gather(query_weight, "mp", axis=1, tiled=True)

    clusters = jnp.arange(MAX_CLUSTERS, dtype=jnp.int32)
    onehot = (ids_own[..., None] == clusters).astype(LOW)
    counts = jnp.sum(onehot, axis=1, dtype=F32)
    counts_pair = jnp.concatenate([counts[:half], counts[half:]], axis=0).reshape(2, n_dp, shard_rows)
    counts_pair = lax.all_to_all(counts_pair.transpose(1, 0, 2), "dp", 0, 0)
    inverse = 1.0 / jnp.maximum(jnp.sum(counts_pair, axis=0), 1.0)
    inverse = jnp.repeat(inverse.T, HEAD_DIM, axis=1)

    token_float = token_rows.astype(F32)
    flat = layer_norm(token_float, gain_one, shift_one).astype(LOW)
    head_shape = (seqs, local_rows, heads, HEAD_DIM)
    queries = (
        (jnp.dot(flat, query_weight, preferred_element_type=F32) + query_shift).astype(LOW).reshape(head_shape)
    )
    keys = jnp.dot(flat, key_weight, preferred_element_type=F32).astype(LOW).reshape(head_shape)
    values = (
        (jnp.dot(flat, value_weight, preferred_element_type=F32) + value_shift).astype(LOW).reshape(head_shape)
    )

    sums = paired(jnp.einsum("sthc,sthd->shcd", onehot, queries, preferred_element_type=F32))
    sums = lax.all_to_all(sums.reshape(n_dp, shard_rows, -1), "dp", 0, 0)
    centroid_shard = (jnp.sum(sums, axis=0) * inverse).astype(LOW)
    centroid = unpaired(gather_by_exchange(centroid_shard, "dp", n_dp), half, heads)

    scores = jnp.einsum("shcd,sthd->shct", centroid, keys, preferred_element_type=F32) * 0.125
    local_top = jnp.max(scores, axis=-1)
    exponent = jnp.exp(scores - local_top[..., None])
    local_total = jnp.sum(exponent, axis=-1)
    local_out = (
        jnp.einsum("shct,sthd->shcd", exponent.astype(LOW), values, preferred_element_type=F32)
        / local_total[..., None]
    )
    local_log = local_top + jnp.log(local_total)

    def log_lanes(log):
        parts = jnp.stack(split3(log), axis=-1)
        return jnp.concatenate([parts[:half], parts[half:]], axis=-1).reshape(table_rows, 6)

    packed = jnp.concatenate(
        [paired(local_out).astype(LOW), log_lanes(local_log), jnp.zeros((table_rows, 122), LOW)], axis=-1
    )
    packed = lax.all_to_all(packed.reshape(n_dp, shard_rows, 256), "dp", 0, 0)
    part_out = packed[..., :128].astype(F32)
    logs = packed[..., 128:134].astype(F32)
    logs = jnp.stack([logs[..., 0] + logs[..., 1] + logs[..., 2], logs[..., 3] + logs[..., 4] + logs[..., 5]], axis=-1)
    top = jnp.max(logs, axis=0)
    weight = jnp.exp(logs - top)
    total = jnp.sum(weight, axis=0)
    log_shard = top + jnp.log(total)
    weight = jnp.repeat(weight / total, HEAD_DIM, axis=-1)
    out_shard = jnp.sum(part_out * weight, axis=0)

    def gathered_table(shard):
        table = gather_by_exchange(shard, both_axes, n_all).reshape(n_dp, n_mp, shard_rows, 128)
        table = table.transpose(1, 0, 2, 3).reshape(n_mp, half, heads, MAX_CLUSTERS, 2, HEAD_DIM)
        return table.transpose(4, 1, 0, 2, 3, 5).reshape(seqs, all_heads, MAX_CLUSTERS, HEAD_DIM)

    out_table = gathered_table(out_shard.astype(LOW))
    onehot_all = (ids_all[..., None] == clusters).astype(LOW)
    attended = (
        jnp.einsum("sthc,shcd->sthd", onehot_all, out_table, preferred_element_type=F32)
        .astype(LOW)
        .reshape(count_rows, all_heads * HEAD_DIM)
    )
    hidden = (
        token_float + jnp.dot(attended, output_whole, preferred_element_type=F32) + output_shift
    )
    second_low = layer_norm(hidden, gain_two, shift_two).astype(LOW)
    grad_rows = whole(gather_rows(cotangent))

    expanded = jnp.dot(second_low, expand_weight, preferred_element_type=F32) + expand_shift
    act_grad = jnp.einsum("td,fd->tf", grad_rows, shrink_weight, preferred_element_type=F32)
    activated, gelu_back = jax.vjp(partial(jax.nn.gelu, approximate=False), expanded)
    activated = activated.astype(LOW)
    expand_grad = gelu_back(act_grad)[0].astype(LOW)
    second_part = jnp.einsum("tf,df->td", expand_grad, expand_weight, preferred_element_type=F32)
    second_grad = scatter_rows(pieces_of(second_part))

    ffn_part = jnp.dot(activated, shrink_weight, preferred_element_type=F32)
    ffn_out = scatter_rows(pieces_of(ffn_part))
    hidden_own = pieces_of(hidden)[0]
    result = (hidden_own + ffn_out + shrink_shift).astype(LOW)

    shrink_weight_grad = jnp.einsum("tf,td->fd", activated, grad_rows, preferred_element_type=F32)
    expand_weight_grad = jnp.einsum("td,tf->df", second_low, expand_grad, preferred_element_type=F32)
    expand_bias_grad = jnp.sum(expand_grad.astype(F32), axis=0)
    shrink_weight_grad, expand_weight_grad = lax.psum(
        (shrink_weight_grad.astype(LOW), expand_weight_grad.astype(LOW)), "dp"
    )

    cotangent_float = cotangent.astype(F32)
    _, second_back = jax.vjp(layer_norm, hidden_own, gain_two, shift_two)
    hidden_in_grad, second_gain_grad, second_shift_grad = second_back(second_grad)
    hidden_grad = cotangent_float + hidden_in_grad
    hidden_low = hidden_grad.astype(LOW)
    shrink_bias_grad = jnp.sum(cotangent_float, axis=(0, 1))
    output_bias_grad = jnp.sum(hidden_grad, axis=(0, 1))

    attended_grad = (
        jnp.einsum("std,ad->sta", hidden_low, output_whole, preferred_element_type=F32)
        .astype(LOW)
        .reshape(seqs, share_rows, all_heads, HEAD_DIM)
    )
    onehot_share = onehot_all[:, :share_rows]
    out_part = jnp.einsum("sthc,sthd->shcd", onehot_share, attended_grad, preferred_element_type=F32).astype(LOW)
    out_part = out_part.reshape(2, half, n_mp, heads * MAX_CLUSTERS, HEAD_DIM).transpose(2, 1, 3, 0, 4)
    out_part = out_part.reshape(n_mp, n_dp, shard_rows, 128).transpose(1, 0, 2, 3).reshape(n_all, shard_rows, 128)
    out_part = lax.all_to_all(out_part, both_axes, 0, 0)
    out_grad_shard = jnp.sum(out_part.astype(F32), axis=0).astype(LOW)
    product = out_grad_shard.astype(F32) * out_shard
    delta_shard = jnp.sum(product.reshape(shard_rows, 2, HEAD_DIM), axis=-1)
    lanes = jnp.stack([*split3(delta_shard), *split3(log_shard)], axis=-1).reshape(shard_rows, 12)
    packed = jnp.concatenate([out_grad_shard, lanes, jnp.zeros((shard_rows, 116), LOW)], axis=-1)
    packed = gather_by_exchange(packed, "dp", n_dp).reshape(table_rows, 256)
    out_grad = unpaired(packed[:, :128], half, heads)
    lanes = packed[:, 128:140].astype(F32).reshape(half, heads, MAX_CLUSTERS, 2, 2, 3).sum(axis=-1)
    lanes = jnp.concatenate([lanes[..., 0, :], lanes[..., 1, :]], axis=0)
    delta, log_all = lanes[..., 0], lanes[..., 1]

    probs = jnp.exp(scores - log_all[..., None])
    prob_grad = jnp.einsum("shcd,sthd->shct", out_grad, values, preferred_element_type=F32)
    score_grad = (probs * (prob_grad - delta[..., None]) * 0.125).astype(LOW)
    probs = probs.astype(LOW)
    centroid_part = paired(jnp.einsum("shct,sthd->shcd", score_grad, keys, preferred_element_type=F32))
    centroid_part = lax.all_to_all(centroid_part.reshape(n_dp, shard_rows, -1), "dp", 0, 0)
    query_shard = (jnp.sum(centroid_part, axis=0) * inverse).astype(LOW)
    query_table = gathered_table(query_shard)

    key_grad = (
        jnp.einsum("shct,shcd->sthd", score_grad, centroid, preferred_element_type=F32)
        .astype(LOW)
        .reshape(count_rows, head_width)
    )
    value_grad = (
        jnp.einsum("shct,shcd->sthd", probs, out_grad, preferred_element_type=F32)
        .astype(LOW)
        .reshape(count_rows, head_width)
    )
    key_weight_grad = jnp.einsum("td,ta->da", flat, key_grad, preferred_element_type=F32)
    value_weight_grad = jnp.einsum("td,ta->da", flat, value_grad, preferred_element_type=F32)
    value_bias_grad = jnp.sum(value_grad.astype(F32), axis=0)
    first_part = jnp.einsum("ta,da->td", key_grad, key_weight, preferred_element_type=F32) + jnp.einsum(
        "ta,da->td", value_grad, value_weight, preferred_element_type=F32
    )
    first_kv = scatter_rows(pieces_of(first_part))

    hidden_rows = whole(gather_rows(hidden_low))
    attended_own = lax.dynamic_slice_in_dim(attended, me * head_width, head_width, 1)
    output_weight_grad = jnp.einsum("ta,td->ad", attended_own, hidden_rows, preferred_element_type=F32)

    def reduced(grad):
        rows, columns = grad.shape
        parts = lax.all_to_all(grad.astype(LOW).reshape(n_dp, rows // n_dp, columns), "dp", 0, 0)
        part = jnp.sum(parts.astype(F32), axis=0).astype(LOW)
        return gather_by_exchange(part, "dp", n_dp).reshape(rows, columns).astype(F32)

    merged = reduced(
        jnp.concatenate([key_weight_grad, value_weight_grad, output_weight_grad.reshape(width, head_width)], axis=1)
    )
    key_weight_grad = merged[:, :head_width]
    value_weight_grad = merged[:, head_width : 2 * head_width]
    output_weight_grad = merged[:, 2 * head_width :].reshape(head_width, width)

    query_grad = jnp.einsum(
        "sthc,shcd->sthd", onehot_share, query_table, preferred_element_type=F32
    ).astype(LOW)
    first_grad = first_kv + jnp.einsum(
        "sta,da->std",
        query_grad.reshape(seqs, share_rows, all_heads * HEAD_DIM),
        query_whole,
        preferred_element_type=F32,
    )
    query_own = lax.dynamic_slice_in_dim(query_table, me * heads, heads, 1)
    query_rows = (
        jnp.einsum("sthc,shcd->sthd", onehot, query_own, preferred_element_type=F32)
        .astype(LOW)
        .reshape(count_rows, head_width)
    )
    query_weight_grad = reduced(jnp.einsum("td,ta->da", flat, query_rows, preferred_element_type=F32))
    query_bias_part = jnp.sum(counts[..., None] * query_own.astype(F32), axis=(0, 2)).reshape(head_width)

    _, first_back = jax.vjp(layer_norm, tokens.astype(F32), gain_one, shift_one)
    token_in_grad, first_gain_grad, first_shift_grad = first_back(first_grad)
    token_grad = hidden_grad + token_in_grad

    small = jnp.stack(
        [
            output_bias_grad,
            shrink_bias_grad,
            first_gain_grad,
            first_shift_grad,
            second_gain_grad,
            second_shift_grad,
            jnp.zeros_like(output_bias_grad).at[:head_width].set(query_bias_part).at[head_width : 2 * head_width].set(value_bias_grad),
            expand_bias_grad,
        ]
    )
    small = gather_by_exchange(small, both_axes, n_all).reshape(n_dp, n_mp, 8, width)
    small_all = jnp.sum(small[:, :, :6], axis=(0, 1))
    small_own = jnp.sum(lax.dynamic_index_in_dim(small[:, :, 6:], me, 1, keepdims=False), axis=0)
    return (
        result,
        token_grad,
        query_weight_grad,
        small_own[0, :head_width],
        key_weight_grad,
        value_weight_grad,
        small_own[0, head_width : 2 * head_width],
        output_weight_grad,
        small_all[0],
        expand_weight_grad.astype(F32),
        small_own[1],
        shrink_weight_grad.astype(F32),
        small_all[1],
        small_all[2],
        small_all[3],
        small_all[4],
        small_all[5],
    )


def solution(mesh):
    return jax.shard_map(
        shards,
        mesh=mesh,
        in_specs=(
            P(None, ("dp", "mp"), None),
            P(None, "dp", "mp"),
            P(None, "mp"),
            P("mp"),
            P(None, "mp"),
            P(None, "mp"),
            P("mp"),
            P("mp", None),
            P(),
            P(None, "mp"),
            P("mp"),
            P("mp", None),
            P(),
            P(),
            P(),
            P(),
            P(),
            P(None, ("dp", "mp"), None),
        ),
        out_specs=(
            P(None, ("dp", "mp"), None),
            P(None, ("dp", "mp"), None),
            P(None, "mp"),
            P("mp"),
            P(None, "mp"),
            P(None, "mp"),
            P("mp"),
            P("mp", None),
            P(),
            P(None, "mp"),
            P("mp"),
            P("mp", None),
            P(),
            P(),
            P(),
            P(),
            P(),
        ),
        check_vma=False,
    )
```

```python
from functools import partial

import jax
import jax.numpy as jnp
from jax import lax
from jax.experimental import pallas as pl
from jax.experimental.pallas import tpu as pltpu
from jax.sharding import PartitionSpec as P

HEAD_DIM = 64
CLUSTERS = 200
SLOTS = 256
NOTES = 4
PAIR = 2 * HEAD_DIM
F32 = jnp.float32
LOW = jnp.bfloat16
MIB = 2**20


def dot(left, right, left_dim=1, right_dim=0):
    return lax.dot_general(
        left, right, (((left_dim,), (right_dim,)), ((), ())), preferred_element_type=F32
    )


def lanes_of(rows, width=PAIR):
    return lax.broadcasted_iota(jnp.int32, (rows, width), 1)


def standard(values):
    average = jnp.mean(values, axis=-1, keepdims=True)
    centered = values - average
    variance = jnp.mean(centered * centered, axis=-1, keepdims=True)
    scale = lax.rsqrt(variance + 1e-05)
    return centered * scale, scale


def norm_back(grad, unit, scale, gain):
    inner = grad * gain
    first = jnp.mean(inner, axis=-1, keepdims=True)
    second = jnp.mean(inner * unit, axis=-1, keepdims=True)
    return scale * (inner - first - unit * second)


def split2(values):
    high = values.astype(LOW).astype(F32)
    return high, (values - high).astype(LOW).astype(F32)


def place(row, valid, size):
    return row + (size - valid) * (row // valid)


def windows(heads, valid, size):
    end = place(heads * CLUSTERS - 1, valid, size) // size * size + size
    found = []
    for h in range(heads):
        start = min(place(h * CLUSTERS, valid, size) // 16 * 16, end - SLOTS)
        runs = []
        for row in range(h * CLUSTERS, (h + 1) * CLUSTERS):
            at = place(row, valid, size) - start
            if runs and runs[-1][1] == at:
                runs[-1][1] = at + 1
            else:
                runs.append([at, at + 1])
        found.append((start, runs))
    return found


def to_notes(column):
    rows = column.shape[0]
    sheet = lax.broadcasted_iota(jnp.int32, (rows, PAIR), 0) == lanes_of(rows)
    found = []
    for p in range(2):
        lane = jnp.sum(jnp.where(sheet, column[:, p * HEAD_DIM : p * HEAD_DIM + 1], 0.0), axis=0, keepdims=True)
        found += list(split2(lane))
    return found


def from_notes(notes, rows):
    sheet = lax.broadcasted_iota(jnp.int32, (rows, PAIR), 0) == lanes_of(rows)
    found = []
    for p in range(2):
        lane = notes[2 * p : 2 * p + 1] + notes[2 * p + 1 : 2 * p + 2]
        found.append(jnp.sum(jnp.where(sheet, lane, 0.0), axis=-1, keepdims=True))
    return found


def with_notes(values, notes, valid):
    row = lax.broadcasted_iota(jnp.int32, values.shape, 0)
    for k, note in enumerate(notes):
        values = jnp.where(row == valid + k, note, values)
    return values


def notes_of(values, valid):
    row = lax.broadcasted_iota(jnp.int32, values.shape, 0)
    return jnp.concatenate(
        [jnp.sum(jnp.where(row == valid + k, values, 0.0), axis=0, keepdims=True) for k in range(NOTES)], axis=0
    )


def onehot_rows(places, start):
    rows = places.shape[0]
    return (lanes_of(rows, SLOTS) == places - start).astype(F32).astype(LOW)


def onehot_columns(places, start):
    columns = places.shape[1]
    return (lax.broadcasted_iota(jnp.int32, (SLOTS, columns), 0) == places - start).astype(F32).astype(LOW)


def side(tile, p):
    lane = lanes_of(tile.shape[0])
    return jnp.where((lane < HEAD_DIM) if p == 0 else (lane >= HEAD_DIM), tile, jnp.zeros_like(tile))


def head_side(values, h, p):
    tile = values[:, h // 2 * PAIR : (h // 2 + 1) * PAIR]
    if tile.shape[1] < PAIR:
        tile = jnp.concatenate([tile, jnp.zeros_like(tile)], axis=1)
    if h % 2 != p:
        tile = pltpu.roll(tile, HEAD_DIM, 1)
    return side(tile, p)


def valid_rows(window):
    row = lax.broadcasted_iota(jnp.int32, (SLOTS, 1), 0)
    kept = row < 0
    for first, end in window[1]:
        kept |= (row >= first) & (row < end)
    return kept


def call(body, grid, out_shape, in_specs, out_specs, scratch=()):
    return pl.pallas_call(
        body,
        grid=grid,
        out_shape=out_shape,
        in_specs=in_specs,
        out_specs=out_specs,
        scratch_shapes=list(scratch),
        compiler_params=pltpu.CompilerParams(
            vmem_limit_bytes=60 * MIB, dimension_semantics=("arbitrary",) * len(grid)
        ),
        cost_estimate=pl.CostEstimate(flops=1, bytes_accessed=1, transcendentals=0),
    )


def shape(dims, kind=LOW):
    return jax.ShapeDtypeStruct(tuple(dims), kind)


def step_spec(dims):
    rest = tuple(dims[1:])
    return pl.BlockSpec((1, *rest), lambda b: (b,) + (0,) * len(rest))


def table_spec(dims, groups):
    rest = tuple(dims[1:])
    return pl.BlockSpec((dims[0] // groups, *rest), lambda b: (b,) + (0,) * len(rest))


def full_spec(dims):
    return pl.BlockSpec(tuple(dims), lambda b: (0,) * len(dims))


def first_kernel(cuts, valid, *refs):
    me, own, near, far, diagonal, places, *rest = refs
    query, key, value, vectors, first_out, kv_out, sums_out, sheet = rest
    gain, shift = vectors[0:1], vectors[1:2]
    query_bias, value_bias = vectors[5:6, : query.shape[0]], vectors[6:7, : query.shape[0]]
    rows = own.shape[2]
    heads = len(cuts)
    wide = heads * PAIR
    sheet[...] = jnp.zeros_like(sheet)
    for p in range(2):
        tokens = jnp.concatenate([r[0, p] for r in (own, near, far, diagonal)], axis=0).astype(F32)
        unit, _ = standard(tokens)
        first = (unit * gain + shift).astype(LOW)
        first_out[0, p] = first
        queries = (dot(first, query[...], 1, 1) + query_bias).astype(LOW).astype(F32)
        keys = dot(first, key[...], 1, 1)
        values = dot(first, value[...], 1, 1) + value_bias
        one = side(jnp.ones((first.shape[0], PAIR), F32), p)
        for h, (start, _) in enumerate(cuts):
            kv_out[0, p, :, h * PAIR : (h + 1) * PAIR] = head_side(keys, h, p).astype(LOW)
            kv_out[0, p, :, wide + h * PAIR : wide + (h + 1) * PAIR] = head_side(values, h, p).astype(LOW)
            both = jnp.concatenate([head_side(queries, h, p), one], axis=1).astype(LOW)
            part = None
            for k in range(4):
                member = onehot_columns(places[0, p, me[0] ^ k, h : h + 1, :], start)
                term = dot(member, both[k * rows : (k + 1) * rows])
                part = term if part is None else part + term
            sheet[start : start + SLOTS] += part
    size = sums_out.shape[1]
    for d in range(sums_out.shape[0]):
        chunk = sheet[d * size : (d + 1) * size]
        notes = to_notes(chunk[:, PAIR:])
        sums_out[d] = with_notes(chunk[:, :PAIR], notes, valid).astype(LOW)


def scores_of(centroid, keys):
    return dot(centroid, keys, 1, 1) * 0.125


def attend_kernel(cuts, valid, centroid, kv, packed, sheet):
    wide = len(cuts) * PAIR
    count, size = packed.shape[0], packed.shape[1]
    table = centroid[...].reshape(count * size, PAIR)
    lane = lanes_of(SLOTS)
    sheet[...] = jnp.zeros_like(sheet)
    for h, window in enumerate(cuts):
        start = window[0]
        mine = table[start : start + SLOTS]
        out = jnp.zeros((SLOTS, PAIR), F32)
        log = jnp.zeros((SLOTS, PAIR), F32)
        for p in range(2):
            keys = kv[0, p, :, h * PAIR : (h + 1) * PAIR]
            values = kv[0, p, :, wide + h * PAIR : wide + (h + 1) * PAIR]
            scores = scores_of(mine, keys)
            top = jnp.max(scores, axis=-1, keepdims=True)
            exponent = jnp.exp(scores - top)
            total = jnp.sum(exponent, axis=-1, keepdims=True)
            out += dot(exponent.astype(LOW), values) / total
            log = jnp.where((lane < HEAD_DIM) if p == 0 else (lane >= HEAD_DIM), top + jnp.log(total), log)
        both = jnp.concatenate([out, log], axis=1)
        sheet[start : start + SLOTS] += jnp.where(valid_rows(window), both, 0.0)
    for d in range(count):
        chunk = sheet[d * size : (d + 1) * size]
        packed[d] = with_notes(chunk[:, :PAIR], to_notes(chunk[:, PAIR:]), valid).astype(LOW)


def half_wise(first, second, rows):
    return jnp.where(lanes_of(rows) < HEAD_DIM, first, second)


def merge_kernel(valid, packed, copies, out_shard):
    count, rows = packed.shape[0], packed.shape[1]
    logs, parts = [], []
    for i in range(count):
        part = packed[i].astype(F32)
        logs.append(half_wise(*from_notes(notes_of(part, valid), rows), rows))
        parts.append(part)
    top = logs[0]
    for log in logs[1:]:
        top = jnp.maximum(top, log)
    total = jnp.zeros((rows, PAIR), F32)
    out = jnp.zeros((rows, PAIR), F32)
    for i in range(count):
        weight = jnp.exp(logs[i] - top)
        total += weight
        out += weight * parts[i]
    out = out / total
    out_shard[...] = out
    low = with_notes(out, to_notes(top + jnp.log(total)), valid).astype(LOW)
    for k in range(copies.shape[0]):
        copies[k] = low


def join_heads(picked, p):
    rows = picked[0].shape[0]
    lane = lanes_of(rows)
    tiles = []
    for g in range(0, len(picked), 2):
        even = picked[g]
        odd = picked[g + 1] if g + 1 < len(picked) else even
        if p == 0:
            tile = jnp.where(lane < HEAD_DIM, even, pltpu.roll(odd, HEAD_DIM, 1))
        else:
            tile = jnp.where(lane < HEAD_DIM, pltpu.roll(even, HEAD_DIM, 1), odd)
        tiles.append(tile)
    joined = jnp.concatenate(tiles, axis=1)
    return joined[:, : len(picked) * HEAD_DIM]


def gelu_parts(values):
    area = 0.5 * (1.0 + lax.erf(values * 0.7071067811865476))
    density = jnp.exp(-0.5 * values * values) * 0.3989422804014327
    return values * area, area + values * density


def lay_out(table, whole):
    size = table.shape[2]
    for m in range(table.shape[1]):
        for d in range(table.shape[0]):
            whole[m, d * size : (d + 1) * size] = table[d, m]


def dense_kernel(cuts, which, *refs):
    (
        me,
        table,
        places,
        tokens_a,
        tokens_b,
        cot_a,
        cot_b,
        output_weight,
        expand_weight,
        shrink_weight,
        vectors,
        second_a,
        second_b,
        ffn_a,
        ffn_b,
        hidden_out,
        mine_out,
        normed_out,
        activated_out,
        expand_out,
        bias_out,
        attended,
        whole,
    ) = refs
    rows = tokens_a.shape[2]
    groups = table.shape[1]
    lay_out(table, whole)
    for p in range(2):
        picked, mine = [], []
        for m in range(groups):
            column = jnp.concatenate([places[m, 0, p, me[0] ^ (2 * which + j)] for j in range(2)], axis=0)
            for h, (start, _) in enumerate(cuts):
                member = onehot_rows(column[:, h : h + 1], start)
                picked.append(dot(member, whole[m, start : start + SLOTS]))
        attended[p * 2 * rows : (p + 1) * 2 * rows] = join_heads(picked, p).astype(LOW)
        column = jnp.concatenate([places[me[0], 0, p, me[0] ^ (2 * which + j)] for j in range(2)], axis=0)
        for h, (start, _) in enumerate(cuts):
            member = onehot_rows(column[:, h : h + 1], start)
            mine.append(dot(member, whole[me[0], start : start + SLOTS]))
        mine_out[0, p * 2 * rows : (p + 1) * 2 * rows] = join_heads(mine, p).astype(LOW)
    tokens = jnp.concatenate([tokens_a[0, 0], tokens_b[0, 0], tokens_a[0, 1], tokens_b[0, 1]], axis=0)
    cotangent = jnp.concatenate([cot_a[0, 0], cot_b[0, 0], cot_a[0, 1], cot_b[0, 1]], axis=0)
    hidden = tokens.astype(F32) + dot(attended[...], output_weight[...]) + vectors[4:5]
    unit, _ = standard(hidden)
    normed = (unit * vectors[2:3] + vectors[3:4]).astype(LOW)
    expanded = dot(normed, expand_weight[...]) + jnp.concatenate([vectors[k : k + 1] for k in range(7, vectors.shape[0])], axis=1)
    active, slope = gelu_parts(expanded)
    active = active.astype(LOW)
    back = (dot(cotangent, shrink_weight[...], 1, 1) * slope).astype(LOW)
    second = dot(back, expand_weight[...], 1, 1)
    ffn = dot(active, shrink_weight[...])
    for j, (second_ref, ffn_ref) in enumerate(((second_a, ffn_a), (second_b, ffn_b))):
        for p in range(2):
            at = (2 * p + j) * rows
            second_ref[0, p] = second[at : at + rows].astype(second_ref.dtype)
            ffn_ref[0, p] = ffn[at : at + rows].astype(ffn_ref.dtype)
    for p in range(2):
        hidden_out[0, p] = hidden[2 * p * rows : (2 * p + 1) * rows]
    normed_out[0] = normed
    activated_out[0] = active
    expand_out[0] = back

    @pl.when(pl.program_id(0) == 0)
    def _():
        bias_out[...] = jnp.zeros_like(bias_out)

    bias_out[...] += jnp.sum(back.astype(F32), axis=0, keepdims=True)


def grads_kernel(terms, steps, *refs):
    refs = list(refs)
    products = []
    for pieces in terms:
        lefts = [refs.pop(0) for _ in range(2)]
        rights = [refs.pop(0) for _ in range(4 if pieces else 2)]
        if pieces:
            near, far = rights[:2], rights[2:]
            right = [r[0, p] for pair in (near, far) for p in range(2) for r in pair]
        else:
            right = [r[0] for r in rights]
        products.append(
            dot(jnp.concatenate([v[0] for v in lefts], axis=0), jnp.concatenate(right, axis=0), 0, 0)
        )
    outs, totals = refs[: len(terms)], refs[len(terms) :]
    for k, (product, out) in enumerate(zip(products, outs)):
        if steps == 1:
            out[...] = product.astype(LOW)
            continue
        total = totals[k]
        total[...] = jnp.where(pl.program_id(0) == 0, product, total[...] + product)
        out[...] = total[...].astype(LOW)


def hidden_kernel(cuts, *refs):
    (
        own,
        near,
        far,
        diagonal,
        hidden,
        cot,
        places,
        output_weight,
        vectors,
        grad_out,
        low_out,
        table_out,
        small_out,
        whole,
    ) = refs
    groups, heads = table_out.shape[1], len(cuts)
    small = [jnp.zeros((1, own.shape[3]), F32) for _ in range(4)]
    parts = []
    for p in range(2):
        grad = own[0, p].astype(F32) + near[0, p].astype(F32) + far[0, p].astype(F32) + diagonal[0, p].astype(F32)
        unit, scale = standard(hidden[0, p])
        dy = cot[0, p].astype(F32)
        total = dy + norm_back(grad, unit, scale, vectors[2:3])
        grad_out[0, p] = total
        low = total.astype(LOW)
        low_out[0, p] = low
        for k, row in enumerate((total, dy, grad * unit, grad)):
            small[k] += jnp.sum(row, axis=0, keepdims=True)
        parts.append(dot(low, output_weight[...], 1, 1))
    whole[...] = jnp.zeros_like(whole)
    for k in range(groups * heads):
        m, h = k // heads, k % heads
        start = cuts[h][0]
        found = None
        for p in range(2):
            member = onehot_columns(places[0, p, k : k + 1, :], start)
            term = dot(member, head_side(parts[p], k, p).astype(LOW))
            found = term if p == 0 else found + term
        whole[m, start : start + SLOTS] += found
    size = table_out.shape[2]
    for m in range(groups):
        for d in range(table_out.shape[0]):
            table_out[d, m] = whole[m, d * size : (d + 1) * size].astype(LOW)

    @pl.when(pl.program_id(0) == 0)
    def _():
        small_out[...] = jnp.zeros_like(small_out)

    for k in range(4):
        small_out[k : k + 1, :] += small[k]


def out_grad_kernel(valid, parts, out_shard, copies):
    count, rows = parts.shape[0], parts.shape[1]
    total = jnp.zeros((rows, PAIR), F32)
    for i in range(count):
        total += parts[i].astype(F32)
    total = total.astype(LOW).astype(F32)
    product = total * out_shard[...]
    deltas = [jnp.sum(side(product, p), axis=-1, keepdims=True) for p in range(2)]
    low = with_notes(total, to_notes(half_wise(*deltas, rows)), valid).astype(LOW)
    for k in range(copies.shape[0]):
        copies[k] = low


def back_kernel(cuts, valid, me, centroid, kv, grads, out_table, part_out, prob_out, score_out, sheet, columns):
    wide = len(cuts) * PAIR
    count, size = part_out.shape[0], part_out.shape[1]
    table = centroid[...].reshape(count * size, PAIR)
    grad_table = grads[...].reshape(count * size, PAIR)
    for d in range(count):
        delta = from_notes(notes_of(grads[d].astype(F32), valid), size)
        log = from_notes(notes_of(out_table[d, me[0]].astype(F32), valid), size)
        for k, column in enumerate((*delta, *log)):
            columns[d * size : (d + 1) * size, k * PAIR : (k + 1) * PAIR] = jnp.broadcast_to(column, (size, PAIR))
    sheet[...] = jnp.zeros_like(sheet)
    for h, window in enumerate(cuts):
        start = window[0]
        mine, out_grad = table[start : start + SLOTS], grad_table[start : start + SLOTS]
        kept = valid_rows(window)
        part = None
        for p in range(2):
            keys = kv[0, p, :, h * PAIR : (h + 1) * PAIR]
            values = kv[0, p, :, wide + h * PAIR : wide + (h + 1) * PAIR]
            delta = columns[start : start + SLOTS, p * PAIR : p * PAIR + 1]
            log = columns[start : start + SLOTS, (2 + p) * PAIR : (2 + p) * PAIR + 1]
            probs = jnp.where(kept, jnp.exp(scores_of(mine, keys) - log), 0.0)
            grad = (probs * (dot(out_grad, values, 1, 1) - delta) * 0.125).astype(LOW)
            term = dot(grad, keys)
            part = term if p == 0 else part + term
            prob_out[0, p, h] = probs.astype(LOW)
            score_out[0, p, h] = grad
        sheet[start : start + SLOTS] += part
    for d in range(count):
        part_out[d] = sheet[d * size : (d + 1) * size].astype(LOW)


def kv_kernel(cuts, *refs):
    centroid, out_grads, probs, grads, key_weight, value_weight, key_out, value_out, own, near, far, diagonal = refs
    share = own.shape[2]
    count, size = centroid.shape[0], centroid.shape[1]
    table = centroid[...].reshape(count * size, PAIR)
    grad_table = out_grads[...].reshape(count * size, PAIR)
    for p in range(2):
        key_parts, value_parts = [], []
        for h, (start, _) in enumerate(cuts):
            key_parts.append(dot(grads[0, p, h], table[start : start + SLOTS], 0, 0))
            value_parts.append(dot(probs[0, p, h], grad_table[start : start + SLOTS], 0, 0))
        keys = join_heads(key_parts, p).astype(LOW)
        values = join_heads(value_parts, p).astype(LOW)
        key_out[0, p] = keys
        value_out[0, p] = values
        first = dot(keys, key_weight[...]) + dot(values, value_weight[...])
        for k, ref in enumerate((own, near, far, diagonal)):
            ref[0, p] = first[k * share : (k + 1) * share].astype(ref.dtype)


def centroid_kernel(valid, parts, copies, inverse):
    count, rows = parts.shape[0], parts.shape[1]
    total = parts[0].astype(F32)
    for i in range(1, count):
        total += parts[i].astype(F32)
    counts = half_wise(*from_notes(notes_of(total, valid), rows), rows)
    share = 1.0 / jnp.maximum(counts, 1.0)
    inverse[...] = share
    row = lax.broadcasted_iota(jnp.int32, (rows, PAIR), 0)
    low = jnp.where(row < valid, total * share, 0.0).astype(LOW)
    for k in range(copies.shape[0]):
        copies[k] = low


def mean_kernel(parts, inverse, copies):
    total = parts[0].astype(F32)
    for i in range(1, parts.shape[0]):
        total += parts[i].astype(F32)
    low = (total * inverse[...]).astype(LOW)
    for k in range(copies.shape[0]):
        copies[k] = low


def last_kernel(cuts, *refs):
    (
        me,
        table,
        places,
        own,
        near,
        far,
        diagonal,
        tokens,
        hidden_grad,
        weight,
        vectors,
        token_out,
        query_out,
        small_out,
        whole,
    ) = refs
    groups = table.shape[1]
    lay_out(table, whole)
    small = [jnp.zeros((1, own.shape[3]), F32) for _ in range(2)]
    for p in range(2):
        picked = []
        for m in range(groups):
            column = places[m, 0, p, me[0]]
            for h, (start, _) in enumerate(cuts):
                member = onehot_rows(column[:, h : h + 1], start)
                picked.append(dot(member, whole[m, start : start + SLOTS]))
        query = join_heads(picked, p).astype(LOW)
        grad = own[0, p].astype(F32) + near[0, p].astype(F32) + far[0, p].astype(F32) + diagonal[0, p].astype(F32)
        grad += dot(query, weight[...])
        unit, scale = standard(tokens[0, p].astype(F32))
        token_out[0, p] = hidden_grad[0, p] + norm_back(grad, unit, scale, vectors[0:1])
        for k, row in enumerate((grad * unit, grad)):
            small[k] += jnp.sum(row, axis=0, keepdims=True)
        picked = []
        column = jnp.concatenate([places[me[0], 0, p, me[0] ^ k] for k in range(4)], axis=0)
        for h, (start, _) in enumerate(cuts):
            member = onehot_rows(column[:, h : h + 1], start)
            picked.append(dot(member, whole[me[0], start : start + SLOTS]))
        query_out[0, p] = join_heads(picked, p).astype(LOW)

    @pl.when(pl.program_id(0) == 0)
    def _():
        small_out[...] = jnp.zeros_like(small_out)

    for k in range(2):
        small_out[k : k + 1, :] += small[k]


def partner(value, step):
    size = lax.axis_size("mp")
    return lax.ppermute(value, "mp", [(i, i ^ step) for i in range(size)])


def gather_rows(value):
    far = partner(value, 2)
    near = partner(value, 1)
    return value, near, far, partner(far, 1)


def exchange(copies, axes):
    return lax.all_to_all(copies, axes, 0, 0)


def after(value, *others):
    return lax.optimization_barrier((value, others))[0]


def together(*values):
    return lax.optimization_barrier(values)


def shards(
    tokens,
    cluster_ids,
    query_weight,
    query_bias,
    key_weight,
    value_weight,
    value_bias,
    output_weight,
    output_bias,
    expand_weight,
    expand_bias,
    shrink_weight,
    shrink_bias,
    first_gain,
    first_shift,
    second_gain,
    second_shift,
    cotangent,
):
    seqs, share, width = tokens.shape
    heads = cluster_ids.shape[2]
    hidden_units = expand_weight.shape[1]
    n_dp, n_mp = lax.axis_size("dp"), lax.axis_size("mp")
    both = ("dp", "mp")
    n_all = n_dp * n_mp
    all_heads = heads * n_mp
    half = seqs // 2
    local = share * n_mp
    head_width = heads * HEAD_DIM
    wide = heads * PAIR
    valid = half * heads * CLUSTERS // n_dp
    size = -(-(valid + NOTES) // 16) * 16
    per_pair = n_dp // half
    cuts = windows(heads, valid, size)
    table_rows = per_pair * size
    me = lax.axis_index("mp")
    me_ref = me.astype(jnp.int32).reshape(1)

    def sequences(value):
        return value.reshape(half, 2, *value.shape[1:])

    pieces = gather_rows(sequences(tokens))
    places = place(cluster_ids + jnp.arange(heads, dtype=jnp.int32) * CLUSTERS, valid, size)
    places_row = places.reshape(half, 2, n_mp, share, heads).transpose(0, 1, 2, 4, 3)
    places_all = jnp.stack(gather_rows(places.reshape(half, 2, n_mp, share, heads)))
    places_all = places_all.reshape(n_mp // 2, 2, *places_all.shape[1:])
    places_all = jnp.where(me % 2 == 1, places_all[:, ::-1], places_all)
    places_all = jnp.where(me // 2 == 1, places_all[::-1], places_all)
    places_all = places_all.reshape(n_mp, half, 2, n_mp, share, heads)
    places_share = lax.dynamic_index_in_dim(places_all, me, 3, keepdims=False)
    places_share = places_share.transpose(1, 2, 0, 4, 3).reshape(half, 2, all_heads, share)
    vectors = jnp.stack(
        [
            jnp.pad(v.astype(F32), (0, width - v.shape[0]))
            for v in (first_gain, first_shift, second_gain, second_shift, output_bias, query_bias, value_bias)
        ]
        + [expand_bias.astype(F32).reshape(-1, width)[k] for k in range(hidden_units // width)]
    )
    *pieces, places_row, vectors = together(*pieces, places_row, vectors)
    output_whole = lax.all_gather(output_weight, "mp", axis=0, tiled=True)
    query_turned, key_turned, value_turned = query_weight.T, key_weight.T, value_weight.T
    query_whole = lax.all_gather(query_turned, "mp", axis=0, tiled=True)

    piece_dims = (half, 2, share, width)
    piece_spec = step_spec(piece_dims)
    square_spec = full_spec((width, width))
    head_spec = full_spec((head_width, width))
    me_spec = pl.BlockSpec(memory_space=pltpu.SMEM)
    kv_dims = (half, 2, local, 2 * wide)
    table_dims = (n_dp, size, PAIR)
    shard_dims = (size, PAIR)
    copies_dims = (n_all, *shard_dims)
    all_dims = (n_dp, n_mp, *shard_dims)
    sheet = pltpu.VMEM((table_rows, 2 * PAIR), F32)
    group_scratch = pltpu.VMEM((n_mp, table_rows, PAIR), LOW)
    places_spec = pl.BlockSpec((n_mp, 1, 2, n_mp, share, heads), lambda b: (0, b, 0, 0, 0, 0))
    vectors_spec = full_spec(vectors.shape)

    first, kv, sums = call(
        partial(first_kernel, cuts, valid),
        (half,),
        (shape((half, 2, local, width)), shape(kv_dims), shape(table_dims)),
        [me_spec]
        + [piece_spec] * 4
        + [step_spec((half, 2, n_mp, heads, share))]
        + [head_spec] * 3
        + [vectors_spec],
        (step_spec((half, 2, local, width)), step_spec(kv_dims), table_spec(table_dims, half)),
        [sheet],
    )(
        me_ref,
        *pieces,
        places_row,
        query_turned,
        key_turned,
        value_turned,
        vectors,
    )
    cotangent_pairs = sequences(cotangent)
    cot_start = after(cotangent_pairs, sums)
    cot_far, cot_near = partner(cot_start, 2), partner(cot_start, 1)

    sums = exchange(sums, "dp")
    sums, cot_far, cot_near = together(sums, cot_far, cot_near)
    cot_diagonal = partner(cot_far, 1)
    copies, inverse = call(
        partial(centroid_kernel, valid),
        (1,),
        (shape(table_dims), shape(shard_dims, F32)),
        [full_spec(table_dims)],
        (full_spec(table_dims), full_spec(shard_dims)),
    )(sums)
    centroid = exchange(copies, "dp")
    centroid, cot_diagonal = together(centroid, cot_diagonal)

    packed = call(
        partial(attend_kernel, cuts, valid),
        (half,),
        shape(table_dims),
        [table_spec(table_dims, half), step_spec(kv_dims)],
        table_spec(table_dims, half),
        [sheet],
    )(centroid, kv)
    packed = exchange(packed, "dp")
    packed, output_whole, query_whole, places_all = together(packed, output_whole, query_whole, places_all)
    copies, out_shard = call(
        partial(merge_kernel, valid),
        (1,),
        (shape(copies_dims), shape(shard_dims, F32)),
        [full_spec(table_dims)],
        (full_spec(copies_dims), full_spec(shard_dims)),
    )(packed)
    out_table = exchange(copies, both).reshape(all_dims)
    out_table, places_share = together(out_table, places_share)

    dense_rows = 4 * share

    def dense(which, kinds, tokens_a, tokens_b, cot_a, cot_b):
        dims = (half, dense_rows)
        return call(
            partial(dense_kernel, cuts, which),
            (half,),
            (
                shape(piece_dims, kinds[0]),
                shape(piece_dims, kinds[1]),
                shape(piece_dims, kinds[0]),
                shape(piece_dims, kinds[1]),
                shape(piece_dims, F32),
                shape((*dims, head_width)),
                shape((*dims, width)),
                shape((*dims, hidden_units)),
                shape((*dims, hidden_units)),
                shape((1, hidden_units), F32),
            ),
            [me_spec, table_spec(all_dims, half), places_spec]
            + [piece_spec] * 4
            + [square_spec, full_spec((width, hidden_units)), full_spec((hidden_units, width)), vectors_spec],
            (
                *[piece_spec] * 5,
                step_spec((*dims, head_width)),
                step_spec((*dims, width)),
                step_spec((*dims, hidden_units)),
                step_spec((*dims, hidden_units)),
                full_spec((1, hidden_units)),
            ),
            [pltpu.VMEM((dense_rows, width), LOW), group_scratch],
        )(
            me_ref,
            out_table,
            places_all,
            tokens_a,
            tokens_b,
            cot_a,
            cot_b,
            output_whole,
            expand_weight,
            shrink_weight,
            vectors,
        )

    beyond = dense(1, (LOW, LOW), pieces[2], pieces[3], cot_far, cot_diagonal)
    far_in, diagonal_in = partner(beyond[0], 2), partner(beyond[1], 3)
    inside = dense(0, (F32, LOW), after(pieces[0], *beyond), pieces[1], cotangent_pairs, cot_near)
    near_in = partner(inside[1], 1)
    hidden_own = inside[4]

    def grads(terms, shapes, operands):
        specs = []
        for value in operands:
            specs.append(step_spec(value.shape))
        return call(
            partial(grads_kernel, terms, half),
            (half,),
            tuple(shape(dims) for dims in shapes),
            specs,
            tuple(full_spec(dims) for dims in shapes),
            [] if half == 1 else [pltpu.VMEM(dims, F32) for dims in shapes],
        )(*operands)

    shrink_weight_grad, expand_weight_grad = grads(
        (True, False),
        ((hidden_units, width), (width, hidden_units)),
        (beyond[7], inside[7], cot_far, cot_diagonal, cotangent_pairs, cot_near)
        + (beyond[6], inside[6], beyond[8], inside[8]),
    )
    expand_bias_grad = beyond[9] + inside[9]
    near_in, far_in, diagonal_in, shrink_weight_grad, expand_weight_grad = together(
        near_in, far_in, diagonal_in, shrink_weight_grad, expand_weight_grad
    )
    ffn_shard = lax.psum_scatter(
        jnp.concatenate([shrink_weight_grad, expand_weight_grad.reshape(hidden_units, width)], axis=0),
        "dp",
        scatter_dimension=0,
        tiled=True,
    )

    hidden_grad, hidden_low, out_part, small_two = call(
        partial(hidden_kernel, cuts),
        (half,),
        (shape(piece_dims, F32), shape(piece_dims), shape(all_dims), shape((8, width), F32)),
        [piece_spec] * 6 + [step_spec((half, 2, all_heads, share)), square_spec, vectors_spec],
        (piece_spec, piece_spec, table_spec(all_dims, half), full_spec((8, width))),
        [pltpu.VMEM((n_mp, table_rows, PAIR), F32)],
    )(
        inside[0],
        near_in,
        far_in,
        diagonal_in,
        hidden_own,
        cotangent_pairs,
        places_share,
        output_whole,
        vectors,
    )
    out_part = exchange(out_part.reshape(copies_dims), both)
    out_grad = call(
        partial(out_grad_kernel, valid),
        (1,),
        shape(table_dims),
        [full_spec(copies_dims), full_spec(shard_dims)],
        full_spec(table_dims),
    )(out_part, out_shard)
    out_grad = exchange(out_grad, "dp")
    low_start = after(hidden_low, out_grad)
    low_near, low_far, low_diagonal = (partner(low_start, k) for k in (1, 2, 3))

    score_dims = (half, 2, heads, SLOTS, local)
    centroid_part, probs, score_grad = call(
        partial(back_kernel, cuts, valid),
        (half,),
        (shape(table_dims), shape(score_dims), shape(score_dims)),
        [me_spec, table_spec(table_dims, half), step_spec(kv_dims)]
        + [table_spec(table_dims, half), table_spec(all_dims, half)],
        (table_spec(table_dims, half), step_spec(score_dims), step_spec(score_dims)),
        [pltpu.VMEM((table_rows, PAIR), F32), pltpu.VMEM((table_rows, 4 * PAIR), F32)],
    )(me_ref, centroid, kv, out_grad, out_table)
    centroid_part = exchange(centroid_part, "dp")

    grad_dims = (half, 2, local, head_width)
    key_grad, value_grad, *first_parts = call(
        partial(kv_kernel, cuts),
        (half,),
        (shape(grad_dims), shape(grad_dims), shape(piece_dims, F32), *[shape(piece_dims)] * 3),
        [table_spec(table_dims, half)] * 2
        + [step_spec(score_dims), step_spec(score_dims)]
        + [head_spec] * 2,
        (step_spec(grad_dims), step_spec(grad_dims), *[piece_spec] * 4),
    )(centroid, out_grad, probs, score_grad, key_turned, value_turned)

    count_rows = seqs * local
    first_flat = first.reshape(count_rows, width)
    value_flat = value_grad.reshape(count_rows, head_width)
    key_weight_grad = dot(key_grad.reshape(count_rows, head_width), first_flat, 0, 0).astype(LOW)
    value_weight_grad = dot(value_flat, first_flat, 0, 0).astype(LOW)
    value_bias_grad = jnp.sum(value_flat.astype(F32), axis=0)
    centroid_part, ffn_shard, low_near, low_far, low_diagonal, *first_parts = together(
        centroid_part, ffn_shard, low_near, low_far, low_diagonal, *first_parts
    )
    ffn_grads = lax.all_gather(ffn_shard, "dp", axis=0, tiled=True)
    (output_weight_grad,) = grads(
        (True,),
        ((head_width, width),),
        (beyond[5], inside[5], low_far, low_diagonal, hidden_low, low_near),
    )
    first_in = [partner(first_parts[k], k) for k in (1, 2, 3)]
    query_copies = call(
        mean_kernel,
        (1,),
        shape(copies_dims),
        [full_spec(table_dims), full_spec(shard_dims)],
        full_spec(copies_dims),
    )(centroid_part, inverse)
    query_table = exchange(query_copies, both).reshape(all_dims)
    def cut(value, count):
        rows, columns = value.shape[0] // count, value.shape[1]
        value = value.reshape(count, n_dp, rows // n_dp, columns).transpose(1, 0, 2, 3)
        return value.reshape(n_dp, count * rows // n_dp, columns)

    def scattered(value, count):
        return jnp.sum(exchange(cut(value, count), "dp").astype(F32), axis=0)

    def thirds(value):
        high = lax.reduce_precision(value, 8, 7)
        middle = lax.reduce_precision(value - high, 8, 7)
        return jnp.concatenate([high, middle, value - high - middle], axis=-2).astype(LOW)

    query_table, key_weight_grad, value_weight_grad, output_weight_grad, *first_in = together(
        query_table, key_weight_grad, value_weight_grad, output_weight_grad, *first_in
    )
    ffn_far, ffn_diagonal = partner(after(beyond[2], query_table), 2), partner(after(beyond[3], query_table), 3)
    ffn_near = partner(after(inside[3], query_table), 1)
    result = (
        hidden_own
        + inside[2]
        + ffn_near.astype(F32)
        + ffn_far.astype(F32)
        + ffn_diagonal.astype(F32)
        + shrink_bias.astype(F32)
    ).astype(LOW)
    early = scattered(jnp.concatenate([key_weight_grad, value_weight_grad, output_weight_grad]), 3)

    token_grad, query_grad, small_one = call(
        partial(last_kernel, cuts),
        (half,),
        (shape(piece_dims, F32), shape(grad_dims), shape((8, width), F32)),
        [me_spec, table_spec(all_dims, half), places_spec] + [piece_spec] * 6 + [square_spec, vectors_spec],
        (piece_spec, step_spec(grad_dims), full_spec((8, width))),
        [group_scratch],
    )(
        me_ref,
        query_table,
        places_all,
        first_parts[0],
        *first_in,
        pieces[0],
        hidden_grad,
        query_whole,
        vectors,
    )
    query_flat = query_grad.reshape(count_rows, head_width)
    query_weight_grad = dot(query_flat, first_flat, 0, 0).astype(LOW)
    query_bias_grad = jnp.sum(query_flat.astype(F32), axis=0)
    sums = jnp.concatenate([small_two[:4], small_one[:2]], axis=0)
    sums += partner(sums, 1)
    sums += partner(sums, 2)
    biases = jnp.concatenate([query_bias_grad, value_bias_grad, jnp.zeros((width - 2 * head_width,), F32)])
    small = jnp.concatenate([sums, biases[None], expand_bias_grad], axis=0)
    part = 8 * width // n_dp
    small = small.reshape(8, n_dp, width // n_dp).transpose(1, 0, 2).reshape(n_dp, 1, part)
    small = jnp.pad(small, ((0, 0), (0, 0), (0, width - part)))
    late = jnp.concatenate([cut(query_weight_grad, 1), thirds(small)], axis=1)
    late, ffn_grads = together(exchange(late, "dp"), ffn_grads)
    late = jnp.sum(late.astype(F32), axis=0)
    each = head_width // n_dp
    small = jnp.sum(late[each:], axis=0, keepdims=True)
    shard = jnp.concatenate([early.astype(LOW), late[:each].astype(LOW), thirds(small)], axis=0)
    found = exchange(jnp.broadcast_to(shard[None], (n_dp, *shard.shape)), "dp")
    weight_grads = [
        found[:, k * each : (k + 1) * each].reshape(head_width, width).astype(F32) for k in range(4)
    ]
    small = jnp.sum(found[:, 4 * each :].astype(F32), axis=1)[:, :part]
    small = small.reshape(n_dp, 8, width // n_dp).transpose(1, 0, 2).reshape(8, width)
    return (
        result.reshape(tokens.shape),
        token_grad.reshape(tokens.shape),
        weight_grads[3].T,
        small[6, :head_width],
        weight_grads[0].T,
        weight_grads[1].T,
        small[6, head_width : 2 * head_width],
        weight_grads[2],
        small[0],
        ffn_grads[hidden_units:].reshape(width, hidden_units).astype(F32),
        small[7],
        ffn_grads[:hidden_units].astype(F32),
        small[1],
        small[4],
        small[5],
        small[2],
        small[3],
    )


def solution(mesh):
    rows = P(None, ("dp", "mp"), None)
    columns, heads, vector, whole = P(None, "mp"), P("mp", None), P("mp"), P()
    return jax.shard_map(
        shards,
        mesh=mesh,
        in_specs=(
            rows,
            P(None, "dp", "mp"),
            columns,
            vector,
            columns,
            columns,
            vector,
            heads,
            whole,
            columns,
            vector,
            heads,
            whole,
            whole,
            whole,
            whole,
            whole,
            rows,
        ),
        out_specs=(
            rows,
            rows,
            columns,
            vector,
            columns,
            columns,
            vector,
            heads,
            whole,
            columns,
            vector,
            heads,
            whole,
            whole,
            whole,
            whole,
            whole,
        ),
        check_vma=False,
    )
```

```python
from functools import partial

import jax
import jax.numpy as jnp
from jax import lax
from jax.experimental import pallas as pl
from jax.experimental.pallas import tpu as pltpu
from jax.sharding import PartitionSpec as P

HEAD_DIM = 64
CLUSTERS = 200
SLOTS = 256
NOTES = 4
PAIR = 2 * HEAD_DIM
F32 = jnp.float32
LOW = jnp.bfloat16
MIB = 2**20


def dot(left, right, left_dim=1, right_dim=0):
    return lax.dot_general(
        left, right, (((left_dim,), (right_dim,)), ((), ())), preferred_element_type=F32
    )


def lanes_of(rows, width=PAIR):
    return lax.broadcasted_iota(jnp.int32, (rows, width), 1)


def standard(values):
    average = jnp.mean(values, axis=-1, keepdims=True)
    centered = values - average
    variance = jnp.mean(centered * centered, axis=-1, keepdims=True)
    scale = lax.rsqrt(variance + 1e-05)
    return centered * scale, scale


def norm_back(grad, unit, scale, gain):
    inner = grad * gain
    first = jnp.mean(inner, axis=-1, keepdims=True)
    second = jnp.mean(inner * unit, axis=-1, keepdims=True)
    return scale * (inner - first - unit * second)


def split2(values):
    high = values.astype(LOW).astype(F32)
    return high, (values - high).astype(LOW).astype(F32)


def place(row, valid, size):
    return row + (size - valid) * (row // valid)


def windows(heads, valid, size):
    end = place(heads * CLUSTERS - 1, valid, size) // size * size + size
    found = []
    for h in range(heads):
        start = min(place(h * CLUSTERS, valid, size) // 16 * 16, end - SLOTS)
        runs = []
        for row in range(h * CLUSTERS, (h + 1) * CLUSTERS):
            at = place(row, valid, size) - start
            if runs and runs[-1][1] == at:
                runs[-1][1] = at + 1
            else:
                runs.append([at, at + 1])
        found.append((start, runs))
    return found


def to_notes(column):
    rows = column.shape[0]
    sheet = lax.broadcasted_iota(jnp.int32, (rows, PAIR), 0) == lanes_of(rows)
    found = []
    for p in range(2):
        lane = jnp.sum(jnp.where(sheet, column[:, p * HEAD_DIM : p * HEAD_DIM + 1], 0.0), axis=0, keepdims=True)
        found += list(split2(lane))
    return found


def from_notes(notes, rows):
    sheet = lax.broadcasted_iota(jnp.int32, (rows, PAIR), 0) == lanes_of(rows)
    found = []
    for p in range(2):
        lane = notes[2 * p : 2 * p + 1] + notes[2 * p + 1 : 2 * p + 2]
        found.append(jnp.sum(jnp.where(sheet, lane, 0.0), axis=-1, keepdims=True))
    return found


def with_notes(values, notes, valid):
    row = lax.broadcasted_iota(jnp.int32, values.shape, 0)
    for k, note in enumerate(notes):
        values = jnp.where(row == valid + k, note, values)
    return values


def notes_of(values, valid):
    row = lax.broadcasted_iota(jnp.int32, values.shape, 0)
    return jnp.concatenate(
        [jnp.sum(jnp.where(row == valid + k, values, 0.0), axis=0, keepdims=True) for k in range(NOTES)], axis=0
    )


def onehot_rows(places, start):
    rows = places.shape[0]
    return (lanes_of(rows, SLOTS) == places - start).astype(F32).astype(LOW)


def onehot_columns(places, start):
    columns = places.shape[1]
    return (lax.broadcasted_iota(jnp.int32, (SLOTS, columns), 0) == places - start).astype(F32).astype(LOW)


def side(tile, p):
    lane = lanes_of(tile.shape[0])
    return jnp.where((lane < HEAD_DIM) if p == 0 else (lane >= HEAD_DIM), tile, jnp.zeros_like(tile))


def head_side(values, h, p):
    tile = values[:, h // 2 * PAIR : (h // 2 + 1) * PAIR]
    if tile.shape[1] < PAIR:
        tile = jnp.concatenate([tile, jnp.zeros_like(tile)], axis=1)
    if h % 2 != p:
        tile = pltpu.roll(tile, HEAD_DIM, 1)
    return side(tile, p)


def valid_rows(window):
    row = lax.broadcasted_iota(jnp.int32, (SLOTS, 1), 0)
    kept = row < 0
    for first, end in window[1]:
        kept |= (row >= first) & (row < end)
    return kept


def call(body, grid, out_shape, in_specs, out_specs, scratch=()):
    return pl.pallas_call(
        body,
        grid=grid,
        out_shape=out_shape,
        in_specs=in_specs,
        out_specs=out_specs,
        scratch_shapes=list(scratch),
        compiler_params=pltpu.CompilerParams(
            vmem_limit_bytes=60 * MIB, dimension_semantics=("arbitrary",) * len(grid)
        ),
        cost_estimate=pl.CostEstimate(flops=1, bytes_accessed=1, transcendentals=0),
    )


def shape(dims, kind=LOW):
    return jax.ShapeDtypeStruct(tuple(dims), kind)


def step_spec(dims):
    rest = tuple(dims[1:])
    return pl.BlockSpec((1, *rest), lambda b: (b,) + (0,) * len(rest))


def table_spec(dims, groups):
    rest = tuple(dims[1:])
    return pl.BlockSpec((dims[0] // groups, *rest), lambda b: (b,) + (0,) * len(rest))


def full_spec(dims):
    return pl.BlockSpec(tuple(dims), lambda b: (0,) * len(dims))


def first_kernel(cuts, valid, *refs):
    me, own, near, far, diagonal, places, *rest = refs
    query, key, value, vectors, first_out, kv_out, sums_out, sheet = rest
    gain, shift = vectors[0:1], vectors[1:2]
    query_bias, value_bias = vectors[5:6, : query.shape[0]], vectors[6:7, : query.shape[0]]
    rows = own.shape[2]
    heads = len(cuts)
    wide = heads * PAIR
    sheet[...] = jnp.zeros_like(sheet)
    for p in range(2):
        tokens = jnp.concatenate([r[0, p] for r in (own, near, far, diagonal)], axis=0).astype(F32)
        unit, _ = standard(tokens)
        first = (unit * gain + shift).astype(LOW)
        first_out[0, p] = first
        queries = (dot(first, query[...], 1, 1) + query_bias).astype(LOW).astype(F32)
        keys = dot(first, key[...], 1, 1)
        values = dot(first, value[...], 1, 1) + value_bias
        one = side(jnp.ones((first.shape[0], PAIR), F32), p)
        for h, (start, _) in enumerate(cuts):
            kv_out[0, p, :, h * PAIR : (h + 1) * PAIR] = head_side(keys, h, p).astype(LOW)
            kv_out[0, p, :, wide + h * PAIR : wide + (h + 1) * PAIR] = head_side(values, h, p).astype(LOW)
            both = jnp.concatenate([head_side(queries, h, p), one], axis=1).astype(LOW)
            part = None
            for k in range(4):
                member = onehot_columns(places[0, p, me[0] ^ k, h : h + 1, :], start)
                term = dot(member, both[k * rows : (k + 1) * rows])
                part = term if part is None else part + term
            sheet[start : start + SLOTS] += part
    size = sums_out.shape[1]
    for d in range(sums_out.shape[0]):
        chunk = sheet[d * size : (d + 1) * size]
        notes = to_notes(chunk[:, PAIR:])
        sums_out[d] = with_notes(chunk[:, :PAIR], notes, valid).astype(LOW)


def scores_of(centroid, keys):
    return dot(centroid, keys, 1, 1) * 0.125


def attend_kernel(cuts, valid, centroid, kv, packed, sheet):
    wide = len(cuts) * PAIR
    count, size = packed.shape[0], packed.shape[1]
    table = centroid[...].reshape(count * size, PAIR)
    lane = lanes_of(SLOTS)
    sheet[...] = jnp.zeros_like(sheet)
    for h, window in enumerate(cuts):
        start = window[0]
        mine = table[start : start + SLOTS]
        out = jnp.zeros((SLOTS, PAIR), F32)
        log = jnp.zeros((SLOTS, PAIR), F32)
        for p in range(2):
            keys = kv[0, p, :, h * PAIR : (h + 1) * PAIR]
            values = kv[0, p, :, wide + h * PAIR : wide + (h + 1) * PAIR]
            scores = scores_of(mine, keys)
            top = jnp.max(scores, axis=-1, keepdims=True)
            exponent = jnp.exp(scores - top)
            total = jnp.sum(exponent, axis=-1, keepdims=True)
            out += dot(exponent.astype(LOW), values) / total
            log = jnp.where((lane < HEAD_DIM) if p == 0 else (lane >= HEAD_DIM), top + jnp.log(total), log)
        both = jnp.concatenate([out, log], axis=1)
        sheet[start : start + SLOTS] += jnp.where(valid_rows(window), both, 0.0)
    for d in range(count):
        chunk = sheet[d * size : (d + 1) * size]
        packed[d] = with_notes(chunk[:, :PAIR], to_notes(chunk[:, PAIR:]), valid).astype(LOW)


def half_wise(first, second, rows):
    return jnp.where(lanes_of(rows) < HEAD_DIM, first, second)


def merge_kernel(valid, packed, copies, out_shard):
    count, rows = packed.shape[0], packed.shape[1]
    logs, parts = [], []
    for i in range(count):
        part = packed[i].astype(F32)
        logs.append(half_wise(*from_notes(notes_of(part, valid), rows), rows))
        parts.append(part)
    top = logs[0]
    for log in logs[1:]:
        top = jnp.maximum(top, log)
    total = jnp.zeros((rows, PAIR), F32)
    out = jnp.zeros((rows, PAIR), F32)
    for i in range(count):
        weight = jnp.exp(logs[i] - top)
        total += weight
        out += weight * parts[i]
    out = out / total
    out_shard[...] = out
    low = with_notes(out, to_notes(top + jnp.log(total)), valid).astype(LOW)
    for k in range(copies.shape[0]):
        copies[k] = low


def join_heads(picked, p):
    rows = picked[0].shape[0]
    lane = lanes_of(rows)
    tiles = []
    for g in range(0, len(picked), 2):
        even = picked[g]
        odd = picked[g + 1] if g + 1 < len(picked) else even
        if p == 0:
            tile = jnp.where(lane < HEAD_DIM, even, pltpu.roll(odd, HEAD_DIM, 1))
        else:
            tile = jnp.where(lane < HEAD_DIM, pltpu.roll(even, HEAD_DIM, 1), odd)
        tiles.append(tile)
    joined = jnp.concatenate(tiles, axis=1)
    return joined[:, : len(picked) * HEAD_DIM]


def gelu_parts(values):
    area = 0.5 * (1.0 + lax.erf(values * 0.7071067811865476))
    density = jnp.exp(-0.5 * values * values) * 0.3989422804014327
    return values * area, area + values * density


def lay_out(table, whole):
    size = table.shape[2]
    for m in range(table.shape[1]):
        for d in range(table.shape[0]):
            whole[m, d * size : (d + 1) * size] = table[d, m]


def dense_kernel(cuts, which, *refs):
    (
        me,
        table,
        places,
        tokens_a,
        tokens_b,
        cot_a,
        cot_b,
        output_weight,
        expand_weight,
        shrink_weight,
        vectors,
        second_a,
        second_b,
        ffn_a,
        ffn_b,
        hidden_out,
        mine_out,
        normed_out,
        activated_out,
        expand_out,
        bias_out,
        attended,
        whole,
    ) = refs
    rows = tokens_a.shape[2]
    groups = table.shape[1]
    lay_out(table, whole)
    for p in range(2):
        picked = []
        for m in range(groups):
            column = jnp.concatenate([places[m, 0, p, me[0] ^ (2 * which + j)].T for j in range(2)], axis=0)
            for h, (start, _) in enumerate(cuts):
                member = onehot_rows(column[:, h : h + 1], start)
                picked.append(dot(member, whole[me[0] ^ m, start : start + SLOTS]))
        attended[p * 2 * rows : (p + 1) * 2 * rows] = join_heads(picked, p).astype(LOW)
        mine_out[0, p * 2 * rows : (p + 1) * 2 * rows] = join_heads(picked[: len(cuts)], p).astype(LOW)
    tokens = jnp.concatenate([tokens_a[0, 0], tokens_b[0, 0], tokens_a[0, 1], tokens_b[0, 1]], axis=0)
    cotangent = jnp.concatenate([cot_a[0, 0], cot_b[0, 0], cot_a[0, 1], cot_b[0, 1]], axis=0)
    hidden = tokens.astype(F32) + dot(attended[...], output_weight[...]) + vectors[4:5]
    unit, _ = standard(hidden)
    normed = (unit * vectors[2:3] + vectors[3:4]).astype(LOW)
    expanded = dot(normed, expand_weight[...]) + jnp.concatenate([vectors[k : k + 1] for k in range(7, vectors.shape[0])], axis=1)
    active, slope = gelu_parts(expanded)
    active = active.astype(LOW)
    back = (dot(cotangent, shrink_weight[...], 1, 1) * slope).astype(LOW)
    second = dot(back, expand_weight[...], 1, 1)
    ffn = dot(active, shrink_weight[...])
    for j, (second_ref, ffn_ref) in enumerate(((second_a, ffn_a), (second_b, ffn_b))):
        for p in range(2):
            at = (2 * p + j) * rows
            second_ref[0, p] = second[at : at + rows].astype(second_ref.dtype)
            ffn_ref[0, p] = ffn[at : at + rows].astype(ffn_ref.dtype)
    for p in range(2):
        hidden_out[0, p] = hidden[2 * p * rows : (2 * p + 1) * rows]
    normed_out[0] = normed
    activated_out[0] = active
    expand_out[0] = back

    @pl.when(pl.program_id(0) == 0)
    def _():
        bias_out[...] = jnp.zeros_like(bias_out)

    bias_out[...] += jnp.sum(back.astype(F32), axis=0, keepdims=True)


def grads_kernel(terms, steps, *refs):
    refs = list(refs)
    products = []
    for pieces in terms:
        lefts = [refs.pop(0) for _ in range(2)]
        rights = [refs.pop(0) for _ in range(4 if pieces else 2)]
        if pieces:
            near, far = rights[:2], rights[2:]
            right = [r[0, p] for pair in (near, far) for p in range(2) for r in pair]
        else:
            right = [r[0] for r in rights]
        products.append(
            dot(jnp.concatenate([v[0] for v in lefts], axis=0), jnp.concatenate(right, axis=0), 0, 0)
        )
    outs, totals = refs[: len(terms)], refs[len(terms) :]
    for k, product in enumerate(products):
        if steps > 1:
            total = totals[k]
            total[...] = jnp.where(pl.program_id(0) == 0, product, total[...] + product)
            product = total[...]
        outs[k][...] = product.astype(LOW)


def hidden_kernel(cuts, *refs):
    (
        me,
        own,
        near,
        across,
        hidden,
        cot,
        places,
        output_weight,
        vectors,
        grad_out,
        low_out,
        table_out,
        small_out,
        whole,
    ) = refs
    groups, heads = table_out.shape[1], len(cuts)
    small = [jnp.zeros((1, own.shape[3]), F32) for _ in range(4)]
    parts = []
    for p in range(2):
        grad = own[0, p] + near[0, p].astype(F32) + across[0, p].astype(F32)
        unit, scale = standard(hidden[0, p])
        dy = cot[0, p].astype(F32)
        total = dy + norm_back(grad, unit, scale, vectors[2:3])
        grad_out[0, p] = total
        low = total.astype(LOW)
        low_out[0, p] = low
        for k, row in enumerate((total, dy, grad * unit, grad)):
            small[k] += jnp.sum(row, axis=0, keepdims=True)
        parts.append(dot(low, output_weight[...], 1, 1))
    whole[...] = jnp.zeros_like(whole)
    for k in range(groups * heads):
        m, h = k // heads, k % heads
        start = cuts[h][0]
        found = None
        for p in range(2):
            member = onehot_columns(places[m, 0, p, me[0], h : h + 1, :], start)
            term = dot(member, head_side(parts[p], k, p).astype(LOW))
            found = term if p == 0 else found + term
        whole[m, start : start + SLOTS] += found
    size = table_out.shape[2]
    for m in range(groups):
        for d in range(table_out.shape[0]):
            table_out[d, me[0] ^ m] = whole[m, d * size : (d + 1) * size].astype(LOW)

    @pl.when(pl.program_id(0) == 0)
    def _():
        small_out[...] = jnp.zeros_like(small_out)

    for k in range(4):
        small_out[k : k + 1, :] += small[k]


def out_grad_kernel(valid, parts, out_shard, copies):
    count, rows = parts.shape[0], parts.shape[1]
    total = jnp.zeros((rows, PAIR), F32)
    for i in range(count):
        total += parts[i].astype(F32)
    total = total.astype(LOW).astype(F32)
    product = total * out_shard[...]
    deltas = [jnp.sum(side(product, p), axis=-1, keepdims=True) for p in range(2)]
    low = with_notes(total, to_notes(half_wise(*deltas, rows)), valid).astype(LOW)
    for k in range(copies.shape[0]):
        copies[k] = low


def back_kernel(cuts, valid, me, centroid, kv, grads, out_table, part_out, prob_out, score_out, sheet, columns):
    wide = len(cuts) * PAIR
    count, size = part_out.shape[0], part_out.shape[1]
    table = centroid[...].reshape(count * size, PAIR)
    grad_table = grads[...].reshape(count * size, PAIR)
    for d in range(count):
        delta = from_notes(notes_of(grads[d].astype(F32), valid), size)
        log = from_notes(notes_of(out_table[d, me[0]].astype(F32), valid), size)
        for k, column in enumerate((*delta, *log)):
            columns[d * size : (d + 1) * size, k * PAIR : (k + 1) * PAIR] = jnp.broadcast_to(column, (size, PAIR))
    sheet[...] = jnp.zeros_like(sheet)
    for h, window in enumerate(cuts):
        start = window[0]
        mine, out_grad = table[start : start + SLOTS], grad_table[start : start + SLOTS]
        kept = valid_rows(window)
        part = None
        for p in range(2):
            keys = kv[0, p, :, h * PAIR : (h + 1) * PAIR]
            values = kv[0, p, :, wide + h * PAIR : wide + (h + 1) * PAIR]
            delta = columns[start : start + SLOTS, p * PAIR : p * PAIR + 1]
            log = columns[start : start + SLOTS, (2 + p) * PAIR : (2 + p) * PAIR + 1]
            probs = jnp.where(kept, jnp.exp(scores_of(mine, keys) - log), 0.0)
            grad = (probs * (dot(out_grad, values, 1, 1) - delta) * 0.125).astype(LOW)
            term = dot(grad, keys)
            part = term if p == 0 else part + term
            prob_out[0, p, h] = probs.astype(LOW)
            score_out[0, p, h] = grad
        sheet[start : start + SLOTS] += part
    for d in range(count):
        part_out[d] = sheet[d * size : (d + 1) * size].astype(LOW)


def kv_kernel(cuts, *refs):
    centroid, out_grads, probs, grads, key_weight, value_weight, key_out, value_out, own, near, far, diagonal = refs
    share = own.shape[2]
    count, size = centroid.shape[0], centroid.shape[1]
    table = centroid[...].reshape(count * size, PAIR)
    grad_table = out_grads[...].reshape(count * size, PAIR)
    for p in range(2):
        key_parts, value_parts = [], []
        for h, (start, _) in enumerate(cuts):
            key_parts.append(dot(grads[0, p, h], table[start : start + SLOTS], 0, 0))
            value_parts.append(dot(probs[0, p, h], grad_table[start : start + SLOTS], 0, 0))
        keys = join_heads(key_parts, p).astype(LOW)
        values = join_heads(value_parts, p).astype(LOW)
        key_out[0, p] = keys
        value_out[0, p] = values
        first = dot(keys, key_weight[...]) + dot(values, value_weight[...])
        for k, ref in enumerate((own, near, far, diagonal)):
            ref[0, p] = first[k * share : (k + 1) * share].astype(ref.dtype)


def centroid_kernel(valid, parts, copies, inverse):
    count, rows = parts.shape[0], parts.shape[1]
    total = parts[0].astype(F32)
    for i in range(1, count):
        total += parts[i].astype(F32)
    counts = half_wise(*from_notes(notes_of(total, valid), rows), rows)
    share = 1.0 / jnp.maximum(counts, 1.0)
    inverse[...] = share
    row = lax.broadcasted_iota(jnp.int32, (rows, PAIR), 0)
    low = jnp.where(row < valid, total * share, 0.0).astype(LOW)
    for k in range(copies.shape[0]):
        copies[k] = low


def mean_kernel(parts, inverse, copies):
    total = parts[0].astype(F32)
    for i in range(1, parts.shape[0]):
        total += parts[i].astype(F32)
    low = (total * inverse[...]).astype(LOW)
    for k in range(copies.shape[0]):
        copies[k] = low


def query_kernel(cuts, steps, *refs):
    me, table, places, first, grad_out, bias_out, *total = refs
    count, size = table.shape[0], table.shape[1]
    whole = table[...].reshape(count * size, PAIR)
    product, bias = None, None
    for p in range(2):
        column = jnp.concatenate([places[0, p, me[0] ^ k].T for k in range(places.shape[2])], axis=0)
        picked = []
        for h, (start, _) in enumerate(cuts):
            member = onehot_rows(column[:, h : h + 1], start)
            picked.append(dot(member, whole[start : start + SLOTS]))
        query = join_heads(picked, p)
        term = dot(query.astype(LOW), first[0, p], 0, 0)
        row = jnp.sum(query, axis=0, keepdims=True)
        product = term if p == 0 else product + term
        bias = row if p == 0 else bias + row
    if steps > 1:
        opening = pl.program_id(0) == 0
        total[0][...] = jnp.where(opening, product, total[0][...] + product)
        total[1][...] = jnp.where(opening, bias, total[1][...] + bias)
        product, bias = total[0][...], total[1][...]
    grad_out[...] = product.astype(LOW)
    bias_out[...] = bias


def last_kernel(cuts, *refs):
    (
        me,
        table_own,
        table_near,
        table_far,
        table_diagonal,
        places,
        own,
        near,
        across,
        tokens,
        hidden_grad,
        weight,
        vectors,
        token_out,
        small_out,
    ) = refs
    tables = [t[...].reshape(-1, PAIR) for t in (table_own, table_near, table_far, table_diagonal)]
    small = [jnp.zeros((1, own.shape[3]), F32) for _ in range(2)]
    for p in range(2):
        picked = []
        for m, whole in enumerate(tables):
            column = places[m, 0, p, me[0]].T
            for h, (start, _) in enumerate(cuts):
                member = onehot_rows(column[:, h : h + 1], start)
                picked.append(dot(member, whole[start : start + SLOTS]))
        query = join_heads(picked, p).astype(LOW)
        grad = own[0, p] + near[0, p].astype(F32) + across[0, p].astype(F32)
        grad += dot(query, weight[...])
        unit, scale = standard(tokens[0, p].astype(F32))
        token_out[0, p] = hidden_grad[0, p] + norm_back(grad, unit, scale, vectors[0:1])
        for k, row in enumerate((grad * unit, grad)):
            small[k] += jnp.sum(row, axis=0, keepdims=True)

    @pl.when(pl.program_id(0) == 0)
    def _():
        small_out[...] = jnp.zeros_like(small_out)

    for k in range(2):
        small_out[k : k + 1, :] += small[k]


def split3(values):
    high = values.astype(LOW).astype(F32)
    middle = (values - high).astype(LOW).astype(F32)
    return high, middle, values - high - middle


def summed(parts):
    total = parts[0].astype(F32)
    for i in range(1, parts.shape[0]):
        total += parts[i].astype(F32)
    return total


def shard_kernel(parts, copies):
    total = summed(parts)
    rows = total.shape[0] - 3
    sums = total[rows : rows + 1] + total[rows + 1 : rows + 2] + total[rows + 2 :]
    low = jnp.concatenate([total[:rows], *split3(sums)], axis=0).astype(LOW)
    for k in range(copies.shape[0]):
        copies[k] = low


def finish_kernel(each, found, query, late, *outs):
    count, width = found.shape[0], found.shape[2]
    parts = [found[d].astype(F32) for d in range(count)]
    for k in range(3):
        outs[k][...] = jnp.concatenate([v[k * each : (k + 1) * each] for v in parts], axis=0)
    outs[3][...] = query[...].astype(F32)
    at = 3 * each
    sums = [v[at : at + 1] + v[at + 1 : at + 2] + v[at + 2 : at + 3] for v in parts]
    part = width // count

    def row(k):
        return jnp.concatenate([v[:, k * part : (k + 1) * part] for v in sums], axis=1)

    query_bias, value_bias, expand_bias = outs[10:]
    for k in range(4):
        outs[4 + k][...] = row(k)[0]
    value_bias[...] = row(4)[0, : value_bias.shape[0]]
    expand_bias[...] = row(5)[0]
    for k in range(2):
        outs[8 + k][...] = late[k]
    query_bias[...] = late[2, : query_bias.shape[0]]


def partner(value, step):
    size = lax.axis_size("mp")
    return lax.ppermute(value, "mp", [(i, i ^ step) for i in range(size)])


def gather_rows(value):
    far = partner(value, 2)
    near = partner(value, 1)
    return value, near, far, partner(far, 1)


def scatter_rows(near, far, diagonal):
    near_in, diagonal_in = partner(near, 1), partner(diagonal, 1)
    across = (far.astype(F32) + diagonal_in.astype(F32)).astype(LOW)
    return near_in, partner(across, 2)


def exchange(copies, axes):
    return lax.all_to_all(copies, axes, 0, 0)


def after(value, *others):
    return lax.optimization_barrier((value, others))[0]


def together(*values):
    return lax.optimization_barrier(values)


def shards(
    tokens,
    cluster_ids,
    query_weight,
    query_bias,
    key_weight,
    value_weight,
    value_bias,
    output_weight,
    output_bias,
    expand_weight,
    expand_bias,
    shrink_weight,
    shrink_bias,
    first_gain,
    first_shift,
    second_gain,
    second_shift,
    cotangent,
):
    seqs, share, width = tokens.shape
    heads = cluster_ids.shape[2]
    hidden_units = expand_weight.shape[1]
    n_dp, n_mp = lax.axis_size("dp"), lax.axis_size("mp")
    both = ("dp", "mp")
    n_all = n_dp * n_mp
    all_heads = heads * n_mp
    half = seqs // 2
    local = share * n_mp
    head_width = heads * HEAD_DIM
    wide = heads * PAIR
    valid = half * heads * CLUSTERS // n_dp
    size = -(-(valid + NOTES) // 16) * 16
    per_pair = n_dp // half
    cuts = windows(heads, valid, size)
    table_rows = per_pair * size
    me = lax.axis_index("mp")
    me_ref = me.astype(jnp.int32).reshape(1)

    def sequences(value):
        return value.reshape(half, 2, *value.shape[1:])

    token_pairs = sequences(tokens)
    token_far, token_near = partner(token_pairs, 2), partner(token_pairs, 1)
    places = place(cluster_ids + jnp.arange(heads, dtype=jnp.int32) * CLUSTERS, valid, size)
    places_row = places.reshape(half, 2, n_mp, share, heads).transpose(0, 1, 2, 4, 3)
    places_row = jnp.pad(places_row, ((0, 0),) * 3 + ((0, 8 - heads), (0, 0)))
    vectors = jnp.stack(
        [
            jnp.pad(v.astype(F32), (0, width - v.shape[0]))
            for v in (first_gain, first_shift, second_gain, second_shift, output_bias, query_bias, value_bias)
        ]
        + [expand_bias.astype(F32).reshape(-1, width)[k] for k in range(hidden_units // width)]
    )
    token_far, places_row, vectors = together(token_far, places_row, vectors)
    pieces = token_pairs, token_near, token_far, partner(token_far, 1)
    places_all = gather_rows(places_row)
    output_whole = jnp.concatenate(gather_rows(output_weight), axis=0)
    query_turned, key_turned, value_turned = query_weight.T, key_weight.T, value_weight.T
    query_pieces = gather_rows(query_turned)

    piece_dims = (half, 2, share, width)
    piece_spec = step_spec(piece_dims)
    square_spec = full_spec((width, width))
    head_spec = full_spec((head_width, width))
    me_spec = pl.BlockSpec(memory_space=pltpu.SMEM)
    kv_dims = (half, 2, local, 2 * wide)
    table_dims = (n_dp, size, PAIR)
    shard_dims = (size, PAIR)
    copies_dims = (n_all, *shard_dims)
    all_dims = (n_dp, n_mp, *shard_dims)
    sheet = pltpu.VMEM((table_rows, 2 * PAIR), F32)
    group_scratch = pltpu.VMEM((n_mp, table_rows, PAIR), LOW)
    places_spec = pl.BlockSpec((n_mp, 1, 2, n_mp, 8, share), lambda b: (0, b, 0, 0, 0, 0))
    vectors_spec = full_spec(vectors.shape)

    first, kv, sums = call(
        partial(first_kernel, cuts, valid),
        (half,),
        (shape((half, 2, local, width)), shape(kv_dims), shape(table_dims)),
        [me_spec]
        + [piece_spec] * 4
        + [step_spec((half, 2, n_mp, 8, share))]
        + [head_spec] * 3
        + [vectors_spec],
        (step_spec((half, 2, local, width)), step_spec(kv_dims), table_spec(table_dims, half)),
        [sheet],
    )(
        me_ref,
        *pieces,
        places_row,
        query_turned,
        key_turned,
        value_turned,
        vectors,
    )
    cotangent_pairs = sequences(cotangent)
    cot_start = after(cotangent_pairs, sums)
    cot_far, cot_near = partner(cot_start, 2), partner(cot_start, 1)

    sums = exchange(sums, "dp")
    sums, cot_far, cot_near = together(sums, cot_far, cot_near)
    cot_diagonal = partner(cot_far, 1)
    copies, inverse = call(
        partial(centroid_kernel, valid),
        (1,),
        (shape(table_dims), shape(shard_dims, F32)),
        [full_spec(table_dims)],
        (full_spec(table_dims), full_spec(shard_dims)),
    )(sums)
    centroid = exchange(copies, "dp")
    centroid, cot_diagonal = together(centroid, cot_diagonal)

    packed = call(
        partial(attend_kernel, cuts, valid),
        (half,),
        shape(table_dims),
        [table_spec(table_dims, half), step_spec(kv_dims)],
        table_spec(table_dims, half),
        [sheet],
    )(centroid, kv)
    packed = exchange(packed, "dp")
    packed, output_whole, *places_all = together(packed, output_whole, *places_all)
    places_all = jnp.stack(places_all)
    copies, out_shard = call(
        partial(merge_kernel, valid),
        (1,),
        (shape(copies_dims), shape(shard_dims, F32)),
        [full_spec(table_dims)],
        (full_spec(copies_dims), full_spec(shard_dims)),
    )(packed)
    out_table = exchange(copies, both).reshape(all_dims)
    out_table, *query_pieces = together(out_table, *query_pieces)
    query_whole = jnp.concatenate(query_pieces, axis=0)

    dense_rows = 4 * share

    def dense(which, kinds, tokens_a, tokens_b, cot_a, cot_b):
        dims = (half, dense_rows)
        return call(
            partial(dense_kernel, cuts, which),
            (half,),
            (
                shape(piece_dims, kinds[0]),
                shape(piece_dims, kinds[1]),
                shape(piece_dims, kinds[0]),
                shape(piece_dims, kinds[1]),
                shape(piece_dims, F32),
                shape((*dims, head_width)),
                shape((*dims, width)),
                shape((*dims, hidden_units)),
                shape((*dims, hidden_units)),
                shape((1, hidden_units), F32),
            ),
            [me_spec, table_spec(all_dims, half), places_spec]
            + [piece_spec] * 4
            + [square_spec, full_spec((width, hidden_units)), full_spec((hidden_units, width)), vectors_spec],
            (
                *[piece_spec] * 5,
                step_spec((*dims, head_width)),
                step_spec((*dims, width)),
                step_spec((*dims, hidden_units)),
                step_spec((*dims, hidden_units)),
                full_spec((1, hidden_units)),
            ),
            [pltpu.VMEM((dense_rows, width), LOW), group_scratch],
        )(
            me_ref,
            out_table,
            places_all,
            tokens_a,
            tokens_b,
            cot_a,
            cot_b,
            output_whole,
            expand_weight,
            shrink_weight,
            vectors,
        )

    beyond = dense(1, (F32, LOW), pieces[2], pieces[3], cot_far, cot_diagonal)
    diagonal_in = partner(beyond[1], 1)
    inside = dense(0, (F32, LOW), after(pieces[0], *beyond), pieces[1], cotangent_pairs, cot_near)
    across_in = partner((beyond[0] + diagonal_in.astype(F32)).astype(LOW), 2)
    near_in = partner(inside[1], 1)
    hidden_own = inside[4]

    def grads(terms, dims, operands):
        return call(
            partial(grads_kernel, terms, half),
            (half,),
            tuple(shape(dims) for _ in terms),
            [step_spec(value.shape) for value in operands],
            tuple(full_spec(dims) for _ in terms),
            [] if half == 1 else [pltpu.VMEM(dims, F32)] * len(terms),
        )(*operands)

    ffn_grads = grads(
        (True, False),
        (hidden_units, width),
        (beyond[7], inside[7], cot_far, cot_diagonal, cotangent_pairs, cot_near)
        + (beyond[6], inside[6], beyond[8], inside[8]),
    )
    my_dp = lax.axis_index("dp")
    steps = n_dp.bit_length() - 1

    def opposite(value, step):
        return lax.ppermute(value, "dp", [(i, i ^ (1 << step)) for i in range(n_dp)])

    def halved(value, step):
        count = value.shape[0] // 2
        upper = (my_dp >> step) % 2 == 1
        return jnp.where(upper, value[count:], value[:count]), jnp.where(upper, value[:count], value[count:])

    def added(kept, arrived):
        return (kept.astype(F32) + arrived.astype(F32)).astype(LOW)

    def joined(value, arrived, step):
        upper = (my_dp >> step) % 2 == 1
        return jnp.where(
            upper, jnp.concatenate([arrived, value], axis=0), jnp.concatenate([value, arrived], axis=0)
        )

    orders = [list(range(steps)), [1, 0, *range(2, steps)]]

    def ffn_step(kept, arrived, index):
        if arrived is not None:
            kept = [added(k, v) for k, v in zip(kept, arrived)]
        cut_in_two = [halved(v, order[index]) for v, order in zip(kept, orders)]
        return [v[0] for v in cut_in_two], [opposite(v[1], order[index]) for v, order in zip(cut_in_two, orders)]

    def ffn_join(kept, arrived, index):
        return [joined(v, w, order[index]) for v, w, order in zip(kept, arrived, orders)]

    def ffn_send(kept, index):
        return [opposite(v, order[index]) for v, order in zip(kept, orders)]

    ffn_now, ffn_in = ffn_step(ffn_grads, None, 0)
    expand_bias_grad = beyond[9] + inside[9]
    near_in, across_in, *ffn_now = together(near_in, across_in, *ffn_now)

    hidden_grad, hidden_low, out_part, small_two = call(
        partial(hidden_kernel, cuts),
        (half,),
        (shape(piece_dims, F32), shape(piece_dims), shape(all_dims), shape((8, width), F32)),
        [me_spec] + [piece_spec] * 5 + [places_spec, square_spec, vectors_spec],
        (piece_spec, piece_spec, table_spec(all_dims, half), full_spec((8, width))),
        [pltpu.VMEM((n_mp, table_rows, PAIR), F32)],
    )(
        me_ref,
        inside[0],
        near_in,
        across_in,
        hidden_own,
        cotangent_pairs,
        places_all,
        output_whole,
        vectors,
    )
    out_part, *ffn_in = together(out_part, *ffn_in)
    ffn_now, ffn_in = ffn_step(ffn_now, ffn_in, 1)
    out_part = exchange(out_part.reshape(copies_dims), both)
    out_part, query_whole, *ffn_in = together(out_part, query_whole, *ffn_in)
    for index in range(2, steps):
        ffn_now, ffn_in = ffn_step(ffn_now, ffn_in, index)
    out_grad = call(
        partial(out_grad_kernel, valid),
        (1,),
        shape(table_dims),
        [full_spec(copies_dims), full_spec(shard_dims)],
        full_spec(table_dims),
    )(out_part, out_shard)
    out_grad = exchange(out_grad, "dp")
    low_start = after(hidden_low, out_grad)
    low_near, low_far = partner(low_start, 1), partner(low_start, 2)
    early_small = small_two[:4]
    for step in range(n_mp.bit_length() - 1):
        early_small += partner(early_small, 1 << step)

    score_dims = (half, 2, heads, SLOTS, local)
    centroid_part, probs, score_grad = call(
        partial(back_kernel, cuts, valid),
        (half,),
        (shape(table_dims), shape(score_dims), shape(score_dims)),
        [me_spec, table_spec(table_dims, half), step_spec(kv_dims)]
        + [table_spec(table_dims, half), table_spec(all_dims, half)],
        (table_spec(table_dims, half), step_spec(score_dims), step_spec(score_dims)),
        [pltpu.VMEM((table_rows, PAIR), F32), pltpu.VMEM((table_rows, 4 * PAIR), F32)],
    )(me_ref, centroid, kv, out_grad, out_table)
    centroid_part, *ffn_in = together(centroid_part, *ffn_in)
    ffn_now = [added(k, v) for k, v in zip(ffn_now, ffn_in)]
    ffn_in = ffn_send(ffn_now, steps - 1)
    low_diagonal = partner(after(low_far, centroid_part), 1)
    centroid_part = exchange(centroid_part, "dp")

    grad_dims = (half, 2, local, head_width)
    key_grad, value_grad, first_own, *first_parts = call(
        partial(kv_kernel, cuts),
        (half,),
        (shape(grad_dims), shape(grad_dims), *[shape(piece_dims, kind) for kind in (F32, LOW, F32, LOW)]),
        [table_spec(table_dims, half)] * 2
        + [step_spec(score_dims), step_spec(score_dims)]
        + [head_spec] * 2,
        (step_spec(grad_dims), step_spec(grad_dims), *[piece_spec] * 4),
    )(centroid, out_grad, probs, score_grad, key_turned, value_turned)

    count_rows = seqs * local
    first_flat = first.reshape(count_rows, width)
    value_flat = value_grad.reshape(count_rows, head_width)
    key_weight_grad = dot(key_grad.reshape(count_rows, head_width), first_flat, 0, 0).astype(LOW)
    value_weight_grad = dot(value_flat, first_flat, 0, 0).astype(LOW)
    value_bias_grad = jnp.sum(value_flat.astype(F32), axis=0)
    early_small = jnp.concatenate(
        [early_small, jnp.pad(value_bias_grad, (0, width - head_width))[None], expand_bias_grad], axis=0
    )
    centroid_part, low_near, low_far, low_diagonal, first_own, *rest = together(
        centroid_part, low_near, low_far, low_diagonal, first_own, *first_parts, *ffn_in
    )
    centroid_part, key_weight_grad, value_weight_grad, early_small = together(
        centroid_part, key_weight_grad, value_weight_grad, early_small
    )
    first_parts, ffn_in = rest[:3], rest[3:]
    for index in range(steps - 1, 1, -1):
        ffn_now = ffn_join(ffn_now, ffn_in, index)
        ffn_in = ffn_send(ffn_now, index - 1)
    (output_weight_grad,) = grads(
        (True,),
        (head_width, width),
        (beyond[5], inside[5], low_far, low_diagonal, hidden_low, low_near),
    )
    first_in = scatter_rows(*first_parts)
    query_copies = call(
        mean_kernel,
        (1,),
        shape(table_dims),
        [full_spec(table_dims), full_spec(shard_dims)],
        full_spec(table_dims),
    )(centroid_part, inverse)
    query_table = exchange(query_copies, "dp")
    def cut(value, count):
        rows, columns = value.shape[0] // count, value.shape[1]
        value = value.reshape(count, n_dp, rows // n_dp, columns).transpose(1, 0, 2, 3)
        return value.reshape(n_dp, count * rows // n_dp, columns)

    part = early_small.shape[0] * width // n_dp
    early_small = early_small.reshape(-1, n_dp, width // n_dp).transpose(1, 0, 2).reshape(n_dp, 1, part)
    early_small = jnp.pad(early_small, ((0, 0), (0, 0), (0, width - part)))
    high = lax.reduce_precision(early_small, 8, 7)
    middle = lax.reduce_precision(early_small - high, 8, 7)
    early_small = jnp.concatenate([high, middle, early_small - high - middle], axis=1).astype(LOW)
    early = cut(jnp.concatenate([key_weight_grad, value_weight_grad, output_weight_grad]), 3)
    early = jnp.concatenate([early, early_small], axis=1)
    query_table, early, *rest = together(query_table, early, *first_in, *ffn_in)
    first_in, ffn_in = rest[:2], rest[2:]
    ffn_now = ffn_join(ffn_now, ffn_in, 1)
    ffn_in = ffn_send(ffn_now, 0)
    early = exchange(early, "dp")
    query_tables = gather_rows(query_table)

    query_weight_grad, query_bias_grad = call(
        partial(query_kernel, cuts, half),
        (half,),
        (shape((head_width, width)), shape((1, head_width), F32)),
        [me_spec, table_spec(table_dims, half), step_spec((half, 2, n_mp, 8, share))]
        + [step_spec((half, 2, local, width))],
        (full_spec((head_width, width)), full_spec((1, head_width))),
        [] if half == 1 else [pltpu.VMEM((head_width, width), F32), pltpu.VMEM((1, head_width), F32)],
    )(me_ref, query_table, places_row, first)
    query_kept, query_sent = halved(query_weight_grad, 0)
    query_in = opposite(query_sent, 0)
    early, query_in = together(early, query_in)
    token_grad, small_one = call(
        partial(last_kernel, cuts),
        (half,),
        (shape(piece_dims, F32), shape((8, width), F32)),
        [me_spec]
        + [table_spec(table_dims, half)] * 4
        + [places_spec]
        + [piece_spec] * 5
        + [square_spec, vectors_spec],
        (piece_spec, full_spec((8, width))),
    )(
        me_ref,
        *query_tables,
        places_all,
        first_own,
        *first_in,
        pieces[0],
        hidden_grad,
        query_whole,
        vectors,
    )

    late = small_one[:2]
    for step in range(n_mp.bit_length() - 1):
        late += partner(late, 1 << step)
    late = jnp.concatenate([late, jnp.pad(query_bias_grad, ((0, 0), (0, width - head_width)))], axis=0)
    each = head_width // n_dp
    found = shape((n_dp, 3 * each + 3, width))
    found = call(shard_kernel, (1,), found, [full_spec(early.shape)], full_spec(found.shape))(early)
    ffn_near, ffn_across = scatter_rows(inside[3], beyond[2], after(beyond[3], found))
    found = exchange(found, "dp")

    for step in range(1, steps):
        query_sum = added(query_kept, query_in)
        query_kept, query_sent = halved(query_sum, step)
        query_in = opposite(query_sent, step)
    query_sum = added(query_kept, query_in)
    for step in range(steps - 1, -1, -1):
        if step == 0:
            found, query_sum, late, *ffn_in = together(found, query_sum, late, *ffn_in)
        count = query_sum.shape[0]
        high = lax.reduce_precision(late, 8, 7)
        message = jnp.concatenate([query_sum, high.astype(LOW), (late - high).astype(LOW)], axis=0)
        message = opposite(message, step)
        query_sum = joined(query_sum, message[:count], step)
        late += message[count : count + 3].astype(F32) + message[count + 3 :].astype(F32)
    shrink_weight_grad, expand_weight_grad = (v.astype(F32) for v in ffn_join(ffn_now, ffn_in, 0))
    result = (
        hidden_own
        + inside[2]
        + ffn_near.astype(F32)
        + ffn_across.astype(F32)
        + shrink_bias.astype(F32)
    ).astype(LOW)
    lengths = [width] * 6 + [head_width] * 2 + [hidden_units]
    key_weight_grad, value_weight_grad, output_weight_grad, query_weight_grad, *vectors = call(
        partial(finish_kernel, each),
        (1,),
        tuple(shape((head_width, width), F32) for _ in range(4)) + tuple(shape((n,), F32) for n in lengths),
        [full_spec(found.shape), full_spec((head_width, width)), full_spec((3, width))],
        tuple(full_spec((head_width, width)) for _ in range(4)) + tuple(full_spec((n,)) for n in lengths),
    )(found, query_sum, late)
    return (
        result.reshape(tokens.shape),
        token_grad.reshape(tokens.shape),
        query_weight_grad.T,
        vectors[6],
        key_weight_grad.T,
        value_weight_grad.T,
        vectors[7],
        output_weight_grad,
        vectors[0],
        expand_weight_grad,
        vectors[8],
        shrink_weight_grad,
        vectors[1],
        vectors[4],
        vectors[5],
        vectors[2],
        vectors[3],
    )


def solution(mesh):
    rows = P(None, ("dp", "mp"), None)
    columns, heads, vector, whole = P(None, "mp"), P("mp", None), P("mp"), P()
    return jax.shard_map(
        shards,
        mesh=mesh,
        in_specs=(
            rows,
            P(None, "dp", "mp"),
            columns,
            vector,
            columns,
            columns,
            vector,
            heads,
            whole,
            columns,
            vector,
            heads,
            whole,
            whole,
            whole,
            whole,
            whole,
            rows,
        ),
        out_specs=(
            rows,
            rows,
            columns,
            vector,
            columns,
            columns,
            vector,
            heads,
            whole,
            columns,
            vector,
            heads,
            whole,
            whole,
            whole,
            whole,
            whole,
        ),
        check_vma=False,
    )
```

```python
from functools import partial

import jax
import jax.numpy as jnp
from jax import lax
from jax.experimental import pallas as pl
from jax.experimental.pallas import tpu as pltpu
from jax.sharding import PartitionSpec as P

HEAD_DIM = 64
CLUSTERS = 200
SLOTS = 256
NOTES = 4
PAIR = 2 * HEAD_DIM
F32 = jnp.float32
LOW = jnp.bfloat16
MIB = 2**20


def dot(left, right, left_dim=1, right_dim=0):
    return lax.dot_general(
        left, right, (((left_dim,), (right_dim,)), ((), ())), preferred_element_type=F32
    )


def lanes_of(rows, width=PAIR):
    return lax.broadcasted_iota(jnp.int32, (rows, width), 1)


def standard(values):
    average = jnp.mean(values, axis=-1, keepdims=True)
    centered = values - average
    variance = jnp.mean(centered * centered, axis=-1, keepdims=True)
    scale = lax.rsqrt(variance + 1e-05)
    return centered * scale, scale


def norm_back(grad, unit, scale, gain):
    inner = grad * gain
    first = jnp.mean(inner, axis=-1, keepdims=True)
    second = jnp.mean(inner * unit, axis=-1, keepdims=True)
    return scale * (inner - first - unit * second)


def split2(values):
    high = values.astype(LOW).astype(F32)
    return high, (values - high).astype(LOW).astype(F32)


def place(row, valid, size):
    return row + (size - valid) * (row // valid)


def windows(heads, valid, size):
    end = place(heads * CLUSTERS - 1, valid, size) // size * size + size
    found = []
    for h in range(heads):
        start = min(place(h * CLUSTERS, valid, size) // 16 * 16, end - SLOTS)
        runs = []
        for row in range(h * CLUSTERS, (h + 1) * CLUSTERS):
            at = place(row, valid, size) - start
            if runs and runs[-1][1] == at:
                runs[-1][1] = at + 1
            else:
                runs.append([at, at + 1])
        found.append((start, runs))
    return found


def to_notes(column):
    rows = column.shape[0]
    sheet = lax.broadcasted_iota(jnp.int32, (rows, PAIR), 0) == lanes_of(rows)
    found = []
    for p in range(2):
        lane = jnp.sum(jnp.where(sheet, column[:, p * HEAD_DIM : p * HEAD_DIM + 1], 0.0), axis=0, keepdims=True)
        found += list(split2(lane))
    return found


def from_notes(notes, rows):
    sheet = lax.broadcasted_iota(jnp.int32, (rows, PAIR), 0) == lanes_of(rows)
    found = []
    for p in range(2):
        lane = notes[2 * p : 2 * p + 1] + notes[2 * p + 1 : 2 * p + 2]
        found.append(jnp.sum(jnp.where(sheet, lane, 0.0), axis=-1, keepdims=True))
    return found


def with_notes(values, notes, valid):
    row = lax.broadcasted_iota(jnp.int32, values.shape, 0)
    for k, note in enumerate(notes):
        values = jnp.where(row == valid + k, note, values)
    return values


def notes_of(values, valid):
    row = lax.broadcasted_iota(jnp.int32, values.shape, 0)
    return jnp.concatenate(
        [jnp.sum(jnp.where(row == valid + k, values, 0.0), axis=0, keepdims=True) for k in range(NOTES)], axis=0
    )


def onehot_rows(places, start):
    rows = places.shape[0]
    return (lanes_of(rows, SLOTS) == places - start).astype(F32).astype(LOW)


def onehot_columns(places, start):
    columns = places.shape[1]
    return (lax.broadcasted_iota(jnp.int32, (SLOTS, columns), 0) == places - start).astype(F32).astype(LOW)


def side(tile, p):
    lane = lanes_of(tile.shape[0])
    return jnp.where((lane < HEAD_DIM) if p == 0 else (lane >= HEAD_DIM), tile, jnp.zeros_like(tile))


def head_side(values, h, p):
    tile = values[:, h // 2 * PAIR : (h // 2 + 1) * PAIR]
    if tile.shape[1] < PAIR:
        tile = jnp.concatenate([tile, jnp.zeros_like(tile)], axis=1)
    if h % 2 != p:
        tile = pltpu.roll(tile, HEAD_DIM, 1)
    return side(tile, p)


def valid_rows(window):
    row = lax.broadcasted_iota(jnp.int32, (SLOTS, 1), 0)
    kept = row < 0
    for first, end in window[1]:
        kept |= (row >= first) & (row < end)
    return kept


def call(body, grid, out_shape, in_specs, out_specs, scratch=(), limit=60):
    return pl.pallas_call(
        body,
        grid=grid,
        out_shape=out_shape,
        in_specs=in_specs,
        out_specs=out_specs,
        scratch_shapes=list(scratch),
        compiler_params=pltpu.CompilerParams(
            vmem_limit_bytes=limit * MIB, dimension_semantics=("arbitrary",) * len(grid)
        ),
        cost_estimate=pl.CostEstimate(flops=1, bytes_accessed=1, transcendentals=0),
    )


def shape(dims, kind=LOW):
    return jax.ShapeDtypeStruct(tuple(dims), kind)


def step_spec(dims):
    rest = tuple(dims[1:])
    return pl.BlockSpec((1, *rest), lambda b: (b,) + (0,) * len(rest))


def table_spec(dims, groups):
    rest = tuple(dims[1:])
    return pl.BlockSpec((dims[0] // groups, *rest), lambda b: (b,) + (0,) * len(rest))


def full_spec(dims):
    return pl.BlockSpec(tuple(dims), lambda b: (0,) * len(dims))


def first_kernel(cuts, valid, *refs):
    me, own, near, far, diagonal, places, *rest = refs
    query, key, value, vectors, first_out, kv_out, sums_out, sheet = rest
    gain, shift = vectors[0:1], vectors[1:2]
    query_bias, value_bias = vectors[5:6, : query.shape[0]], vectors[6:7, : query.shape[0]]
    rows = own.shape[2]
    heads = len(cuts)
    wide = heads * PAIR
    sheet[...] = jnp.zeros_like(sheet)
    for p in range(2):
        tokens = jnp.concatenate([r[0, p] for r in (own, near, far, diagonal)], axis=0).astype(F32)
        unit, _ = standard(tokens)
        first = (unit * gain + shift).astype(LOW)
        first_out[0, p] = first
        queries = (dot(first, query[...], 1, 1) + query_bias).astype(LOW).astype(F32)
        keys = dot(first, key[...], 1, 1)
        values = dot(first, value[...], 1, 1) + value_bias
        one = side(jnp.ones((first.shape[0], PAIR), F32), p)
        for h, (start, _) in enumerate(cuts):
            kv_out[0, p, :, h * PAIR : (h + 1) * PAIR] = head_side(keys, h, p).astype(LOW)
            kv_out[0, p, :, wide + h * PAIR : wide + (h + 1) * PAIR] = head_side(values, h, p).astype(LOW)
            both = jnp.concatenate([head_side(queries, h, p), one], axis=1).astype(LOW)
            part = None
            for k in range(4):
                member = onehot_columns(places[0, p, me[0] ^ k, h : h + 1, :], start)
                term = dot(member, both[k * rows : (k + 1) * rows])
                part = term if part is None else part + term
            sheet[start : start + SLOTS] += part
    size = sums_out.shape[1]
    for d in range(sums_out.shape[0]):
        chunk = sheet[d * size : (d + 1) * size]
        notes = to_notes(chunk[:, PAIR:])
        sums_out[d] = with_notes(chunk[:, :PAIR], notes, valid).astype(LOW)


def scores_of(centroid, keys):
    return dot(centroid, keys, 1, 1) * 0.125


def attend_kernel(cuts, valid, centroid, kv, packed, sheet):
    wide = len(cuts) * PAIR
    count, size = packed.shape[0], packed.shape[1]
    table = centroid[...].reshape(count * size, PAIR)
    lane = lanes_of(SLOTS)
    sheet[...] = jnp.zeros_like(sheet)
    for h, window in enumerate(cuts):
        start = window[0]
        mine = table[start : start + SLOTS]
        out = jnp.zeros((SLOTS, PAIR), F32)
        log = jnp.zeros((SLOTS, PAIR), F32)
        for p in range(2):
            keys = kv[0, p, :, h * PAIR : (h + 1) * PAIR]
            values = kv[0, p, :, wide + h * PAIR : wide + (h + 1) * PAIR]
            scores = scores_of(mine, keys)
            top = jnp.max(scores, axis=-1, keepdims=True)
            exponent = jnp.exp(scores - top)
            total = jnp.sum(exponent, axis=-1, keepdims=True)
            out += dot(exponent.astype(LOW), values) / total
            log = jnp.where((lane < HEAD_DIM) if p == 0 else (lane >= HEAD_DIM), top + jnp.log(total), log)
        both = jnp.concatenate([out, log], axis=1)
        sheet[start : start + SLOTS] += jnp.where(valid_rows(window), both, 0.0)
    for d in range(count):
        chunk = sheet[d * size : (d + 1) * size]
        packed[d] = with_notes(chunk[:, :PAIR], to_notes(chunk[:, PAIR:]), valid).astype(LOW)


def half_wise(first, second, rows):
    return jnp.where(lanes_of(rows) < HEAD_DIM, first, second)


def merge_kernel(valid, packed, copies, out_shard):
    count, rows = packed.shape[0], packed.shape[1]
    logs, parts = [], []
    for i in range(count):
        part = packed[i].astype(F32)
        logs.append(half_wise(*from_notes(notes_of(part, valid), rows), rows))
        parts.append(part)
    top = logs[0]
    for log in logs[1:]:
        top = jnp.maximum(top, log)
    total = jnp.zeros((rows, PAIR), F32)
    out = jnp.zeros((rows, PAIR), F32)
    for i in range(count):
        weight = jnp.exp(logs[i] - top)
        total += weight
        out += weight * parts[i]
    out = out / total
    out_shard[...] = out
    low = with_notes(out, to_notes(top + jnp.log(total)), valid).astype(LOW)
    for k in range(copies.shape[0]):
        copies[k] = low


def join_heads(picked, p):
    rows = picked[0].shape[0]
    lane = lanes_of(rows)
    tiles = []
    for g in range(0, len(picked), 2):
        even = picked[g]
        odd = picked[g + 1] if g + 1 < len(picked) else even
        if p == 0:
            tile = jnp.where(lane < HEAD_DIM, even, pltpu.roll(odd, HEAD_DIM, 1))
        else:
            tile = jnp.where(lane < HEAD_DIM, pltpu.roll(even, HEAD_DIM, 1), odd)
        tiles.append(tile)
    joined = jnp.concatenate(tiles, axis=1)
    return joined[:, : len(picked) * HEAD_DIM]


def gelu_parts(values):
    area = 0.5 * (1.0 + lax.erf(values * 0.7071067811865476))
    density = jnp.exp(-0.5 * values * values) * 0.3989422804014327
    return values * area, area + values * density


def lay_out(table, whole):
    size = table.shape[2]
    for m in range(table.shape[1]):
        for d in range(table.shape[0]):
            whole[m, d * size : (d + 1) * size] = table[d, m]


def dense_kernel(cuts, which, *refs):
    (
        me,
        table,
        places,
        tokens_a,
        tokens_b,
        cot_a,
        cot_b,
        output_weight,
        expand_weight,
        shrink_weight,
        vectors,
        second_a,
        second_b,
        ffn_a,
        ffn_b,
        hidden_out,
        mine_out,
        normed_out,
        activated_out,
        expand_out,
        bias_out,
        attended,
        whole,
    ) = refs
    rows = tokens_a.shape[2]
    groups = table.shape[1]
    lay_out(table, whole)
    for p in range(2):
        picked = []
        for m in range(groups):
            column = jnp.concatenate([places[m, 0, p, me[0] ^ (2 * which + j)].T for j in range(2)], axis=0)
            for h, (start, _) in enumerate(cuts):
                member = onehot_rows(column[:, h : h + 1], start)
                picked.append(dot(member, whole[me[0] ^ m, start : start + SLOTS]))
        attended[p * 2 * rows : (p + 1) * 2 * rows] = join_heads(picked, p).astype(LOW)
        mine_out[0, p * 2 * rows : (p + 1) * 2 * rows] = join_heads(picked[: len(cuts)], p).astype(LOW)
    tokens = jnp.concatenate([tokens_a[0, 0], tokens_b[0, 0], tokens_a[0, 1], tokens_b[0, 1]], axis=0)
    cotangent = jnp.concatenate([cot_a[0, 0], cot_b[0, 0], cot_a[0, 1], cot_b[0, 1]], axis=0)
    hidden = tokens.astype(F32) + dot(attended[...], output_weight[...]) + vectors[4:5]
    unit, _ = standard(hidden)
    normed = (unit * vectors[2:3] + vectors[3:4]).astype(LOW)
    expanded = dot(normed, expand_weight[...]) + jnp.concatenate([vectors[k : k + 1] for k in range(7, vectors.shape[0])], axis=1)
    active, slope = gelu_parts(expanded)
    active = active.astype(LOW)
    back = (dot(cotangent, shrink_weight[...], 1, 1) * slope).astype(LOW)
    second = dot(back, expand_weight[...], 1, 1)
    ffn = dot(active, shrink_weight[...])
    for j, (second_ref, ffn_ref) in enumerate(((second_a, ffn_a), (second_b, ffn_b))):
        for p in range(2):
            at = (2 * p + j) * rows
            second_ref[0, p] = second[at : at + rows].astype(second_ref.dtype)
            ffn_ref[0, p] = ffn[at : at + rows].astype(ffn_ref.dtype)
    for p in range(2):
        hidden_out[0, p] = hidden[2 * p * rows : (2 * p + 1) * rows]
    normed_out[0] = normed
    activated_out[0] = active
    expand_out[0] = back

    @pl.when(pl.program_id(0) == 0)
    def _():
        bias_out[...] = jnp.zeros_like(bias_out)

    bias_out[...] += jnp.sum(back.astype(F32), axis=0, keepdims=True)


def products_of(terms, refs):
    refs = list(refs)
    products = []
    for pieces in terms:
        lefts = [refs.pop(0) for _ in range(2)]
        rights = [refs.pop(0) for _ in range(4 if pieces else 2)]
        if pieces:
            near, far = rights[:2], rights[2:]
            right = [r[0, p] for pair in (near, far) for p in range(2) for r in pair]
        else:
            right = [r[0] for r in rights]
        products.append(
            dot(jnp.concatenate([v[0] for v in lefts], axis=0), jnp.concatenate(right, axis=0), 0, 0)
        )
    return products


def grads_kernel(terms, steps, *refs):
    inputs = sum(2 + (4 if pieces else 2) for pieces in terms)
    products, refs = products_of(terms, refs[:inputs]), refs[inputs:]
    outs, totals = refs[: len(terms)], refs[len(terms) :]
    for k, product in enumerate(products):
        if steps > 1:
            total = totals[k]
            total[...] = jnp.where(pl.program_id(0) == 0, product, total[...] + product)
            product = total[...]
        outs[k][...] = product.astype(LOW)


def halves_kernel(terms, steps, uppers, *refs):
    inputs = sum(2 + (4 if pieces else 2) for pieces in terms)
    outs, totals = refs[inputs : inputs + 2 * len(terms)], refs[inputs + 2 * len(terms) :]
    for k, product in enumerate(products_of(terms, refs[:inputs])):
        total = totals[k]
        if steps > 1:
            product = jnp.where(pl.program_id(0) == 0, product, total[...] + product)
        total[...] = product
        count = total.shape[0] // 2
        upper = uppers[k]
        outs[2 * k][...] = total[pl.ds(pl.multiple_of(upper * count, count), count)].astype(LOW)
        outs[2 * k + 1][...] = total[pl.ds(pl.multiple_of((1 - upper) * count, count), count)].astype(LOW)


def hidden_kernel(cuts, *refs):
    (
        me,
        own,
        near,
        across,
        hidden,
        cot,
        places,
        output_weight,
        vectors,
        grad_out,
        low_out,
        table_out,
        small_out,
        whole,
    ) = refs
    groups, heads = table_out.shape[1], len(cuts)
    small = [jnp.zeros((1, own.shape[3]), F32) for _ in range(4)]
    parts = []
    for p in range(2):
        grad = own[0, p] + near[0, p].astype(F32) + across[0, p].astype(F32)
        unit, scale = standard(hidden[0, p])
        dy = cot[0, p].astype(F32)
        total = dy + norm_back(grad, unit, scale, vectors[2:3])
        grad_out[0, p] = total
        low = total.astype(LOW)
        low_out[0, p] = low
        for k, row in enumerate((total, dy, grad * unit, grad)):
            small[k] += jnp.sum(row, axis=0, keepdims=True)
        parts.append(dot(low, output_weight[...], 1, 1))
    whole[...] = jnp.zeros_like(whole)
    for k in range(groups * heads):
        m, h = k // heads, k % heads
        start = cuts[h][0]
        found = None
        for p in range(2):
            member = onehot_columns(places[m, 0, p, me[0], h : h + 1, :], start)
            term = dot(member, head_side(parts[p], k, p).astype(LOW))
            found = term if p == 0 else found + term
        whole[m, start : start + SLOTS] += found
    size = table_out.shape[2]
    for m in range(groups):
        for d in range(table_out.shape[0]):
            table_out[d, me[0] ^ m] = whole[m, d * size : (d + 1) * size].astype(LOW)

    @pl.when(pl.program_id(0) == 0)
    def _():
        small_out[...] = jnp.zeros_like(small_out)

    for k in range(4):
        small_out[k : k + 1, :] += small[k]


def out_grad_kernel(valid, parts, out_shard, copies):
    count, rows = parts.shape[0], parts.shape[1]
    total = jnp.zeros((rows, PAIR), F32)
    for i in range(count):
        total += parts[i].astype(F32)
    total = total.astype(LOW).astype(F32)
    product = total * out_shard[...]
    deltas = [jnp.sum(side(product, p), axis=-1, keepdims=True) for p in range(2)]
    low = with_notes(total, to_notes(half_wise(*deltas, rows)), valid).astype(LOW)
    for k in range(copies.shape[0]):
        copies[k] = low


def back_kernel(cuts, valid, me, centroid, kv, grads, out_table, part_out, prob_out, score_out, sheet, columns):
    wide = len(cuts) * PAIR
    count, size = part_out.shape[0], part_out.shape[1]
    table = centroid[...].reshape(count * size, PAIR)
    grad_table = grads[...].reshape(count * size, PAIR)
    for d in range(count):
        delta = from_notes(notes_of(grads[d].astype(F32), valid), size)
        log = from_notes(notes_of(out_table[d, me[0]].astype(F32), valid), size)
        for k, column in enumerate((*delta, *log)):
            columns[d * size : (d + 1) * size, k * PAIR : (k + 1) * PAIR] = jnp.broadcast_to(column, (size, PAIR))
    sheet[...] = jnp.zeros_like(sheet)
    for h, window in enumerate(cuts):
        start = window[0]
        mine, out_grad = table[start : start + SLOTS], grad_table[start : start + SLOTS]
        kept = valid_rows(window)
        part = None
        for p in range(2):
            keys = kv[0, p, :, h * PAIR : (h + 1) * PAIR]
            values = kv[0, p, :, wide + h * PAIR : wide + (h + 1) * PAIR]
            delta = columns[start : start + SLOTS, p * PAIR : p * PAIR + 1]
            log = columns[start : start + SLOTS, (2 + p) * PAIR : (2 + p) * PAIR + 1]
            probs = jnp.where(kept, jnp.exp(scores_of(mine, keys) - log), 0.0)
            grad = (probs * (dot(out_grad, values, 1, 1) - delta) * 0.125).astype(LOW)
            term = dot(grad, keys)
            part = term if p == 0 else part + term
            prob_out[0, p, h] = probs.astype(LOW)
            score_out[0, p, h] = grad
        sheet[start : start + SLOTS] += part
    for d in range(count):
        part_out[d] = sheet[d * size : (d + 1) * size].astype(LOW)


def kv_kernel(cuts, *refs):
    centroid, out_grads, probs, grads, key_weight, value_weight, key_out, value_out, own, near, far, diagonal = refs
    share = own.shape[2]
    count, size = centroid.shape[0], centroid.shape[1]
    table = centroid[...].reshape(count * size, PAIR)
    grad_table = out_grads[...].reshape(count * size, PAIR)
    for p in range(2):
        key_parts, value_parts = [], []
        for h, (start, _) in enumerate(cuts):
            key_parts.append(dot(grads[0, p, h], table[start : start + SLOTS], 0, 0))
            value_parts.append(dot(probs[0, p, h], grad_table[start : start + SLOTS], 0, 0))
        keys = join_heads(key_parts, p).astype(LOW)
        values = join_heads(value_parts, p).astype(LOW)
        key_out[0, p] = keys
        value_out[0, p] = values
        first = dot(keys, key_weight[...]) + dot(values, value_weight[...])
        for k, ref in enumerate((own, near, far, diagonal)):
            ref[0, p] = first[k * share : (k + 1) * share].astype(ref.dtype)


def centroid_kernel(valid, parts, copies, inverse):
    count, rows = parts.shape[0], parts.shape[1]
    total = parts[0].astype(F32)
    for i in range(1, count):
        total += parts[i].astype(F32)
    counts = half_wise(*from_notes(notes_of(total, valid), rows), rows)
    share = 1.0 / jnp.maximum(counts, 1.0)
    inverse[...] = share
    row = lax.broadcasted_iota(jnp.int32, (rows, PAIR), 0)
    low = jnp.where(row < valid, total * share, 0.0).astype(LOW)
    for k in range(copies.shape[0]):
        copies[k] = low


def mean_kernel(parts, inverse, copies):
    total = parts[0].astype(F32)
    for i in range(1, parts.shape[0]):
        total += parts[i].astype(F32)
    low = (total * inverse[...]).astype(LOW)
    for k in range(copies.shape[0]):
        copies[k] = low


def query_kernel(cuts, steps, *refs):
    me, table, places, first, early, grad_out, bias_out, *total = refs
    count, size = table.shape[0], table.shape[1]
    whole = table[...].reshape(count * size, PAIR)
    product, bias = None, None
    for p in range(2):
        column = jnp.concatenate([places[0, p, me[0] ^ k].T for k in range(places.shape[2])], axis=0)
        picked = []
        for h, (start, _) in enumerate(cuts):
            member = onehot_rows(column[:, h : h + 1], start)
            picked.append(dot(member, whole[start : start + SLOTS]))
        query = join_heads(picked, p)
        term = dot(query.astype(LOW), first[0, p], 0, 0)
        row = jnp.sum(query, axis=0, keepdims=True)
        product = term if p == 0 else product + term
        bias = row if p == 0 else bias + row
    if steps > 1:
        opening = pl.program_id(0) == 0
        total[0][...] = jnp.where(opening, product, total[0][...] + product)
        total[1][...] = jnp.where(opening, bias, total[1][...] + bias)
        product, bias = total[0][...], total[1][...]
    each = product.shape[0] // early.shape[0]
    for d in range(early.shape[0]):
        rows = [early[d].astype(F32), product[d * each : (d + 1) * each]]
        grad_out[d] = jnp.concatenate(rows, axis=0).astype(LOW)
    bias_out[...] = bias


def last_kernel(cuts, *refs):
    (
        me,
        table_own,
        table_near,
        table_far,
        table_diagonal,
        places,
        own,
        near,
        across,
        tokens,
        hidden_grad,
        weight,
        vectors,
        token_out,
        small_out,
    ) = refs
    tables = [t[...].reshape(-1, PAIR) for t in (table_own, table_near, table_far, table_diagonal)]
    small = [jnp.zeros((1, own.shape[3]), F32) for _ in range(2)]
    for p in range(2):
        picked = []
        for m, whole in enumerate(tables):
            column = places[m, 0, p, me[0]].T
            for h, (start, _) in enumerate(cuts):
                member = onehot_rows(column[:, h : h + 1], start)
                picked.append(dot(member, whole[start : start + SLOTS]))
        query = join_heads(picked, p).astype(LOW)
        grad = own[0, p] + near[0, p].astype(F32) + across[0, p].astype(F32)
        grad += dot(query, weight[...])
        unit, scale = standard(tokens[0, p].astype(F32))
        token_out[0, p] = hidden_grad[0, p] + norm_back(grad, unit, scale, vectors[0:1])
        for k, row in enumerate((grad * unit, grad)):
            small[k] += jnp.sum(row, axis=0, keepdims=True)

    @pl.when(pl.program_id(0) == 0)
    def _():
        small_out[...] = jnp.zeros_like(small_out)

    for k in range(2):
        small_out[k : k + 1, :] += small[k]


def split3(values):
    high = values.astype(LOW).astype(F32)
    middle = (values - high).astype(LOW).astype(F32)
    return high, middle, values - high - middle


def summed(parts):
    total = parts[0].astype(F32)
    for i in range(1, parts.shape[0]):
        total += parts[i].astype(F32)
    return total


def shard_kernel(parts, late, copies):
    total = summed(parts)
    sums = total[:1] + total[1:2] + total[2:3]
    low = jnp.concatenate([total[3:], *split3(sums), *split2(late[...])], axis=0).astype(LOW)
    for k in range(copies.shape[0]):
        copies[k] = low


def finish_kernel(each, found, *outs):
    count, width = found.shape[0], found.shape[2]
    parts = [found[d].astype(F32) for d in range(count)]
    for k in range(4):
        outs[k][...] = jnp.concatenate([v[k * each : (k + 1) * each] for v in parts], axis=0)
    at = 4 * each
    sums = [v[at : at + 1] + v[at + 1 : at + 2] + v[at + 2 : at + 3] for v in parts]
    late = parts[0][at + 3 :]
    for v in parts[1:]:
        late += v[at + 3 :]
    late = late[:3] + late[3:]
    part = width // count

    def row(k):
        return jnp.concatenate([v[:, k * part : (k + 1) * part] for v in sums], axis=1)

    query_bias, value_bias, expand_bias = outs[10:]
    for k in range(4):
        outs[4 + k][...] = row(k)[0]
    value_bias[...] = row(4)[0, : value_bias.shape[0]]
    expand_bias[...] = row(5)[0]
    for k in range(2):
        outs[8 + k][...] = late[k]
    query_bias[...] = late[2, : query_bias.shape[0]]


def partner(value, step):
    size = lax.axis_size("mp")
    return lax.ppermute(value, "mp", [(i, i ^ step) for i in range(size)])


def gather_rows(value):
    far = partner(value, 2)
    near = partner(value, 1)
    return value, near, far, partner(far, 1)


def scatter_rows(near, far, diagonal):
    near_in, diagonal_in = partner(near, 1), partner(diagonal, 1)
    across = (far.astype(F32) + diagonal_in.astype(F32)).astype(LOW)
    return near_in, partner(across, 2)


def exchange(copies, axes):
    return lax.all_to_all(copies, axes, 0, 0)


def after(value, *others):
    return lax.optimization_barrier((value, others))[0]


def together(*values):
    return lax.optimization_barrier(values)


def shards(
    tokens,
    cluster_ids,
    query_weight,
    query_bias,
    key_weight,
    value_weight,
    value_bias,
    output_weight,
    output_bias,
    expand_weight,
    expand_bias,
    shrink_weight,
    shrink_bias,
    first_gain,
    first_shift,
    second_gain,
    second_shift,
    cotangent,
):
    seqs, share, width = tokens.shape
    heads = cluster_ids.shape[2]
    hidden_units = expand_weight.shape[1]
    n_dp, n_mp = lax.axis_size("dp"), lax.axis_size("mp")
    both = ("dp", "mp")
    n_all = n_dp * n_mp
    all_heads = heads * n_mp
    half = seqs // 2
    local = share * n_mp
    head_width = heads * HEAD_DIM
    wide = heads * PAIR
    valid = half * heads * CLUSTERS // n_dp
    size = -(-(valid + NOTES) // 16) * 16
    per_pair = n_dp // half
    cuts = windows(heads, valid, size)
    table_rows = per_pair * size
    me = lax.axis_index("mp")
    me_ref = me.astype(jnp.int32).reshape(1)

    def sequences(value):
        return value.reshape(half, 2, *value.shape[1:])

    token_pairs = sequences(tokens)
    token_far, token_near = partner(token_pairs, 2), partner(token_pairs, 1)
    places = place(cluster_ids + jnp.arange(heads, dtype=jnp.int32) * CLUSTERS, valid, size)
    places_row = places.reshape(half, 2, n_mp, share, heads).transpose(0, 1, 2, 4, 3)
    places_row = jnp.pad(places_row, ((0, 0),) * 3 + ((0, 8 - heads), (0, 0)))
    vectors = jnp.stack(
        [
            jnp.pad(v.astype(F32), (0, width - v.shape[0]))
            for v in (first_gain, first_shift, second_gain, second_shift, output_bias, query_bias, value_bias)
        ]
        + [expand_bias.astype(F32).reshape(-1, width)[k] for k in range(hidden_units // width)]
    )
    token_far, places_row, vectors = together(token_far, places_row, vectors)
    pieces = token_pairs, token_near, token_far, partner(token_far, 1)
    places_all = gather_rows(places_row)
    output_whole = jnp.concatenate(gather_rows(output_weight), axis=0)
    query_turned, key_turned, value_turned = query_weight.T, key_weight.T, value_weight.T
    query_pieces = gather_rows(query_turned)

    piece_dims = (half, 2, share, width)
    piece_spec = step_spec(piece_dims)
    square_spec = full_spec((width, width))
    head_spec = full_spec((head_width, width))
    me_spec = pl.BlockSpec(memory_space=pltpu.SMEM)
    kv_dims = (half, 2, local, 2 * wide)
    table_dims = (n_dp, size, PAIR)
    shard_dims = (size, PAIR)
    copies_dims = (n_all, *shard_dims)
    all_dims = (n_dp, n_mp, *shard_dims)
    sheet = pltpu.VMEM((table_rows, 2 * PAIR), F32)
    group_scratch = pltpu.VMEM((n_mp, table_rows, PAIR), LOW)
    places_spec = pl.BlockSpec((n_mp, 1, 2, n_mp, 8, share), lambda b: (0, b, 0, 0, 0, 0))
    vectors_spec = full_spec(vectors.shape)

    first, kv, sums = call(
        partial(first_kernel, cuts, valid),
        (half,),
        (shape((half, 2, local, width)), shape(kv_dims), shape(table_dims)),
        [me_spec]
        + [piece_spec] * 4
        + [step_spec((half, 2, n_mp, 8, share))]
        + [head_spec] * 3
        + [vectors_spec],
        (step_spec((half, 2, local, width)), step_spec(kv_dims), table_spec(table_dims, half)),
        [sheet],
    )(
        me_ref,
        *pieces,
        places_row,
        query_turned,
        key_turned,
        value_turned,
        vectors,
    )
    cotangent_pairs = sequences(cotangent)
    cot_start = after(cotangent_pairs, sums)
    cot_far, cot_near = partner(cot_start, 2), partner(cot_start, 1)

    sums = exchange(sums, "dp")
    sums, cot_far, cot_near = together(sums, cot_far, cot_near)
    cot_diagonal = partner(cot_far, 1)
    copies, inverse = call(
        partial(centroid_kernel, valid),
        (1,),
        (shape(table_dims), shape(shard_dims, F32)),
        [full_spec(table_dims)],
        (full_spec(table_dims), full_spec(shard_dims)),
    )(sums)
    centroid = exchange(copies, "dp")
    centroid, cot_diagonal = together(centroid, cot_diagonal)

    packed = call(
        partial(attend_kernel, cuts, valid),
        (half,),
        shape(table_dims),
        [table_spec(table_dims, half), step_spec(kv_dims)],
        table_spec(table_dims, half),
        [sheet],
    )(centroid, kv)
    packed = exchange(packed, "dp")
    packed, output_whole, *places_all = together(packed, output_whole, *places_all)
    places_all = jnp.stack(places_all)
    copies, out_shard = call(
        partial(merge_kernel, valid),
        (1,),
        (shape(copies_dims), shape(shard_dims, F32)),
        [full_spec(table_dims)],
        (full_spec(copies_dims), full_spec(shard_dims)),
    )(packed)
    out_table = exchange(copies, both).reshape(all_dims)
    out_table, *query_pieces = together(out_table, *query_pieces)
    query_whole = jnp.concatenate(query_pieces, axis=0)

    dense_rows = 4 * share

    def dense(which, kinds, tokens_a, tokens_b, cot_a, cot_b):
        dims = (half, dense_rows)
        return call(
            partial(dense_kernel, cuts, which),
            (half,),
            (
                shape(piece_dims, kinds[0]),
                shape(piece_dims, kinds[1]),
                shape(piece_dims, kinds[0]),
                shape(piece_dims, kinds[1]),
                shape(piece_dims, F32),
                shape((*dims, head_width)),
                shape((*dims, width)),
                shape((*dims, hidden_units)),
                shape((*dims, hidden_units)),
                shape((1, hidden_units), F32),
            ),
            [me_spec, table_spec(all_dims, half), places_spec]
            + [piece_spec] * 4
            + [square_spec, full_spec((width, hidden_units)), full_spec((hidden_units, width)), vectors_spec],
            (
                *[piece_spec] * 5,
                step_spec((*dims, head_width)),
                step_spec((*dims, width)),
                step_spec((*dims, hidden_units)),
                step_spec((*dims, hidden_units)),
                full_spec((1, hidden_units)),
            ),
            [pltpu.VMEM((dense_rows, width), LOW), group_scratch],
        )(
            me_ref,
            out_table,
            places_all,
            tokens_a,
            tokens_b,
            cot_a,
            cot_b,
            output_whole,
            expand_weight,
            shrink_weight,
            vectors,
        )

    beyond = dense(1, (F32, LOW), pieces[2], pieces[3], cot_far, cot_diagonal)
    diagonal_in = partner(beyond[1], 1)
    inside = dense(0, (F32, LOW), after(pieces[0], *beyond), pieces[1], cotangent_pairs, cot_near)
    across_in = partner((beyond[0] + diagonal_in.astype(F32)).astype(LOW), 2)
    near_in = partner(inside[1], 1)
    hidden_own = inside[4]

    def grads(terms, dims, operands):
        return call(
            partial(grads_kernel, terms, half),
            (half,),
            tuple(shape(dims) for _ in terms),
            [step_spec(value.shape) for value in operands],
            tuple(full_spec(dims) for _ in terms),
            [] if half == 1 else [pltpu.VMEM(dims, F32)] * len(terms),
        )(*operands)

    my_dp = lax.axis_index("dp")
    steps = n_dp.bit_length() - 1

    def opposite(value, step):
        return lax.ppermute(value, "dp", [(i, i ^ (1 << step)) for i in range(n_dp)])

    def halved(value, step):
        count = value.shape[0] // 2
        upper = (my_dp >> step) % 2 == 1
        return jnp.where(upper, value[count:], value[:count]), jnp.where(upper, value[:count], value[count:])

    def added(kept, arrived):
        return (kept.astype(F32) + arrived.astype(F32)).astype(LOW)

    def joined(value, arrived, step):
        upper = (my_dp >> step) % 2 == 1
        return jnp.where(
            upper, jnp.concatenate([arrived, value], axis=0), jnp.concatenate([value, arrived], axis=0)
        )

    orders = [list(range(steps)), [1, 0, *range(2, steps)]]

    def ffn_step(kept, arrived, index):
        if arrived is not None:
            kept = [added(k, v) for k, v in zip(kept, arrived)]
        cut_in_two = [halved(v, order[index]) for v, order in zip(kept, orders)]
        return [v[0] for v in cut_in_two], [opposite(v[1], order[index]) for v, order in zip(cut_in_two, orders)]

    def ffn_join(kept, arrived, index):
        return [joined(v, w, order[index]) for v, w, order in zip(kept, arrived, orders)]

    def ffn_send(kept, index):
        return [opposite(v, order[index]) for v, order in zip(kept, orders)]

    operands = (
        (beyond[7], inside[7], cot_far, cot_diagonal, cotangent_pairs, cot_near)
        + (beyond[6], inside[6], beyond[8], inside[8])
    )
    uppers = jnp.stack([(my_dp >> order[0]) % 2 for order in orders]).astype(jnp.int32)
    half_dims = (hidden_units // 2, width)
    ffn_halves = call(
        partial(halves_kernel, (True, False), half),
        (half,),
        tuple(shape(half_dims) for _ in range(4)),
        [me_spec] + [step_spec(value.shape) for value in operands],
        tuple(full_spec(half_dims) for _ in range(4)),
        [pltpu.VMEM((hidden_units, width), F32)] * 2,
    )(uppers, *operands)
    ffn_now = [ffn_halves[0], ffn_halves[2]]
    ffn_in = [opposite(ffn_halves[2 * k + 1], order[0]) for k, order in enumerate(orders)]
    expand_bias_grad = beyond[9] + inside[9]
    near_in, across_in, *ffn_now = together(near_in, across_in, *ffn_now)

    hidden_grad, hidden_low, out_part, small_two = call(
        partial(hidden_kernel, cuts),
        (half,),
        (shape(piece_dims, F32), shape(piece_dims), shape(all_dims), shape((8, width), F32)),
        [me_spec] + [piece_spec] * 5 + [places_spec, square_spec, vectors_spec],
        (piece_spec, piece_spec, table_spec(all_dims, half), full_spec((8, width))),
        [pltpu.VMEM((n_mp, table_rows, PAIR), F32)],
    )(
        me_ref,
        inside[0],
        near_in,
        across_in,
        hidden_own,
        cotangent_pairs,
        places_all,
        output_whole,
        vectors,
    )
    out_part, *ffn_in = together(out_part, *ffn_in)
    ffn_now, ffn_in = ffn_step(ffn_now, ffn_in, 1)
    out_part = exchange(out_part.reshape(copies_dims), both)
    out_part, query_whole, *ffn_in = together(out_part, query_whole, *ffn_in)
    for index in range(2, steps):
        ffn_now, ffn_in = ffn_step(ffn_now, ffn_in, index)
    out_grad = call(
        partial(out_grad_kernel, valid),
        (1,),
        shape(table_dims),
        [full_spec(copies_dims), full_spec(shard_dims)],
        full_spec(table_dims),
    )(out_part, out_shard)
    out_grad = exchange(out_grad, "dp")
    low_start = after(hidden_low, out_grad)
    low_near, low_far = partner(low_start, 1), partner(low_start, 2)
    early_small = small_two[:4]
    for step in range(n_mp.bit_length() - 1):
        early_small += partner(early_small, 1 << step)

    score_dims = (half, 2, heads, SLOTS, local)
    centroid_part, probs, score_grad = call(
        partial(back_kernel, cuts, valid),
        (half,),
        (shape(table_dims), shape(score_dims), shape(score_dims)),
        [me_spec, table_spec(table_dims, half), step_spec(kv_dims)]
        + [table_spec(table_dims, half), table_spec(all_dims, half)],
        (table_spec(table_dims, half), step_spec(score_dims), step_spec(score_dims)),
        [pltpu.VMEM((table_rows, PAIR), F32), pltpu.VMEM((table_rows, 4 * PAIR), F32)],
    )(me_ref, centroid, kv, out_grad, out_table)
    centroid_part, *ffn_in = together(centroid_part, *ffn_in)
    ffn_now = [added(k, v) for k, v in zip(ffn_now, ffn_in)]
    ffn_in = ffn_send(ffn_now, steps - 1)
    low_diagonal = partner(after(low_far, centroid_part), 1)
    centroid_part = exchange(centroid_part, "dp")

    grad_dims = (half, 2, local, head_width)
    key_grad, value_grad, first_own, *first_parts = call(
        partial(kv_kernel, cuts),
        (half,),
        (shape(grad_dims), shape(grad_dims), *[shape(piece_dims, kind) for kind in (F32, LOW, F32, LOW)]),
        [table_spec(table_dims, half)] * 2
        + [step_spec(score_dims), step_spec(score_dims)]
        + [head_spec] * 2,
        (step_spec(grad_dims), step_spec(grad_dims), *[piece_spec] * 4),
    )(centroid, out_grad, probs, score_grad, key_turned, value_turned)

    count_rows = seqs * local
    first_flat = first.reshape(count_rows, width)
    value_flat = value_grad.reshape(count_rows, head_width)
    key_weight_grad = dot(key_grad.reshape(count_rows, head_width), first_flat, 0, 0).astype(LOW)
    value_weight_grad = dot(value_flat, first_flat, 0, 0).astype(LOW)
    value_bias_grad = jnp.sum(value_flat.astype(F32), axis=0)
    early_small = jnp.concatenate(
        [early_small, jnp.pad(value_bias_grad, (0, width - head_width))[None], expand_bias_grad], axis=0
    )
    key_weight_grad, value_weight_grad, *ffn_in = together(key_weight_grad, value_weight_grad, *ffn_in)
    near_in, diagonal_in = partner(first_parts[0], 1), partner(first_parts[2], 1)
    across = (first_parts[1].astype(F32) + diagonal_in.astype(F32)).astype(LOW)
    centroid_part, low_near, low_far, low_diagonal, first_own, early_small, key_weight_grad, *rest = together(
        centroid_part, low_near, low_far, low_diagonal, first_own, early_small, key_weight_grad, near_in, across, *ffn_in
    )
    (near_in, across), ffn_in = rest[:2], rest[2:]
    for index in range(steps - 1, 1, -1):
        ffn_now = ffn_join(ffn_now, ffn_in, index)
        ffn_in = ffn_send(ffn_now, index - 1)
    (output_weight_grad,) = grads(
        (True,),
        (head_width, width),
        (beyond[5], inside[5], low_far, low_diagonal, hidden_low, low_near),
    )
    first_in = near_in, partner(across, 2)
    query_copies = call(
        mean_kernel,
        (1,),
        shape(table_dims),
        [full_spec(table_dims), full_spec(shard_dims)],
        full_spec(table_dims),
    )(centroid_part, inverse)
    query_table = exchange(query_copies, "dp")
    def cut(value, count):
        rows, columns = value.shape[0] // count, value.shape[1]
        value = value.reshape(count, n_dp, rows // n_dp, columns).transpose(1, 0, 2, 3)
        return value.reshape(n_dp, count * rows // n_dp, columns)

    part = early_small.shape[0] * width // n_dp
    early_small = early_small.reshape(-1, n_dp, width // n_dp).transpose(1, 0, 2).reshape(n_dp, 1, part)
    early_small = jnp.pad(early_small, ((0, 0), (0, 0), (0, width - part)))
    high = lax.reduce_precision(early_small, 8, 7)
    middle = lax.reduce_precision(early_small - high, 8, 7)
    early_small = jnp.concatenate([high, middle, early_small - high - middle], axis=1).astype(LOW)
    early = cut(jnp.concatenate([key_weight_grad, value_weight_grad, output_weight_grad]), 3)
    early = jnp.concatenate([early_small, early], axis=1)
    query_table, early, *rest = together(query_table, early, *first_in, *ffn_in)
    first_in, ffn_in = rest[:2], rest[2:]
    ffn_now = ffn_join(ffn_now, ffn_in, 1)
    ffn_in = ffn_send(ffn_now, 0)
    query_tables = gather_rows(query_table)

    merged = (n_dp, 3 + 4 * head_width // n_dp, width)
    merged_grads, query_bias_grad = call(
        partial(query_kernel, cuts, half),
        (half,),
        (shape(merged), shape((1, head_width), F32)),
        [me_spec, table_spec(table_dims, half), step_spec((half, 2, n_mp, 8, share))]
        + [step_spec((half, 2, local, width)), full_spec(early.shape)],
        (full_spec(merged), full_spec((1, head_width))),
        [] if half == 1 else [pltpu.VMEM((head_width, width), F32), pltpu.VMEM((1, head_width), F32)],
    )(me_ref, query_table, places_row, first, early)
    found = exchange(merged_grads, "dp")

    token_grad, small_one = call(
        partial(last_kernel, cuts),
        (half,),
        (shape(piece_dims, F32), shape((8, width), F32)),
        [me_spec]
        + [table_spec(table_dims, half)] * 4
        + [places_spec]
        + [piece_spec] * 5
        + [square_spec, vectors_spec],
        (piece_spec, full_spec((8, width))),
    )(
        me_ref,
        *query_tables,
        places_all,
        first_own,
        *first_in,
        pieces[0],
        hidden_grad,
        query_whole,
        vectors,
    )

    late = small_one[:2]
    for step in range(n_mp.bit_length() - 1):
        late += partner(late, 1 << step)
    late = jnp.concatenate([late, jnp.pad(query_bias_grad, ((0, 0), (0, width - head_width)))], axis=0)
    each = head_width // n_dp
    parts, late, *ffn_in = together(found, late, *ffn_in)
    shrink_weight_grad, expand_weight_grad = (v.astype(F32) for v in ffn_join(ffn_now, ffn_in, 0))
    found = shape((n_dp, 4 * each + 9, width))
    found = call(
        shard_kernel,
        (1,),
        found,
        [full_spec(parts.shape), full_spec(late.shape)],
        full_spec(found.shape),
        limit=64,
    )(parts, late)
    ffn_near, ffn_across = scatter_rows(inside[3], beyond[2], after(beyond[3], found))
    found = exchange(found, "dp")
    found, shrink_weight_grad, expand_weight_grad = together(found, shrink_weight_grad, expand_weight_grad)
    result = (
        hidden_own
        + inside[2]
        + ffn_near.astype(F32)
        + ffn_across.astype(F32)
        + shrink_bias.astype(F32)
    ).astype(LOW)
    lengths = [width] * 6 + [head_width] * 2 + [hidden_units]
    key_weight_grad, value_weight_grad, output_weight_grad, query_weight_grad, *vectors = call(
        partial(finish_kernel, each),
        (1,),
        tuple(shape((head_width, width), F32) for _ in range(4)) + tuple(shape((n,), F32) for n in lengths),
        [full_spec(found.shape)],
        tuple(full_spec((head_width, width)) for _ in range(4)) + tuple(full_spec((n,)) for n in lengths),
        limit=64,
    )(found)
    return (
        result.reshape(tokens.shape),
        token_grad.reshape(tokens.shape),
        query_weight_grad.T,
        vectors[6],
        key_weight_grad.T,
        value_weight_grad.T,
        vectors[7],
        output_weight_grad,
        vectors[0],
        expand_weight_grad,
        vectors[8],
        shrink_weight_grad,
        vectors[1],
        vectors[4],
        vectors[5],
        vectors[2],
        vectors[3],
    )


def solution(mesh):
    rows = P(None, ("dp", "mp"), None)
    columns, heads, vector, whole = P(None, "mp"), P("mp", None), P("mp"), P()
    return jax.shard_map(
        shards,
        mesh=mesh,
        in_specs=(
            rows,
            P(None, "dp", "mp"),
            columns,
            vector,
            columns,
            columns,
            vector,
            heads,
            whole,
            columns,
            vector,
            heads,
            whole,
            whole,
            whole,
            whole,
            whole,
            rows,
        ),
        out_specs=(
            rows,
            rows,
            columns,
            vector,
            columns,
            columns,
            vector,
            heads,
            whole,
            columns,
            vector,
            heads,
            whole,
            whole,
            whole,
            whole,
            whole,
        ),
        check_vma=False,
    )
```

```python
from functools import partial

import jax
import jax.numpy as jnp
from jax import lax
from jax.experimental import pallas as pl
from jax.experimental.pallas import tpu as pltpu
from jax.sharding import PartitionSpec as P

HEAD_DIM = 64
CLUSTERS = 200
SLOTS = 256
NOTES = 4
PAIR = 2 * HEAD_DIM
F32 = jnp.float32
LOW = jnp.bfloat16
MIB = 2**20


def dot(left, right, left_dim=1, right_dim=0):
    return lax.dot_general(
        left, right, (((left_dim,), (right_dim,)), ((), ())), preferred_element_type=F32
    )


def lanes_of(rows, width=PAIR):
    return lax.broadcasted_iota(jnp.int32, (rows, width), 1)


def standard(values):
    average = jnp.mean(values, axis=-1, keepdims=True)
    centered = values - average
    variance = jnp.mean(centered * centered, axis=-1, keepdims=True)
    scale = lax.rsqrt(variance + 1e-05)
    return centered * scale, scale


def norm_back(grad, unit, scale, gain):
    inner = grad * gain
    first = jnp.mean(inner, axis=-1, keepdims=True)
    second = jnp.mean(inner * unit, axis=-1, keepdims=True)
    return scale * (inner - first - unit * second)


def split2(values):
    high = values.astype(LOW).astype(F32)
    return high, (values - high).astype(LOW).astype(F32)


def place(row, valid, size):
    return row + (size - valid) * (row // valid)


def windows(heads, valid, size):
    end = place(heads * CLUSTERS - 1, valid, size) // size * size + size
    found = []
    for h in range(heads):
        start = min(place(h * CLUSTERS, valid, size) // 16 * 16, end - SLOTS)
        runs = []
        for row in range(h * CLUSTERS, (h + 1) * CLUSTERS):
            at = place(row, valid, size) - start
            if runs and runs[-1][1] == at:
                runs[-1][1] = at + 1
            else:
                runs.append([at, at + 1])
        found.append((start, runs))
    return found


def to_notes(column):
    rows = column.shape[0]
    sheet = lax.broadcasted_iota(jnp.int32, (rows, PAIR), 0) == lanes_of(rows)
    found = []
    for p in range(2):
        lane = jnp.sum(jnp.where(sheet, column[:, p * HEAD_DIM : p * HEAD_DIM + 1], 0.0), axis=0, keepdims=True)
        found += list(split2(lane))
    return found


def from_notes(notes, rows):
    sheet = lax.broadcasted_iota(jnp.int32, (rows, PAIR), 0) == lanes_of(rows)
    found = []
    for p in range(2):
        lane = notes[2 * p : 2 * p + 1] + notes[2 * p + 1 : 2 * p + 2]
        found.append(jnp.sum(jnp.where(sheet, lane, 0.0), axis=-1, keepdims=True))
    return found


def with_notes(values, notes, valid):
    row = lax.broadcasted_iota(jnp.int32, values.shape, 0)
    for k, note in enumerate(notes):
        values = jnp.where(row == valid + k, note, values)
    return values


def notes_of(values, valid):
    row = lax.broadcasted_iota(jnp.int32, values.shape, 0)
    return jnp.concatenate(
        [jnp.sum(jnp.where(row == valid + k, values, 0.0), axis=0, keepdims=True) for k in range(NOTES)], axis=0
    )


def onehot_rows(places, start):
    rows = places.shape[0]
    return (lanes_of(rows, SLOTS) == places - start).astype(F32).astype(LOW)


def onehot_columns(places, start):
    columns = places.shape[1]
    return (lax.broadcasted_iota(jnp.int32, (SLOTS, columns), 0) == places - start).astype(F32).astype(LOW)


def side(tile, p):
    lane = lanes_of(tile.shape[0])
    return jnp.where((lane < HEAD_DIM) if p == 0 else (lane >= HEAD_DIM), tile, jnp.zeros_like(tile))


def head_side(values, h, p):
    tile = values[:, h // 2 * PAIR : (h // 2 + 1) * PAIR]
    if tile.shape[1] < PAIR:
        tile = jnp.concatenate([tile, jnp.zeros_like(tile)], axis=1)
    if h % 2 != p:
        tile = pltpu.roll(tile, HEAD_DIM, 1)
    return side(tile, p)


def valid_rows(window):
    row = lax.broadcasted_iota(jnp.int32, (SLOTS, 1), 0)
    kept = row < 0
    for first, end in window[1]:
        kept |= (row >= first) & (row < end)
    return kept


def call(body, grid, out_shape, in_specs, out_specs, scratch=(), limit=58):
    return pl.pallas_call(
        body,
        grid=grid,
        out_shape=out_shape,
        in_specs=in_specs,
        out_specs=out_specs,
        scratch_shapes=list(scratch),
        compiler_params=pltpu.CompilerParams(
            vmem_limit_bytes=limit * MIB, dimension_semantics=("arbitrary",) * len(grid)
        ),
        cost_estimate=pl.CostEstimate(flops=1, bytes_accessed=1, transcendentals=0),
    )


def shape(dims, kind=LOW):
    return jax.ShapeDtypeStruct(tuple(dims), kind)


def step_spec(dims):
    rest = tuple(dims[1:])
    return pl.BlockSpec((1, *rest), lambda b: (b,) + (0,) * len(rest))


def table_spec(dims, groups):
    rest = tuple(dims[1:])
    return pl.BlockSpec((dims[0] // groups, *rest), lambda b: (b,) + (0,) * len(rest))


def full_spec(dims):
    return pl.BlockSpec(tuple(dims), lambda b: (0,) * len(dims))


def first_kernel(cuts, valid, *refs):
    me, own, near, far, diagonal, places, *rest = refs
    query, key, value, vectors, first_out, kv_out, sums_out, sheet = rest
    gain, shift = vectors[0:1], vectors[1:2]
    query_bias, value_bias = vectors[5:6, : query.shape[0]], vectors[6:7, : query.shape[0]]
    rows = own.shape[2]
    heads = len(cuts)
    wide = heads * PAIR
    sheet[...] = jnp.zeros_like(sheet)
    for p in range(2):
        tokens = jnp.concatenate([r[0, p] for r in (own, near, far, diagonal)], axis=0).astype(F32)
        unit, _ = standard(tokens)
        first = (unit * gain + shift).astype(LOW)
        first_out[0, p] = first
        queries = (dot(first, query[...], 1, 1) + query_bias).astype(LOW).astype(F32)
        keys = dot(first, key[...], 1, 1)
        values = dot(first, value[...], 1, 1) + value_bias
        one = side(jnp.ones((first.shape[0], PAIR), F32), p)
        for h, (start, _) in enumerate(cuts):
            kv_out[0, p, :, h * PAIR : (h + 1) * PAIR] = head_side(keys, h, p).astype(LOW)
            kv_out[0, p, :, wide + h * PAIR : wide + (h + 1) * PAIR] = head_side(values, h, p).astype(LOW)
            both = jnp.concatenate([head_side(queries, h, p), one], axis=1).astype(LOW)
            part = None
            for k in range(4):
                member = onehot_columns(places[0, p, me[0] ^ k, h : h + 1, :], start)
                term = dot(member, both[k * rows : (k + 1) * rows])
                part = term if part is None else part + term
            sheet[start : start + SLOTS] += part
    size = sums_out.shape[1]
    for d in range(sums_out.shape[0]):
        chunk = sheet[d * size : (d + 1) * size]
        notes = to_notes(chunk[:, PAIR:])
        sums_out[d] = with_notes(chunk[:, :PAIR], notes, valid).astype(LOW)


def scores_of(centroid, keys):
    return dot(centroid, keys, 1, 1) * 0.125


def attend_kernel(cuts, valid, centroid, kv, packed, sheet):
    wide = len(cuts) * PAIR
    count, size = packed.shape[0], packed.shape[1]
    table = centroid[...].reshape(count * size, PAIR)
    lane = lanes_of(SLOTS)
    sheet[...] = jnp.zeros_like(sheet)
    for h, window in enumerate(cuts):
        start = window[0]
        mine = table[start : start + SLOTS]
        out = jnp.zeros((SLOTS, PAIR), F32)
        log = jnp.zeros((SLOTS, PAIR), F32)
        for p in range(2):
            keys = kv[0, p, :, h * PAIR : (h + 1) * PAIR]
            values = kv[0, p, :, wide + h * PAIR : wide + (h + 1) * PAIR]
            scores = scores_of(mine, keys)
            top = jnp.max(scores, axis=-1, keepdims=True)
            exponent = jnp.exp(scores - top)
            total = jnp.sum(exponent, axis=-1, keepdims=True)
            out += dot(exponent.astype(LOW), values) / total
            log = jnp.where((lane < HEAD_DIM) if p == 0 else (lane >= HEAD_DIM), top + jnp.log(total), log)
        both = jnp.concatenate([out, log], axis=1)
        sheet[start : start + SLOTS] += jnp.where(valid_rows(window), both, 0.0)
    for d in range(count):
        chunk = sheet[d * size : (d + 1) * size]
        packed[d] = with_notes(chunk[:, :PAIR], to_notes(chunk[:, PAIR:]), valid).astype(LOW)


def half_wise(first, second, rows):
    return jnp.where(lanes_of(rows) < HEAD_DIM, first, second)


def merge_kernel(valid, packed, copies, out_shard):
    count, rows = packed.shape[0], packed.shape[1]
    logs, parts = [], []
    for i in range(count):
        part = packed[i].astype(F32)
        logs.append(half_wise(*from_notes(notes_of(part, valid), rows), rows))
        parts.append(part)
    top = logs[0]
    for log in logs[1:]:
        top = jnp.maximum(top, log)
    total = jnp.zeros((rows, PAIR), F32)
    out = jnp.zeros((rows, PAIR), F32)
    for i in range(count):
        weight = jnp.exp(logs[i] - top)
        total += weight
        out += weight * parts[i]
    out = out / total
    out_shard[...] = out
    low = with_notes(out, to_notes(top + jnp.log(total)), valid).astype(LOW)
    for k in range(copies.shape[0]):
        copies[k] = low


def join_heads(picked, p):
    rows = picked[0].shape[0]
    lane = lanes_of(rows)
    tiles = []
    for g in range(0, len(picked), 2):
        even = picked[g]
        odd = picked[g + 1] if g + 1 < len(picked) else even
        if p == 0:
            tile = jnp.where(lane < HEAD_DIM, even, pltpu.roll(odd, HEAD_DIM, 1))
        else:
            tile = jnp.where(lane < HEAD_DIM, pltpu.roll(even, HEAD_DIM, 1), odd)
        tiles.append(tile)
    joined = jnp.concatenate(tiles, axis=1)
    return joined[:, : len(picked) * HEAD_DIM]


def gelu_parts(values):
    area = 0.5 * (1.0 + lax.erf(values * 0.7071067811865476))
    density = jnp.exp(-0.5 * values * values) * 0.3989422804014327
    return values * area, area + values * density


def lay_out(table, whole):
    size = table.shape[2]
    for m in range(table.shape[1]):
        for d in range(table.shape[0]):
            whole[m, d * size : (d + 1) * size] = table[d, m]


def dense_kernel(cuts, which, *refs):
    (
        me,
        table,
        places,
        tokens_a,
        tokens_b,
        cot_a,
        cot_b,
        output_weight,
        expand_weight,
        shrink_weight,
        vectors,
        second_a,
        second_b,
        ffn_a,
        ffn_b,
        hidden_out,
        mine_out,
        normed_out,
        activated_out,
        expand_out,
        bias_out,
        attended,
        whole,
    ) = refs
    rows = tokens_a.shape[2]
    groups = table.shape[1]
    lay_out(table, whole)
    for p in range(2):
        picked = []
        for m in range(groups):
            column = jnp.concatenate([places[m, 0, p, me[0] ^ (2 * which + j)].T for j in range(2)], axis=0)
            for h, (start, _) in enumerate(cuts):
                member = onehot_rows(column[:, h : h + 1], start)
                picked.append(dot(member, whole[me[0] ^ m, start : start + SLOTS]))
        attended[p * 2 * rows : (p + 1) * 2 * rows] = join_heads(picked, p).astype(LOW)
        mine_out[0, p * 2 * rows : (p + 1) * 2 * rows] = join_heads(picked[: len(cuts)], p).astype(LOW)
    tokens = jnp.concatenate([tokens_a[0, 0], tokens_b[0, 0], tokens_a[0, 1], tokens_b[0, 1]], axis=0)
    cotangent = jnp.concatenate([cot_a[0, 0], cot_b[0, 0], cot_a[0, 1], cot_b[0, 1]], axis=0)
    hidden = tokens.astype(F32) + dot(attended[...], output_weight[...]) + vectors[4:5]
    unit, _ = standard(hidden)
    normed = (unit * vectors[2:3] + vectors[3:4]).astype(LOW)
    expanded = dot(normed, expand_weight[...]) + jnp.concatenate([vectors[k : k + 1] for k in range(7, vectors.shape[0])], axis=1)
    active, slope = gelu_parts(expanded)
    active = active.astype(LOW)
    back = (dot(cotangent, shrink_weight[...], 1, 1) * slope).astype(LOW)
    second = dot(back, expand_weight[...], 1, 1)
    ffn = dot(active, shrink_weight[...])
    for j, (second_ref, ffn_ref) in enumerate(((second_a, ffn_a), (second_b, ffn_b))):
        for p in range(2):
            at = (2 * p + j) * rows
            second_ref[0, p] = second[at : at + rows].astype(second_ref.dtype)
            ffn_ref[0, p] = ffn[at : at + rows].astype(ffn_ref.dtype)
    for p in range(2):
        hidden_out[0, p] = hidden[2 * p * rows : (2 * p + 1) * rows]
    normed_out[0] = normed
    activated_out[0] = active
    expand_out[0] = back

    @pl.when(pl.program_id(0) == 0)
    def _():
        bias_out[...] = jnp.zeros_like(bias_out)

    bias_out[...] += jnp.sum(back.astype(F32), axis=0, keepdims=True)


def products_of(terms, refs):
    refs = list(refs)
    products = []
    for pieces in terms:
        lefts = [refs.pop(0) for _ in range(2)]
        rights = [refs.pop(0) for _ in range(4 if pieces else 2)]
        if pieces:
            near, far = rights[:2], rights[2:]
            right = [r[0, p] for pair in (near, far) for p in range(2) for r in pair]
        else:
            right = [r[0] for r in rights]
        products.append(
            dot(jnp.concatenate([v[0] for v in lefts], axis=0), jnp.concatenate(right, axis=0), 0, 0)
        )
    return products


def grads_kernel(terms, steps, *refs):
    inputs = sum(2 + (4 if pieces else 2) for pieces in terms)
    products, refs = products_of(terms, refs[:inputs]), refs[inputs:]
    outs, totals = refs[: len(terms)], refs[len(terms) :]
    for k, product in enumerate(products):
        if steps > 1:
            total = totals[k]
            total[...] = jnp.where(pl.program_id(0) == 0, product, total[...] + product)
            product = total[...]
        outs[k][...] = product.astype(LOW)


def halves_kernel(terms, steps, uppers, *refs):
    inputs = sum(2 + (4 if pieces else 2) for pieces in terms)
    outs, totals = refs[inputs : inputs + 2 * len(terms)], refs[inputs + 2 * len(terms) :]
    for k, product in enumerate(products_of(terms, refs[:inputs])):
        total = totals[k]
        if steps > 1:
            product = jnp.where(pl.program_id(0) == 0, product, total[...] + product)
        total[...] = product
        count = total.shape[0] // 2
        upper = uppers[k]
        outs[2 * k][...] = total[pl.ds(pl.multiple_of(upper * count, count), count)].astype(LOW)
        outs[2 * k + 1][...] = total[pl.ds(pl.multiple_of((1 - upper) * count, count), count)].astype(LOW)


def hidden_kernel(cuts, *refs):
    (
        me,
        own,
        near,
        across,
        hidden,
        cot,
        places,
        output_weight,
        vectors,
        grad_out,
        low_out,
        table_out,
        small_out,
        whole,
    ) = refs
    groups, heads = table_out.shape[1], len(cuts)
    small = [jnp.zeros((1, own.shape[3]), F32) for _ in range(4)]
    parts = []
    for p in range(2):
        grad = own[0, p] + near[0, p].astype(F32) + across[0, p].astype(F32)
        unit, scale = standard(hidden[0, p])
        dy = cot[0, p].astype(F32)
        total = dy + norm_back(grad, unit, scale, vectors[2:3])
        grad_out[0, p] = total
        low = total.astype(LOW)
        low_out[0, p] = low
        for k, row in enumerate((total, dy, grad * unit, grad)):
            small[k] += jnp.sum(row, axis=0, keepdims=True)
        parts.append(dot(low, output_weight[...], 1, 1))
    whole[...] = jnp.zeros_like(whole)
    for k in range(groups * heads):
        m, h = k // heads, k % heads
        start = cuts[h][0]
        found = None
        for p in range(2):
            member = onehot_columns(places[m, 0, p, me[0], h : h + 1, :], start)
            term = dot(member, head_side(parts[p], k, p).astype(LOW))
            found = term if p == 0 else found + term
        whole[m, start : start + SLOTS] += found
    size = table_out.shape[2]
    for m in range(groups):
        for d in range(table_out.shape[0]):
            table_out[d, me[0] ^ m] = whole[m, d * size : (d + 1) * size].astype(LOW)

    @pl.when(pl.program_id(0) == 0)
    def _():
        small_out[...] = jnp.zeros_like(small_out)

    for k in range(4):
        small_out[k : k + 1, :] += small[k]


def out_grad_kernel(valid, parts, out_shard, copies):
    count, rows = parts.shape[0], parts.shape[1]
    total = jnp.zeros((rows, PAIR), F32)
    for i in range(count):
        total += parts[i].astype(F32)
    total = total.astype(LOW).astype(F32)
    product = total * out_shard[...]
    deltas = [jnp.sum(side(product, p), axis=-1, keepdims=True) for p in range(2)]
    low = with_notes(total, to_notes(half_wise(*deltas, rows)), valid).astype(LOW)
    for k in range(copies.shape[0]):
        copies[k] = low


def back_kernel(cuts, valid, me, centroid, kv, grads, out_table, part_out, prob_out, score_out, sheet, columns):
    wide = len(cuts) * PAIR
    count, size = part_out.shape[0], part_out.shape[1]
    table = centroid[...].reshape(count * size, PAIR)
    grad_table = grads[...].reshape(count * size, PAIR)
    for d in range(count):
        delta = from_notes(notes_of(grads[d].astype(F32), valid), size)
        log = from_notes(notes_of(out_table[d, me[0]].astype(F32), valid), size)
        for k, column in enumerate((*delta, *log)):
            columns[d * size : (d + 1) * size, k * PAIR : (k + 1) * PAIR] = jnp.broadcast_to(column, (size, PAIR))
    sheet[...] = jnp.zeros_like(sheet)
    for h, window in enumerate(cuts):
        start = window[0]
        mine, out_grad = table[start : start + SLOTS], grad_table[start : start + SLOTS]
        kept = valid_rows(window)
        part = None
        for p in range(2):
            keys = kv[0, p, :, h * PAIR : (h + 1) * PAIR]
            values = kv[0, p, :, wide + h * PAIR : wide + (h + 1) * PAIR]
            delta = columns[start : start + SLOTS, p * PAIR : p * PAIR + 1]
            log = columns[start : start + SLOTS, (2 + p) * PAIR : (2 + p) * PAIR + 1]
            probs = jnp.where(kept, jnp.exp(scores_of(mine, keys) - log), 0.0)
            grad = (probs * (dot(out_grad, values, 1, 1) - delta) * 0.125).astype(LOW)
            term = dot(grad, keys)
            part = term if p == 0 else part + term
            prob_out[0, p, h] = probs.astype(LOW)
            score_out[0, p, h] = grad
        sheet[start : start + SLOTS] += part
    for d in range(count):
        part_out[d] = sheet[d * size : (d + 1) * size].astype(LOW)


def kv_kernel(cuts, *refs):
    centroid, out_grads, probs, grads, key_weight, value_weight, key_out, value_out, own, near, far, diagonal = refs
    share = own.shape[2]
    count, size = centroid.shape[0], centroid.shape[1]
    table = centroid[...].reshape(count * size, PAIR)
    grad_table = out_grads[...].reshape(count * size, PAIR)
    for p in range(2):
        key_parts, value_parts = [], []
        for h, (start, _) in enumerate(cuts):
            key_parts.append(dot(grads[0, p, h], table[start : start + SLOTS], 0, 0))
            value_parts.append(dot(probs[0, p, h], grad_table[start : start + SLOTS], 0, 0))
        keys = join_heads(key_parts, p).astype(LOW)
        values = join_heads(value_parts, p).astype(LOW)
        key_out[0, p] = keys
        value_out[0, p] = values
        first = dot(keys, key_weight[...]) + dot(values, value_weight[...])
        for k, ref in enumerate((own, near, far, diagonal)):
            ref[0, p] = first[k * share : (k + 1) * share].astype(ref.dtype)


def centroid_kernel(valid, parts, copies, inverse):
    count, rows = parts.shape[0], parts.shape[1]
    total = parts[0].astype(F32)
    for i in range(1, count):
        total += parts[i].astype(F32)
    counts = half_wise(*from_notes(notes_of(total, valid), rows), rows)
    share = 1.0 / jnp.maximum(counts, 1.0)
    inverse[...] = share
    row = lax.broadcasted_iota(jnp.int32, (rows, PAIR), 0)
    low = jnp.where(row < valid, total * share, 0.0).astype(LOW)
    for k in range(copies.shape[0]):
        copies[k] = low


def mean_kernel(parts, inverse, copies):
    total = parts[0].astype(F32)
    for i in range(1, parts.shape[0]):
        total += parts[i].astype(F32)
    low = (total * inverse[...]).astype(LOW)
    for k in range(copies.shape[0]):
        copies[k] = low


def query_kernel(cuts, steps, *refs):
    me, table, places, first, early, grad_out, bias_out, *total = refs
    count, size = table.shape[0], table.shape[1]
    whole = table[...].reshape(count * size, PAIR)
    product, bias = None, None
    for p in range(2):
        column = jnp.concatenate([places[0, p, me[0] ^ k].T for k in range(places.shape[2])], axis=0)
        picked = []
        for h, (start, _) in enumerate(cuts):
            member = onehot_rows(column[:, h : h + 1], start)
            picked.append(dot(member, whole[start : start + SLOTS]))
        query = join_heads(picked, p)
        term = dot(query.astype(LOW), first[0, p], 0, 0)
        row = jnp.sum(query, axis=0, keepdims=True)
        product = term if p == 0 else product + term
        bias = row if p == 0 else bias + row
    if steps > 1:
        opening = pl.program_id(0) == 0
        total[0][...] = jnp.where(opening, product, total[0][...] + product)
        total[1][...] = jnp.where(opening, bias, total[1][...] + bias)
        product, bias = total[0][...], total[1][...]
    each = product.shape[0] // early.shape[0]
    for d in range(early.shape[0]):
        rows = [early[d].astype(F32), product[d * each : (d + 1) * each]]
        grad_out[d] = jnp.concatenate(rows, axis=0).astype(LOW)
    bias_out[...] = bias


def last_kernel(cuts, *refs):
    (
        me,
        table_own,
        table_near,
        table_far,
        table_diagonal,
        places,
        own,
        near,
        across,
        tokens,
        hidden_grad,
        weight,
        vectors,
        token_out,
        small_out,
    ) = refs
    tables = [t[...].reshape(-1, PAIR) for t in (table_own, table_near, table_far, table_diagonal)]
    small = [jnp.zeros((1, own.shape[3]), F32) for _ in range(2)]
    for p in range(2):
        picked = []
        for m, whole in enumerate(tables):
            column = places[m, 0, p, me[0]].T
            for h, (start, _) in enumerate(cuts):
                member = onehot_rows(column[:, h : h + 1], start)
                picked.append(dot(member, whole[start : start + SLOTS]))
        query = join_heads(picked, p).astype(LOW)
        grad = own[0, p] + near[0, p].astype(F32) + across[0, p].astype(F32)
        grad += dot(query, weight[...])
        unit, scale = standard(tokens[0, p].astype(F32))
        token_out[0, p] = hidden_grad[0, p] + norm_back(grad, unit, scale, vectors[0:1])
        for k, row in enumerate((grad * unit, grad)):
            small[k] += jnp.sum(row, axis=0, keepdims=True)

    @pl.when(pl.program_id(0) == 0)
    def _():
        small_out[...] = jnp.zeros_like(small_out)

    for k in range(2):
        small_out[k : k + 1, :] += small[k]


def split3(values):
    high = values.astype(LOW).astype(F32)
    middle = (values - high).astype(LOW).astype(F32)
    return high, middle, values - high - middle


def summed(parts):
    total = parts[0].astype(F32)
    for i in range(1, parts.shape[0]):
        total += parts[i].astype(F32)
    return total


def shard_kernel(parts, late, copies):
    total = summed(parts)
    sums = total[:1] + total[1:2] + total[2:3]
    low = jnp.concatenate([total[3:], *split3(sums), *split2(late[...])], axis=0).astype(LOW)
    for k in range(copies.shape[0]):
        copies[k] = low


def finish_kernel(each, found, *outs):
    count, width = found.shape[0], found.shape[2]
    parts = [found[d].astype(F32) for d in range(count)]
    for k in range(4):
        outs[k][...] = jnp.concatenate([v[k * each : (k + 1) * each] for v in parts], axis=0)
    at = 4 * each
    sums = [v[at : at + 1] + v[at + 1 : at + 2] + v[at + 2 : at + 3] for v in parts]
    late = parts[0][at + 3 :]
    for v in parts[1:]:
        late += v[at + 3 :]
    late = late[:3] + late[3:]
    part = width // count

    def row(k):
        return jnp.concatenate([v[:, k * part : (k + 1) * part] for v in sums], axis=1)

    query_bias, value_bias, expand_bias = outs[10:]
    for k in range(4):
        outs[4 + k][...] = row(k)[0]
    value_bias[...] = row(4)[0, : value_bias.shape[0]]
    expand_bias[...] = row(5)[0]
    for k in range(2):
        outs[8 + k][...] = late[k]
    query_bias[...] = late[2, : query_bias.shape[0]]


def partner(value, step):
    size = lax.axis_size("mp")
    return lax.ppermute(value, "mp", [(i, i ^ step) for i in range(size)])


def gather_rows(value):
    far = partner(value, 2)
    near = partner(value, 1)
    return value, near, far, partner(far, 1)


def scatter_rows(near, far, diagonal):
    near_in, diagonal_in = partner(near, 1), partner(diagonal, 1)
    across = (far.astype(F32) + diagonal_in.astype(F32)).astype(LOW)
    return near_in, partner(across, 2)


def exchange(copies, axes):
    return lax.all_to_all(copies, axes, 0, 0)


def after(value, *others):
    return lax.optimization_barrier((value, others))[0]


def together(*values):
    return lax.optimization_barrier(values)


def shards(
    tokens,
    cluster_ids,
    query_weight,
    query_bias,
    key_weight,
    value_weight,
    value_bias,
    output_weight,
    output_bias,
    expand_weight,
    expand_bias,
    shrink_weight,
    shrink_bias,
    first_gain,
    first_shift,
    second_gain,
    second_shift,
    cotangent,
):
    seqs, share, width = tokens.shape
    heads = cluster_ids.shape[2]
    hidden_units = expand_weight.shape[1]
    n_dp, n_mp = lax.axis_size("dp"), lax.axis_size("mp")
    both = ("dp", "mp")
    n_all = n_dp * n_mp
    all_heads = heads * n_mp
    half = seqs // 2
    local = share * n_mp
    head_width = heads * HEAD_DIM
    wide = heads * PAIR
    valid = half * heads * CLUSTERS // n_dp
    size = -(-(valid + NOTES) // 16) * 16
    per_pair = n_dp // half
    cuts = windows(heads, valid, size)
    table_rows = per_pair * size
    me = lax.axis_index("mp")
    me_ref = me.astype(jnp.int32).reshape(1)

    def sequences(value):
        return value.reshape(half, 2, *value.shape[1:])

    token_pairs = sequences(tokens)
    token_far, token_near = partner(token_pairs, 2), partner(token_pairs, 1)
    places = place(cluster_ids + jnp.arange(heads, dtype=jnp.int32) * CLUSTERS, valid, size)
    places_row = places.reshape(half, 2, n_mp, share, heads).transpose(0, 1, 2, 4, 3)
    places_row = jnp.pad(places_row, ((0, 0),) * 3 + ((0, 8 - heads), (0, 0)))
    vectors = jnp.stack(
        [
            jnp.pad(v.astype(F32), (0, width - v.shape[0]))
            for v in (first_gain, first_shift, second_gain, second_shift, output_bias, query_bias, value_bias)
        ]
        + [expand_bias.astype(F32).reshape(-1, width)[k] for k in range(hidden_units // width)]
    )
    token_far, places_row, vectors = together(token_far, places_row, vectors)
    pieces = token_pairs, token_near, token_far, partner(token_far, 1)
    places_all = gather_rows(places_row)
    output_whole = jnp.concatenate(gather_rows(output_weight), axis=0)
    query_turned, key_turned, value_turned = query_weight.T, key_weight.T, value_weight.T
    query_pieces = gather_rows(query_turned)

    piece_dims = (half, 2, share, width)
    piece_spec = step_spec(piece_dims)
    square_spec = full_spec((width, width))
    head_spec = full_spec((head_width, width))
    me_spec = pl.BlockSpec(memory_space=pltpu.SMEM)
    kv_dims = (half, 2, local, 2 * wide)
    table_dims = (n_dp, size, PAIR)
    shard_dims = (size, PAIR)
    copies_dims = (n_all, *shard_dims)
    all_dims = (n_dp, n_mp, *shard_dims)
    sheet = pltpu.VMEM((table_rows, 2 * PAIR), F32)
    group_scratch = pltpu.VMEM((n_mp, table_rows, PAIR), LOW)
    places_spec = pl.BlockSpec((n_mp, 1, 2, n_mp, 8, share), lambda b: (0, b, 0, 0, 0, 0))
    vectors_spec = full_spec(vectors.shape)

    first, kv, sums = call(
        partial(first_kernel, cuts, valid),
        (half,),
        (shape((half, 2, local, width)), shape(kv_dims), shape(table_dims)),
        [me_spec]
        + [piece_spec] * 4
        + [step_spec((half, 2, n_mp, 8, share))]
        + [head_spec] * 3
        + [vectors_spec],
        (step_spec((half, 2, local, width)), step_spec(kv_dims), table_spec(table_dims, half)),
        [sheet],
    )(
        me_ref,
        *pieces,
        places_row,
        query_turned,
        key_turned,
        value_turned,
        vectors,
    )
    cotangent_pairs = sequences(cotangent)
    cot_start = after(cotangent_pairs, sums)
    cot_far, cot_near = partner(cot_start, 2), partner(cot_start, 1)

    sums = exchange(sums, "dp")
    sums, cot_far, cot_near = together(sums, cot_far, cot_near)
    cot_diagonal = partner(cot_far, 1)
    copies, inverse = call(
        partial(centroid_kernel, valid),
        (1,),
        (shape(table_dims), shape(shard_dims, F32)),
        [full_spec(table_dims)],
        (full_spec(table_dims), full_spec(shard_dims)),
    )(sums)
    centroid = exchange(copies, "dp")
    centroid, cot_diagonal = together(centroid, cot_diagonal)

    packed = call(
        partial(attend_kernel, cuts, valid),
        (half,),
        shape(table_dims),
        [table_spec(table_dims, half), step_spec(kv_dims)],
        table_spec(table_dims, half),
        [sheet],
    )(centroid, kv)
    packed = exchange(packed, "dp")
    packed, output_whole, *places_all = together(packed, output_whole, *places_all)
    places_all = jnp.stack(places_all)
    copies, out_shard = call(
        partial(merge_kernel, valid),
        (1,),
        (shape(copies_dims), shape(shard_dims, F32)),
        [full_spec(table_dims)],
        (full_spec(copies_dims), full_spec(shard_dims)),
    )(packed)
    out_table = exchange(copies, both).reshape(all_dims)
    out_table, *query_pieces = together(out_table, *query_pieces)
    query_whole = jnp.concatenate(query_pieces, axis=0)

    dense_rows = 4 * share

    def dense(which, kinds, tokens_a, tokens_b, cot_a, cot_b):
        dims = (half, dense_rows)
        return call(
            partial(dense_kernel, cuts, which),
            (half,),
            (
                shape(piece_dims, kinds[0]),
                shape(piece_dims, kinds[1]),
                shape(piece_dims, kinds[0]),
                shape(piece_dims, kinds[1]),
                shape(piece_dims, F32),
                shape((*dims, head_width)),
                shape((*dims, width)),
                shape((*dims, hidden_units)),
                shape((*dims, hidden_units)),
                shape((1, hidden_units), F32),
            ),
            [me_spec, table_spec(all_dims, half), places_spec]
            + [piece_spec] * 4
            + [square_spec, full_spec((width, hidden_units)), full_spec((hidden_units, width)), vectors_spec],
            (
                *[piece_spec] * 5,
                step_spec((*dims, head_width)),
                step_spec((*dims, width)),
                step_spec((*dims, hidden_units)),
                step_spec((*dims, hidden_units)),
                full_spec((1, hidden_units)),
            ),
            [pltpu.VMEM((dense_rows, width), LOW), group_scratch],
        )(
            me_ref,
            out_table,
            places_all,
            tokens_a,
            tokens_b,
            cot_a,
            cot_b,
            output_whole,
            expand_weight,
            shrink_weight,
            vectors,
        )

    beyond = dense(1, (F32, LOW), pieces[2], pieces[3], cot_far, cot_diagonal)
    diagonal_in = partner(beyond[1], 1)
    inside = dense(0, (F32, LOW), after(pieces[0], *beyond), pieces[1], cotangent_pairs, cot_near)
    across_in = partner((beyond[0] + diagonal_in.astype(F32)).astype(LOW), 2)
    near_in = partner(inside[1], 1)
    hidden_own = inside[4]

    def grads(terms, dims, operands):
        return call(
            partial(grads_kernel, terms, half),
            (half,),
            tuple(shape(dims) for _ in terms),
            [step_spec(value.shape) for value in operands],
            tuple(full_spec(dims) for _ in terms),
            [] if half == 1 else [pltpu.VMEM(dims, F32)] * len(terms),
        )(*operands)

    my_dp = lax.axis_index("dp")
    steps = n_dp.bit_length() - 1

    def opposite(value, step):
        return lax.ppermute(value, "dp", [(i, i ^ (1 << step)) for i in range(n_dp)])

    def halved(value, step):
        count = value.shape[0] // 2
        upper = (my_dp >> step) % 2 == 1
        return jnp.where(upper, value[count:], value[:count]), jnp.where(upper, value[:count], value[count:])

    def added(kept, arrived):
        return (kept.astype(F32) + arrived.astype(F32)).astype(LOW)

    def joined(value, arrived, step):
        upper = (my_dp >> step) % 2 == 1
        return jnp.where(
            upper, jnp.concatenate([arrived, value], axis=0), jnp.concatenate([value, arrived], axis=0)
        )

    orders = [list(range(steps)), [1, 0, *range(2, steps)]]

    def ffn_step(kept, arrived, index):
        if arrived is not None:
            kept = [added(k, v) for k, v in zip(kept, arrived)]
        cut_in_two = [halved(v, order[index]) for v, order in zip(kept, orders)]
        return [v[0] for v in cut_in_two], [opposite(v[1], order[index]) for v, order in zip(cut_in_two, orders)]

    def ffn_join(kept, arrived, index):
        return [joined(v, w, order[index]) for v, w, order in zip(kept, arrived, orders)]

    def ffn_send(kept, index):
        return [opposite(v, order[index]) for v, order in zip(kept, orders)]

    operands = (
        (beyond[7], inside[7], cot_far, cot_diagonal, cotangent_pairs, cot_near)
        + (beyond[6], inside[6], beyond[8], inside[8])
    )
    uppers = jnp.stack([(my_dp >> order[0]) % 2 for order in orders]).astype(jnp.int32)
    half_dims = (hidden_units // 2, width)
    ffn_halves = call(
        partial(halves_kernel, (True, False), half),
        (half,),
        tuple(shape(half_dims) for _ in range(4)),
        [me_spec] + [step_spec(value.shape) for value in operands],
        tuple(full_spec(half_dims) for _ in range(4)),
        [pltpu.VMEM((hidden_units, width), F32)] * 2,
    )(uppers, *operands)
    ffn_now = [ffn_halves[0], ffn_halves[2]]
    ffn_in = [opposite(ffn_halves[2 * k + 1], order[0]) for k, order in enumerate(orders)]
    expand_bias_grad = beyond[9] + inside[9]
    near_in, across_in, *ffn_now = together(near_in, across_in, *ffn_now)

    hidden_grad, hidden_low, out_part, small_two = call(
        partial(hidden_kernel, cuts),
        (half,),
        (shape(piece_dims, F32), shape(piece_dims), shape(all_dims), shape((8, width), F32)),
        [me_spec] + [piece_spec] * 5 + [places_spec, square_spec, vectors_spec],
        (piece_spec, piece_spec, table_spec(all_dims, half), full_spec((8, width))),
        [pltpu.VMEM((n_mp, table_rows, PAIR), F32)],
    )(
        me_ref,
        inside[0],
        near_in,
        across_in,
        hidden_own,
        cotangent_pairs,
        places_all,
        output_whole,
        vectors,
    )
    out_part, *ffn_in = together(out_part, *ffn_in)
    ffn_now, ffn_in = ffn_step(ffn_now, ffn_in, 1)
    out_part = exchange(out_part.reshape(copies_dims), both)
    out_part, query_whole, *ffn_in = together(out_part, query_whole, *ffn_in)
    for index in range(2, steps):
        ffn_now, ffn_in = ffn_step(ffn_now, ffn_in, index)
    out_grad = call(
        partial(out_grad_kernel, valid),
        (1,),
        shape(table_dims),
        [full_spec(copies_dims), full_spec(shard_dims)],
        full_spec(table_dims),
    )(out_part, out_shard)
    out_grad = exchange(out_grad, "dp")
    low_start = after(hidden_low, out_grad)
    low_near, low_far = partner(low_start, 1), partner(low_start, 2)
    early_small = small_two[:4]
    for step in range(n_mp.bit_length() - 1):
        early_small += partner(early_small, 1 << step)

    score_dims = (half, 2, heads, SLOTS, local)
    centroid_part, probs, score_grad = call(
        partial(back_kernel, cuts, valid),
        (half,),
        (shape(table_dims), shape(score_dims), shape(score_dims)),
        [me_spec, table_spec(table_dims, half), step_spec(kv_dims)]
        + [table_spec(table_dims, half), table_spec(all_dims, half)],
        (table_spec(table_dims, half), step_spec(score_dims), step_spec(score_dims)),
        [pltpu.VMEM((table_rows, PAIR), F32), pltpu.VMEM((table_rows, 4 * PAIR), F32)],
    )(me_ref, centroid, kv, out_grad, out_table)
    centroid_part, *ffn_in = together(centroid_part, *ffn_in)
    ffn_now = [added(k, v) for k, v in zip(ffn_now, ffn_in)]
    ffn_in = ffn_send(ffn_now, steps - 1)
    low_diagonal = partner(after(low_far, centroid_part), 1)
    centroid_part = exchange(centroid_part, "dp")

    grad_dims = (half, 2, local, head_width)
    key_grad, value_grad, first_own, *first_parts = call(
        partial(kv_kernel, cuts),
        (half,),
        (shape(grad_dims), shape(grad_dims), *[shape(piece_dims, kind) for kind in (F32, LOW, F32, LOW)]),
        [table_spec(table_dims, half)] * 2
        + [step_spec(score_dims), step_spec(score_dims)]
        + [head_spec] * 2,
        (step_spec(grad_dims), step_spec(grad_dims), *[piece_spec] * 4),
    )(centroid, out_grad, probs, score_grad, key_turned, value_turned)

    count_rows = seqs * local
    first_flat = first.reshape(count_rows, width)
    value_flat = value_grad.reshape(count_rows, head_width)
    key_weight_grad = dot(key_grad.reshape(count_rows, head_width), first_flat, 0, 0).astype(LOW)
    value_weight_grad = dot(value_flat, first_flat, 0, 0).astype(LOW)
    value_bias_grad = jnp.sum(value_flat.astype(F32), axis=0)
    early_small = jnp.concatenate(
        [early_small, jnp.pad(value_bias_grad, (0, width - head_width))[None], expand_bias_grad], axis=0
    )
    key_weight_grad, value_weight_grad, *ffn_in = together(key_weight_grad, value_weight_grad, *ffn_in)
    near_in, diagonal_in = partner(first_parts[0], 1), partner(first_parts[2], 1)
    across = (first_parts[1].astype(F32) + diagonal_in.astype(F32)).astype(LOW)
    centroid_part, low_near, low_far, low_diagonal, first_own, early_small, key_weight_grad, *rest = together(
        centroid_part, low_near, low_far, low_diagonal, first_own, early_small, key_weight_grad, near_in, across, *ffn_in
    )
    (near_in, across), ffn_in = rest[:2], rest[2:]
    for index in range(steps - 1, 1, -1):
        ffn_now = ffn_join(ffn_now, ffn_in, index)
        ffn_in = ffn_send(ffn_now, index - 1)
    (output_weight_grad,) = grads(
        (True,),
        (head_width, width),
        (beyond[5], inside[5], low_far, low_diagonal, hidden_low, low_near),
    )
    first_in = near_in, partner(across, 2)
    query_copies = call(
        mean_kernel,
        (1,),
        shape(table_dims),
        [full_spec(table_dims), full_spec(shard_dims)],
        full_spec(table_dims),
    )(centroid_part, inverse)
    query_table = exchange(query_copies, "dp")
    def cut(value, count):
        rows, columns = value.shape[0] // count, value.shape[1]
        value = value.reshape(count, n_dp, rows // n_dp, columns).transpose(1, 0, 2, 3)
        return value.reshape(n_dp, count * rows // n_dp, columns)

    part = early_small.shape[0] * width // n_dp
    early_small = early_small.reshape(-1, n_dp, width // n_dp).transpose(1, 0, 2).reshape(n_dp, 1, part)
    early_small = jnp.pad(early_small, ((0, 0), (0, 0), (0, width - part)))
    high = lax.reduce_precision(early_small, 8, 7)
    middle = lax.reduce_precision(early_small - high, 8, 7)
    early_small = jnp.concatenate([high, middle, early_small - high - middle], axis=1).astype(LOW)
    early = cut(jnp.concatenate([key_weight_grad, value_weight_grad, output_weight_grad]), 3)
    early = jnp.concatenate([early_small, early], axis=1)
    query_table, early, *rest = together(query_table, early, *first_in, *ffn_in)
    first_in, ffn_in = rest[:2], rest[2:]
    ffn_now = ffn_join(ffn_now, ffn_in, 1)
    ffn_in = ffn_send(ffn_now, 0)
    query_tables = gather_rows(query_table)

    merged = (n_dp, 3 + 4 * head_width // n_dp, width)
    merged_grads, query_bias_grad = call(
        partial(query_kernel, cuts, half),
        (half,),
        (shape(merged), shape((1, head_width), F32)),
        [me_spec, table_spec(table_dims, half), step_spec((half, 2, n_mp, 8, share))]
        + [step_spec((half, 2, local, width)), full_spec(early.shape)],
        (full_spec(merged), full_spec((1, head_width))),
        [] if half == 1 else [pltpu.VMEM((head_width, width), F32), pltpu.VMEM((1, head_width), F32)],
    )(me_ref, query_table, places_row, first, early)
    found = exchange(merged_grads, "dp")

    token_grad, small_one = call(
        partial(last_kernel, cuts),
        (half,),
        (shape(piece_dims, F32), shape((8, width), F32)),
        [me_spec]
        + [table_spec(table_dims, half)] * 4
        + [places_spec]
        + [piece_spec] * 5
        + [square_spec, vectors_spec],
        (piece_spec, full_spec((8, width))),
    )(
        me_ref,
        *query_tables,
        places_all,
        first_own,
        *first_in,
        pieces[0],
        hidden_grad,
        query_whole,
        vectors,
    )

    late = small_one[:2]
    for step in range(n_mp.bit_length() - 1):
        late += partner(late, 1 << step)
    late = jnp.concatenate([late, jnp.pad(query_bias_grad, ((0, 0), (0, width - head_width)))], axis=0)
    each = head_width // n_dp
    parts, late, *ffn_in = together(found, late, *ffn_in)
    shrink_weight_grad, expand_weight_grad = (v.astype(F32) for v in ffn_join(ffn_now, ffn_in, 0))
    found = shape((n_dp, 4 * each + 9, width))
    found = call(
        shard_kernel,
        (1,),
        found,
        [full_spec(parts.shape), full_spec(late.shape)],
        full_spec(found.shape),
        limit=64,
    )(parts, late)
    ffn_near, ffn_across = scatter_rows(inside[3], beyond[2], after(beyond[3], found))
    found = exchange(found, "dp")
    found, shrink_weight_grad, expand_weight_grad = together(found, shrink_weight_grad, expand_weight_grad)
    result = (
        hidden_own
        + inside[2]
        + ffn_near.astype(F32)
        + ffn_across.astype(F32)
        + shrink_bias.astype(F32)
    ).astype(LOW)
    lengths = [width] * 6 + [head_width] * 2 + [hidden_units]
    key_weight_grad, value_weight_grad, output_weight_grad, query_weight_grad, *vectors = call(
        partial(finish_kernel, each),
        (1,),
        tuple(shape((head_width, width), F32) for _ in range(4)) + tuple(shape((n,), F32) for n in lengths),
        [full_spec(found.shape)],
        tuple(full_spec((head_width, width)) for _ in range(4)) + tuple(full_spec((n,)) for n in lengths),
        limit=64,
    )(found)
    return (
        result.reshape(tokens.shape),
        token_grad.reshape(tokens.shape),
        query_weight_grad.T,
        vectors[6],
        key_weight_grad.T,
        value_weight_grad.T,
        vectors[7],
        output_weight_grad,
        vectors[0],
        expand_weight_grad,
        vectors[8],
        shrink_weight_grad,
        vectors[1],
        vectors[4],
        vectors[5],
        vectors[2],
        vectors[3],
    )


def solution(mesh):
    rows = P(None, ("dp", "mp"), None)
    columns, heads, vector, whole = P(None, "mp"), P("mp", None), P("mp"), P()
    return jax.shard_map(
        shards,
        mesh=mesh,
        in_specs=(
            rows,
            P(None, "dp", "mp"),
            columns,
            vector,
            columns,
            columns,
            vector,
            heads,
            whole,
            columns,
            vector,
            heads,
            whole,
            whole,
            whole,
            whole,
            whole,
            rows,
        ),
        out_specs=(
            rows,
            rows,
            columns,
            vector,
            columns,
            columns,
            vector,
            heads,
            whole,
            columns,
            vector,
            heads,
            whole,
            whole,
            whole,
            whole,
            whole,
        ),
        check_vma=False,
    )
```
